512 devices in a mesh: slab: 64 (over z_hi, y, core), coil: 8 (over z_lo, x).
Axes of the slice: x: 4, y: 8, z: 8 (z_hi: 4, z_lo: 2; z = z_hi * 2 + z_lo), core: 2. Of those that a mesh axis runs over, the one named last changes fastest.
Arguments:
- image: float32 [64, 32, 2, 320], P('slab', 'coil'), may hold values from -6 to 6
- sampled_lines: int32 [64, 80], P('slab'), may hold values from 0 to 319, as said below
- coil_maps: float32 [32, 64, 32, 2, 320], P('coil', 'slab'), may hold values from -2 to 2
- kspace: float32 [32, 64, 32, 2, 320], P('coil', 'slab'), may hold values from -16 to 16
- reg_weight: float32 [1], replicated, may hold values from 0.05 to 0.5
- conv_first: bfloat16 [3, 3, 3, 2, 64], replicated, may hold values from -1.25 to 1.25
- conv_middle: bfloat16 [2, 3, 3, 3, 64, 64], replicated, may hold values from -0.21875 to 0.21875
- conv_last: bfloat16 [3, 3, 3, 64, 2], replicated, may hold values from -0.15625 to 0.15625
Outputs:
- denoised: float32 [64, 32, 2, 320], P('slab', 'coil')
- reconstruction: float32 [64, 32, 2, 320], P('slab', 'coil')
The draws below stay inside these ranges and needn't reach their ends.
Inputs may be any that keep to these rules, and one draw needn't show every extreme that they name: `sampled_lines`: each row holds 80 different line indices; among them are the 24 lines starting at 148 and the lines 0 and 319.
All inputs are finite; a program needn't handle non-finite values.
Results may differ from the reference program's by a relative error of at most 0.0059.
Values may be sent and summed in bfloat16 or wider, within the bound.
A program may use at most 64 MiB of HBM per device.

```python
import math
import jax
import jax.numpy as jnp
from jax import lax

Y = 320
CH = 64
C = 32
MID = 2
ITERS = 4
NS = 80
ACS = 24
Z = 64
XW = 32


def draw_sampled_lines(key, part):
    key = jax.random.fold_in(key, 3)
    positions = jnp.arange(Y, dtype=jnp.int32)
    scores = jax.random.randint(key, (Z, Y), 0, 1 << 20, dtype=jnp.int32) * Y + positions[None, :]
    centre = Y // 2 - ACS // 2
    forced = (positions >= centre) & (positions < centre + ACS) | (positions == 0) | (positions == Y - 1)
    scores = scores + jnp.where(forced, 1 << 29, 0).astype(jnp.int32)[None, :]
    ranking = jnp.argsort(-scores, axis=1)
    return ranking[:, :NS].astype(jnp.int32)


def draw_kspace(key, part):
    key = jax.random.fold_in(key, 5)
    noise_key = jax.random.fold_in(key, 0)
    slices = jnp.arange(Z, dtype=jnp.float32) / max(Z - 1, 1)
    growth = jnp.exp(math.log(3.0) * slices)
    values = jax.random.truncated_normal(noise_key, -4.0, 4.0, (C, Z, XW, 2, Y), jnp.float32)
    return values * growth[None, :, None, None, None]


def levels(stream_key, extent, cuts, least, largest):
    level, own = 1.0, jax.random.fold_in(stream_key, 6)
    for dim, blocks in cuts:
        heights = jnp.exp(jax.random.uniform(jax.random.fold_in(own, dim), (blocks,), jnp.float32, least / len(cuts), largest / len(cuts)))
        level = level * jnp.repeat(heights, extent[dim] // blocks).reshape([-1 if axis == dim else 1 for axis in range(len(extent))])
    return level


def gaussian(stream_key, dims, deviation, reach, pieces=(), kind=jnp.bfloat16):
    level = levels(stream_key, dims, pieces, -0.22, 0.18) if pieces else 1.0
    array = jax.random.normal(stream_key, dims, jnp.float32) * deviation * level
    return jnp.minimum(jnp.maximum(array, -reach), reach).astype(kind)


def setup_inputs(seed: int = 0) -> dict:
    splits = jax.random.split(jax.random.key(seed), 9)
    image = gaussian(splits[0], (Z, XW, 2, Y), 1.0, 6.0, ((0, 64), (1, 8)), jnp.float32)
    sampled_lines = draw_sampled_lines(jax.random.fold_in(splits[8], 71), 0)
    coil_maps = gaussian(splits[2], (C, Z, XW, 2, Y), 0.125, 2.0, ((0, 8), (1, 64)), jnp.float32)
    kspace = draw_kspace(jax.random.fold_in(splits[8], 71), 0)
    reg_weight = jnp.clip(jnp.exp(jax.random.uniform(splits[4], (1,), jnp.float32, math.log(0.05), math.log(0.5))), 0.05, 0.5)
    conv_first = gaussian(splits[5], (3, 3, 3, 2, CH), 27 ** -0.5, 1.25)
    conv_middle = gaussian(splits[6], (MID, 3, 3, 3, CH, CH), (27 * CH // 2) ** -0.5, 0.21875)
    conv_last = gaussian(splits[7], (3, 3, 3, CH, 2), (27 * CH) ** -0.5, 0.15625)
    return {"image": image, "sampled_lines": sampled_lines, "coil_maps": coil_maps, "kspace": kspace, "reg_weight": reg_weight, "conv_first": conv_first, "conv_middle": conv_middle, "conv_last": conv_last}


def convolve(features, weight):
    return lax.conv_general_dilated(features.astype(jnp.float32)[None], weight.astype(jnp.float32), (1, 1, 1), "SAME", dimension_numbers=("NDHWC", "DHWIO", "NDHWC"), precision=lax.Precision.HIGHEST)[0]


def to_complex(complex_field):
    return complex_field[..., 0, :] + 1j * complex_field[..., 1, :]


def inner_product(first_vector, second_vector):
    return jnp.sum(jnp.real(jnp.conj(first_vector) * second_vector))


def reference(image, sampled_lines, coil_maps, kspace, reg_weight, conv_first, conv_middle, conv_last):
    hidden = jnp.transpose(image, (0, 1, 3, 2)).astype(jnp.bfloat16)
    hidden = jax.nn.relu(convolve(hidden, conv_first)).astype(jnp.bfloat16)
    for layer_index in range(MID):
        hidden = jax.nn.relu(convolve(hidden, conv_middle[layer_index])).astype(jnp.bfloat16)
    denoised = image + jnp.transpose(convolve(hidden, conv_last), (0, 1, 3, 2))
    sampled = jnp.sum((sampled_lines[:, :, None] == jnp.arange(Y, dtype=jnp.int32)[None, None, :]).astype(jnp.float32), axis=1)
    sampling = sampled[None, :, None, :]
    sensitivity = to_complex(coil_maps)
    regular = reg_weight[0]

    def normal_map(vector):
        spectrum = jnp.fft.fft(sensitivity * vector[None], axis=-1, norm="ortho") * sampling
        return jnp.sum(jnp.conj(sensitivity) * jnp.fft.ifft(spectrum, axis=-1, norm="ortho"), axis=0) + regular * vector

    measured = jnp.fft.ifft(to_complex(kspace) * sampling, axis=-1, norm="ortho")
    right_side = jnp.sum(jnp.conj(sensitivity) * measured, axis=0) + regular * to_complex(denoised)
    solution = jnp.zeros_like(right_side)
    residual = right_side
    direction = right_side
    norm_now = inner_product(residual, residual)
    for iteration in range(ITERS):
        mapped = normal_map(direction)
        step_size = norm_now / inner_product(direction, mapped)
        solution = solution + step_size * direction
        residual = residual - step_size * mapped
        norm_next = inner_product(residual, residual)
        direction = residual + (norm_next / norm_now) * direction
        norm_now = norm_next
    reconstruction = jnp.stack([jnp.real(solution), jnp.imag(solution)], axis=2).astype(jnp.float32)
    return denoised, reconstruction
```

```python
import functools
import math

import jax
import jax.numpy as jnp
from jax import lax
from jax.experimental import pallas as pl
from jax.experimental.pallas import tpu as pltpu
from jax.sharding import PartitionSpec as P

MESH = pl.DeviceIdType.MESH
F32 = jnp.float32
BF16 = jnp.bfloat16

Y = 320
YP = 384
XB = 4
CH = 64
C = 32
CL = 4
NS = 80
HALO = 4
XW = 32
Z = 64
X_CHIPS = 4
Y_CHIPS = 8
Z_CHIPS = 8
LIMIT = 56 * 2**20


def dot(a, b):
    return jnp.dot(a, b, preferred_element_type=F32)


def dot_t(a, b):
    return lax.dot_general(a, b, (((1,), (1,)), ((), ())), preferred_element_type=F32)


def split(v):
    high = v.astype(BF16)
    return high, (v - high.astype(F32)).astype(BF16)


def dot3(v, high_ref, low_ref, op):
    high, low = split(v)
    table = high_ref[...]
    return op(high, table) + op(low, table) + op(high, low_ref[...])


def lane_roll(v, amount):
    return pltpu.roll(v, amount % v.shape[1], axis=1)


def kernel(
    image_ref, lines_ref, maps_hbm, kspace_hbm, reg_ref, first_ref, middle_ref, last_ref,
    denoised_ref, out_ref,
    halo, feats, w1f, w1, wt, wm, w4f, w4, p1, p2, p3, sums, tall,
    table_hi, table_lo, pick, local_maps, local_kspace, own_maps, inter, planes, maps_re, maps_im,
    part_send, part_recv, pair, slots,
    local_sem, img_send, img_recv, map_send, map_recv, rhs_send, rhs_recv, sum_send, sum_recv,
):
    s = lax.axis_index("slab")
    c = lax.axis_index("coil")
    x_chip, z_lo = c % X_CHIPS, c // X_CHIPS
    core, y_chip, z_hi = s % 2, (s // 2) % Y_CHIPS, s // (2 * Y_CHIPS)
    z_chip = z_hi * 2 + z_lo

    offsets = [(dz, dx) for dz in range(-HALO, HALO + 1) for dx in (-1, 0, 1) if (dz, dx) != (0, 0)]

    def shifted(dz, dx):
        return ((s + dz + Z) % Z, (c + dx + 8) % 8)

    def stage_partner(stage, d):
        if stage == 0:
            return (
                z_hi * 16 + y_chip * 2 + (core + d // 4) % 2,
                z_lo * 4 + (x_chip + d % 4) % 4,
            )
        if stage == 1:
            return (z_hi * 16 + ((y_chip + d) % 8) * 2 + core, c)
        z_new = (z_chip + d) % 8
        return ((z_new // 2) * 16 + y_chip * 2 + core, (z_new % 2) * 4 + x_chip)

    stage_index = (core * 4 + x_chip, y_chip, z_chip)

    partners = [shifted(dz, dx) for dz, dx in offsets]
    partners += [shifted(0, d) for d in range(1, 8)]
    partners += [stage_partner(stage, d) for stage in range(3) for d in range(1, 8)]
    barrier = pltpu.get_barrier_semaphore()
    for partner in partners:
        pl.semaphore_signal(barrier, inc=1, device_id=partner, device_id_type=MESH)

    local_copies = [
        pltpu.make_async_copy(maps_hbm.at[:, 0], local_maps, local_sem.at[0]),
        pltpu.make_async_copy(kspace_hbm.at[:, 0], local_kspace, local_sem.at[1]),
        pltpu.make_async_copy(
            maps_hbm.at[:, 0, pl.ds(c * XB, XB)], own_maps.at[pl.ds(c * CL, CL)], local_sem.at[2]
        ),
    ]
    for copy in local_copies:
        copy.start()

    halo[HALO, 8:16] = jnp.zeros((8, YP), F32)
    for x in range(XB):
        halo[HALO, 8 + 2 * x : 10 + 2 * x, 0:Y] = image_ref[0, x]

    pl.semaphore_wait(barrier, len(partners))

    image_copies = []
    for i, (dz, dx) in enumerate(offsets):
        copy = pltpu.make_async_remote_copy(
            src_ref=halo.at[HALO, pl.ds(8, 8)],
            dst_ref=halo.at[HALO - dz, pl.ds(8 - 8 * dx, 8)],
            send_sem=img_send.at[i],
            recv_sem=img_recv.at[i],
            device_id=shifted(dz, dx),
            device_id_type=MESH,
        )
        copy.start()
        image_copies.append(copy)
    map_copies = []
    for d in range(1, 8):
        target = (c + d) % 8
        copy = pltpu.make_async_remote_copy(
            src_ref=maps_hbm.at[:, 0, pl.ds(target * XB, XB)],
            dst_ref=own_maps.at[pl.ds(c * CL, CL)],
            send_sem=map_send.at[d - 1],
            recv_sem=map_recv.at[d - 1],
            device_id=(s, target),
            device_id_type=MESH,
        )
        copy.start()
        map_copies.append(copy)

    lines = jnp.concatenate([lines_ref[...], jnp.full((1, 128 - NS), -1, jnp.int32)], axis=1)
    position = lax.broadcasted_iota(jnp.int32, (YP, 128), 0)
    line = jnp.broadcast_to(lines, (YP, 128))
    inside = (position < Y) & (line >= 0)
    product = (position * line).astype(F32)
    phase = product - Y * jnp.floor((product + 0.5) * (1.0 / Y))
    half = jnp.abs(jnp.where(phase > Y / 2, phase - Y, phase))
    sine_sign = jnp.where(phase > Y / 2, -1.0, 1.0)
    low_half = half <= Y / 4
    angle = jnp.where(low_half, half, Y / 2 - half) * (2.0 * math.pi / Y)
    square = angle * angle
    cosine = jnp.full((YP, 128), 1.0 / math.factorial(14), F32) * -1.0
    sine = jnp.full((YP, 128), 1.0 / math.factorial(13), F32)
    for order in range(6, -1, -1):
        cosine = cosine * square + (-1.0) ** order / math.factorial(2 * order)
        if order < 6:
            sine = sine * square + (-1.0) ** order / math.factorial(2 * order + 1)
    scale = 1.0 / math.sqrt(Y)
    cosine = jnp.where(inside, jnp.where(low_half, cosine, -cosine) * scale, 0.0)
    sine = jnp.where(inside, sine * angle * sine_sign * scale, 0.0)
    for row, column, value in (
        (0, 0, cosine), (0, 128, -sine), (YP, 0, sine), (YP, 128, cosine),
    ):
        high, low = split(value)
        table_hi[row : row + YP, column : column + 128] = high
        table_lo[row : row + YP, column : column + 128] = low
    pick[...] = jnp.where(inside & (position == line), 1.0, 0.0).astype(BF16)

    for copy in local_copies:
        copy.wait()
    inter[...] = jnp.zeros_like(inter)
    groups = inter.reshape(3, C, 8, 128)
    tiles = ((0, 128), (1, 128), (2, Y - 256))

    def plane_of(ref, start, count):
        return jnp.concatenate([ref[t, pl.ds(start, count, stride=2), :] for t in range(3)], axis=1)

    def load_planes(source):
        def move(group, carry):
            for x in range(XB):
                value = source(group, x)
                for t, width in tiles:
                    groups[t, group, 2 * x : 2 * x + 2, 0:width] = value[:, 128 * t : 128 * t + width]
            return carry

        lax.fori_loop(0, C, move, 0)
        return plane_of(inter, 0, 4 * C), plane_of(inter, 1, 4 * C)

    kspace_re, kspace_im = load_planes(lambda group, x: local_kspace[group // 8, (group % 8) * XB + x])
    spectrum = []
    for plane in (kspace_re, kspace_im):
        high, low = split(plane)
        spectrum.append(dot(high, pick[...]) + dot(low, pick[...]))
    field = dot3(jnp.concatenate(spectrum, axis=1), table_hi, table_lo, dot_t)
    planes[...] = field
    s_re, s_im = load_planes(lambda group, x: local_maps[group // 8, (group % 8) * XB + x])
    energy = s_re * s_re + s_im * s_im
    energy = jnp.sum(energy.reshape(16, 8, YP), axis=0)
    energy = energy[:, 0:128] + energy[:, 128:256] + energy[:, 256:384]
    f_re, f_im = planes[:, 0:YP], planes[:, YP : 2 * YP]
    sum_re = jnp.sum((s_re * f_re + s_im * f_im).reshape(CL, XW, YP), axis=0)
    sum_im = jnp.sum((s_re * f_im - s_im * f_re).reshape(CL, XW, YP), axis=0)
    for k in range(8):
        part_send[k, 0:4] = sum_re[4 * k : 4 * k + 4]
        part_send[k, 4:8] = sum_im[4 * k : 4 * k + 4]
    part_recv[c] = part_send[c]
    rhs_copies = []
    for d in range(1, 8):
        target = (c + d) % 8
        copy = pltpu.make_async_remote_copy(
            src_ref=part_send.at[target],
            dst_ref=part_recv.at[c],
            send_sem=rhs_send.at[d - 1],
            recv_sem=rhs_recv.at[d - 1],
            device_id=(s, target),
            device_id_type=MESH,
        )
        copy.start()
        rhs_copies.append(copy)

    def start_stage(which, stage, value):
        index = stage_index[stage]
        slots[which, stage, index] = value
        copies = []
        for d in range(1, 8):
            copy = pltpu.make_async_remote_copy(
                src_ref=slots.at[which, stage, index],
                dst_ref=slots.at[which, stage, index],
                send_sem=sum_send.at[which, stage, d - 1],
                recv_sem=sum_recv.at[which, stage, d - 1],
                device_id=stage_partner(stage, d),
                device_id_type=MESH,
            )
            copy.start()
            copies.append(copy)
        return copies

    def finish_stage(which, stage, copies):
        for copy in copies:
            copy.wait()
        return jnp.sum(slots[which, stage], axis=0)

    energy_copies = start_stage(0, 0, jnp.concatenate([energy, jnp.zeros((8, 128), F32)], axis=0))

    wt[...] = jnp.zeros_like(wt)
    for dy in range(3):
        for dz in range(3):
            for dx in range(3):
                row = 2 * (dy * 9 + dz * 3 + dx)
                wt[row : row + 2, 0:CH] = first_ref[dz * 9 + dx * 3 + dy].astype(F32)
    w1f[...] = jnp.zeros_like(w1f)
    row8 = lax.broadcasted_iota(jnp.int32, (8, 128), 0)
    for q in range(9):
        low = jnp.where(row8 < 6, wt[6 * q : 6 * q + 8, :], 0.0)
        both = low + lane_roll(pltpu.roll(low, 2, axis=0), CH)
        for x in range(10):
            if x < 9:
                w1f[24 * q + 2 * x : 24 * q + 2 * x + 8, 128 * x : 128 * x + 128] = both
            else:
                w1f[24 * q + 18 : 24 * q + 24, 128 * x : 128 * x + 128] = low[0:6]
    w1[...] = w1f[0:256, :].astype(BF16)

    wm[...] = jnp.zeros_like(wm)

    def middle_weights(i, carry):
        layer, dz = i // 3, i % 3
        for dx in range(3):
            taps = [middle_ref[i * 9 + dx * 3 + dy] for dy in range(3)]
            wm[layer, pl.ds(pl.multiple_of(dz * 256 + dx * CH, CH), CH), 0:128] = jnp.concatenate([taps[0], taps[2]], axis=1)
            wm[layer, pl.ds(pl.multiple_of(dz * 256 + dx * CH, CH), CH), 128:256] = jnp.concatenate([taps[1], taps[1]], axis=1)
        return carry

    lax.fori_loop(0, 6, middle_weights, 0)

    w4f[...] = jnp.zeros_like(w4f)
    for dz in range(3):
        for dx in range(3):
            merged = None
            for dy in range(3):
                tap = last_ref[dz * 9 + dx * 3 + dy].astype(F32)
                tap = jnp.concatenate([tap, jnp.zeros((CH, 126), F32)], axis=1)
                tap = tap if dy == 0 else lane_roll(tap, 8 * dy)
                merged = tap if merged is None else merged + tap
            for x in range(XB):
                base = dz * 384 + (x + dx) * CH
                w4f[base : base + CH, :] += merged if x == 0 else lane_roll(merged, 2 * x)
    w4[...] = w4f[...].astype(BF16)

    for copy in image_copies:
        copy.wait()
    row24 = lax.broadcasted_iota(jnp.int32, (24, YP), 0) // 8 + (c - 1)

    def feature_slice(zi, carry):
        slice_index = s + zi - HALO
        valid = (row24 >= 0) & (row24 < 8) & (slice_index >= 0) & (slice_index < Z)
        value = jnp.where(valid, halo[zi].astype(BF16).astype(F32), 0.0)
        feats[0, zi] = lane_roll(value, 1)
        feats[1, zi] = value
        feats[2, zi] = lane_roll(value, -1)
        return carry

    lax.fori_loop(0, 2 * HALO + 1, feature_slice, 0)

    lane = lax.broadcasted_iota(jnp.int32, (1, 256), 1)

    def first_layer(z, carry):
        slice_index = s + z - 3
        slice_valid = (slice_index >= 0) & (slice_index < Z)
        columns = jnp.concatenate(
            [feats[dy, pl.ds(z, 3)].reshape(72, YP) for dy in range(3)] + [jnp.zeros((40, YP), F32)],
            axis=0,
        )
        tall[...] = jnp.transpose(columns).astype(BF16)
        for x in range(0, 10, 2):
            at = c * XB - 3 + x + lane // CH - lane // 128
            mask = jnp.where((at >= 0) & (at < XW) & slice_valid, 1.0, 0.0)
            product = dot(tall[0:Y, :], w1[:, 128 * x : 128 * x + 256])
            product = (jnp.maximum(product, 0.0) * mask).astype(BF16)
            p1[z, x] = product[:, 0:128]
            p1[z, x + 1] = product[:, 128:256]
        return carry

    lax.fori_loop(0, 7, first_layer, 0)
    energy = finish_stage(0, 0, energy_copies)
    energy_copies = start_stage(0, 1, energy)

    sums[...] = jnp.zeros_like(sums)
    low_lanes = lax.broadcasted_iota(jnp.int32, (Y, 128), 1) < CH

    def middle_layer(layer, source, target, slices, rows):
        reach_z, reach_x = slices // 2, (rows - XB) // 2

        def one_slice(z, carry):
            slice_index = s + z - reach_z
            slice_valid = (slice_index >= 0) & (slice_index < Z)
            for x in range(rows):
                operand = jnp.concatenate(
                    [source[z + dz, x + 2 * k] for dz in range(3) for k in range(2)], axis=1
                )
                sums[x, 8 : 8 + Y, :] = dot(operand, wm[layer])
            following = None
            for x in range(rows - 1, -1, -1):
                at = c * XB - reach_x + x
                mask = jnp.where((at >= 0) & (at < XW) & slice_valid, 1.0, 0.0).astype(F32)
                outer = jnp.where(low_lanes, sums[x, 7 : 7 + Y, 0:128], sums[x, 9 : 9 + Y, 0:128])
                value = outer + lane_roll(outer, CH) + sums[x, 8 : 8 + Y, 128:256]
                value = jnp.maximum(value, 0.0) * mask
                target[z, x] = jnp.where(low_lanes, value, value if following is None else following).astype(BF16)
                following = value
            return carry

        lax.fori_loop(0, slices, one_slice, 0)

    middle_layer(0, p1, p2, 5, 8)
    energy = finish_stage(0, 1, energy_copies)
    energy_copies = start_stage(0, 2, energy)
    middle_layer(1, p2, p3, 3, 6)
    energy = finish_stage(0, 2, energy_copies)

    operand = jnp.concatenate([p3[dz, 2 * k] for dz in range(3) for k in range(3)], axis=1)
    w1f[0:YP, 0:128] = jnp.zeros((YP, 128), F32)
    w1f[0:Y, 0:128] = dot(operand, w4[...])
    turned = jnp.transpose(w1f[0:YP, 0:128])
    residual = lane_roll(turned[0:8], 1) + turned[8:16] + lane_roll(turned[16:24], -1)
    lane8 = lax.broadcasted_iota(jnp.int32, (8, YP), 1)
    denoised = halo[HALO, 8:16] + jnp.where(lane8 < Y, residual, 0.0)
    for t in range(3):
        pair[t, 0:8] = denoised[:, 128 * t : 128 * t + 128]
        pair[t, 8:16] = denoised[:, 128 * t : 128 * t + 128]

    def write(ref):
        for x in range(XB):
            for t, width in tiles:
                ref[0, x, :, 128 * t : 128 * t + width] = pair[t, 2 * x : 2 * x + 2, 0:width]

    write(denoised_ref)
    den_re, den_im = plane_of(pair, 0, 8), plane_of(pair, 1, 8)

    reg = reg_ref[0]
    for copy in rhs_copies:
        copy.wait()
    adjoint = jnp.sum(part_recv[...], axis=0)
    other = pltpu.roll(adjoint, 4, axis=0)
    first_rows = lax.broadcasted_iota(jnp.int32, (8, YP), 0) < 4
    right = (
        jnp.where(first_rows, adjoint, other) + reg * den_re,
        jnp.where(first_rows, other, adjoint) + reg * den_im,
    )
    for copy in map_copies:
        copy.wait()
    s_re, s_im = load_planes(lambda group, x: own_maps[group, x])
    maps_re[...] = s_re
    maps_im[...] = s_im

    mean = jnp.sum(jnp.sum(energy, axis=0, keepdims=True), axis=1, keepdims=True) * (NS / Y / (Z * XW * Y))

    def spectrum_of(vector):
        v_re = jnp.broadcast_to(vector[0][None], (16, 8, YP)).reshape(128, YP)
        v_im = jnp.broadcast_to(vector[1][None], (16, 8, YP)).reshape(128, YP)
        m_re, m_im = maps_re[...], maps_im[...]
        weighted = jnp.concatenate([m_re * v_re - m_im * v_im, m_re * v_im + m_im * v_re], axis=1)
        return dot3(weighted, table_hi, table_lo, dot)

    def gram_map(vector):
        planes[...] = dot3(spectrum_of(vector), table_hi, table_lo, dot_t)
        m_re, m_im = maps_re[...], maps_im[...]
        f_re, f_im = planes[:, 0:YP], planes[:, YP : 2 * YP]
        real = jnp.sum((m_re * f_re + m_im * f_im).reshape(16, 8, YP), axis=0)
        imag = jnp.sum((m_re * f_im - m_im * f_re).reshape(16, 8, YP), axis=0)
        return real + pltpu.roll(real, 4, axis=0), imag + pltpu.roll(imag, 4, axis=0)

    basis = [right]
    for _ in range(3):
        mapped = gram_map(basis[-1])
        basis.append((mapped[0] - mean * basis[-1][0], mapped[1] - mean * basis[-1][1]))
    last_spectrum = spectrum_of(basis[-1])
    last_energy = jnp.sum((last_spectrum * last_spectrum).reshape(16, 8, 256), axis=0)
    last_energy = last_energy[:, 0:128] + last_energy[:, 128:256]

    def folded(first, second):
        product = first[0] * second[0] + first[1] * second[1]
        product = product[:, 0:128] + product[:, 128:256] + product[:, 256:384]
        return 0.5 * jnp.sum(product, axis=0, keepdims=True)

    pairs = [(i, j) for i in range(4) for j in range(i, 4)]
    rows = [folded(basis[i], basis[j]) for i, j in pairs]
    rows.append(jnp.sum(last_energy, axis=0, keepdims=True))
    rows.append(jnp.zeros((16 - len(rows), 128), F32))
    moments = jnp.concatenate(rows, axis=0)
    for stage in range(3):
        moments = finish_stage(1, stage, start_stage(1, stage, moments))
    moments = jnp.sum(moments, axis=1, keepdims=True)
    gram = {}
    for row, (i, j) in enumerate(pairs):
        gram[i, j] = gram[j, i] = moments[row : row + 1]
    shift = mean + reg
    matrix = {}
    for i in range(4):
        for j in range(i, 4):
            value = gram[i + 1, j] + shift * gram[i, j] if i < 3 else moments[10:11] + reg * gram[3, 3]
            matrix[i, j] = matrix[j, i] = value
    norm = [jnp.where(matrix[i, i] > 1e-37, lax.rsqrt(jnp.maximum(matrix[i, i], 1e-37)), 0.0) for i in range(4)]
    side = [gram[0, i] * norm[i] for i in range(4)]
    for i in range(4):
        for j in range(i, 4):
            matrix[i, j] = matrix[j, i] = matrix[i, j] * norm[i] * norm[j]
    inverse = []
    for k in range(4):
        pivot = matrix[k, k]
        inverse.append(jnp.where(pivot > 2e-6, 1.0 / jnp.maximum(pivot, 2e-6), 0.0))
        for i in range(k + 1, 4):
            factor = matrix[i, k] * inverse[k]
            for j in range(i, 4):
                matrix[i, j] = matrix[j, i] = matrix[i, j] - factor * matrix[k, j]
            side[i] = side[i] - factor * side[k]
    weights = [None] * 4
    for k in range(3, -1, -1):
        value = side[k]
        for j in range(k + 1, 4):
            value = value - matrix[k, j] * weights[j]
        weights[k] = value * inverse[k]
    real = sum(weights[k] * norm[k] * basis[k][0] for k in range(4))
    imag = sum(weights[k] * norm[k] * basis[k][1] for k in range(4))
    for t in range(3):
        pair[t, pl.ds(0, 8, stride=2), :] = real[:, 128 * t : 128 * t + 128]
        pair[t, pl.ds(1, 8, stride=2), :] = imag[:, 128 * t : 128 * t + 128]
    write(out_ref)


def local(image, sampled_lines, coil_maps, kspace, reg_weight, conv_first, conv_middle, conv_last):
    vmem = pl.BlockSpec(memory_space=pltpu.VMEM)
    anywhere = pl.BlockSpec(memory_space=pl.ANY)
    block = jax.ShapeDtypeStruct((1, XB, 2, Y), F32)
    dma = pltpu.SemaphoreType.DMA
    return pl.pallas_call(
        kernel,
        out_shape=(block, block),
        in_specs=[vmem, vmem, anywhere, anywhere, pl.BlockSpec(memory_space=pltpu.SMEM), vmem, vmem, vmem],
        out_specs=(vmem, vmem),
        scratch_shapes=[
            pltpu.VMEM((9, 24, YP), F32),
            pltpu.VMEM((3, 9, 24, YP), F32),
            pltpu.VMEM((YP, 1280), F32),
            pltpu.VMEM((256, 1280), BF16),
            pltpu.VMEM((64, 128), F32),
            pltpu.VMEM((2, 768, 256), BF16),
            pltpu.VMEM((1152, 128), F32),
            pltpu.VMEM((1152, 128), BF16),
            pltpu.VMEM((7, 10, Y, 128), BF16),
            pltpu.VMEM((5, 8, Y, 128), BF16),
            pltpu.VMEM((3, 6, Y, 128), BF16),
            pltpu.VMEM((8, Y + 16, 256), F32),
            pltpu.VMEM((YP, 256), BF16),
            pltpu.VMEM((2 * YP, 256), BF16),
            pltpu.VMEM((2 * YP, 256), BF16),
            pltpu.VMEM((YP, 128), BF16),
            pltpu.VMEM((CL, XW, 2, Y), F32),
            pltpu.VMEM((CL, XW, 2, Y), F32),
            pltpu.VMEM((C, XB, 2, Y), F32),
            pltpu.VMEM((3, 8 * C, 128), F32),
            pltpu.VMEM((4 * C, 2 * YP), F32),
            pltpu.VMEM((4 * C, YP), F32),
            pltpu.VMEM((4 * C, YP), F32),
            pltpu.VMEM((8, 8, YP), F32),
            pltpu.VMEM((8, 8, YP), F32),
            pltpu.VMEM((3, 16, 128), F32),
            pltpu.VMEM((2, 3, 8, 16, 128), F32),
            dma((3,)), dma((26,)), dma((26,)), dma((7,)), dma((7,)), dma((7,)), dma((7,)),
            dma((2, 3, 7)), dma((2, 3, 7)),
        ],
        compiler_params=pltpu.CompilerParams(
            collective_id=0, has_side_effects=True, vmem_limit_bytes=LIMIT
        ),
    )(
        image, sampled_lines, coil_maps, kspace, reg_weight,
        conv_first.reshape(27, 2, CH), conv_middle.reshape(54, CH, CH), conv_last.reshape(27, CH, 2),
    )


def solution(mesh):
    in_specs = (
        P("slab", "coil", None, None),
        P("slab", None),
        P("coil", "slab", None, None, None),
        P("coil", "slab", None, None, None),
        P(),
        P(),
        P(),
        P(),
    )
    out_specs = (P("slab", "coil", None, None), P("slab", "coil", None, None))
    return jax.shard_map(local, mesh=mesh, in_specs=in_specs, out_specs=out_specs, check_vma=False)
```

```python
import functools
import math

import jax
import jax.numpy as jnp
from jax import lax
from jax.experimental import pallas as pl
from jax.experimental.pallas import tpu as pltpu
from jax.sharding import PartitionSpec as P

MESH = pl.DeviceIdType.MESH
F32 = jnp.float32
BF16 = jnp.bfloat16

Y = 320
YP = 384
XB = 4
CH = 64
C = 32
CL = 4
NS = 80
HALO = 4
XW = 32
Z = 64
X_CHIPS = 4
Y_CHIPS = 8
Z_CHIPS = 8
CHUNK = 1
LIMIT = 56 * 2**20


def dot(a, b):
    return jnp.dot(a, b, preferred_element_type=F32)


def dot_t(a, b):
    return lax.dot_general(a, b, (((1,), (1,)), ((), ())), preferred_element_type=F32)


def split(v):
    high = v.astype(BF16)
    return high, (v - high.astype(F32)).astype(BF16)


def dot3(v, high_ref, low_ref, op):
    high, low = split(v)
    rows = v.shape[0]
    both = op(jnp.concatenate([high, low], axis=0), high_ref[...])
    return both[0:rows] + both[rows : 2 * rows] + op(high, low_ref[...])


def lane_roll(v, amount):
    return pltpu.roll(v, amount % v.shape[1], axis=1)


def kernel(
    image_ref, lines_ref, maps_hbm, kspace_hbm, reg_ref, first_ref, middle_ref, last_ref,
    denoised_ref, out_ref,
    halo, feats, w1f, w1, wt, wl, wm, w4f, w4, p1, p2, p3,
    table_hi, table_lo, pick, local_maps, local_kspace, own_maps, inter, planes, maps_re, maps_im,
    part_send, part_recv, pair, energy_out, slots,
    local_sem, img_send, img_recv, map_send, map_recv, rhs_send, rhs_recv, sum_send, sum_recv,
):
    s = lax.axis_index("slab")
    c = lax.axis_index("coil")
    x_chip, z_lo = c % X_CHIPS, c // X_CHIPS
    core, y_chip, z_hi = s % 2, (s // 2) % Y_CHIPS, s // (2 * Y_CHIPS)
    z_chip = z_hi * 2 + z_lo

    offsets = [(dz, dx) for dz in range(-HALO, HALO + 1) for dx in (-1, 0, 1) if (dz, dx) != (0, 0)]

    def shifted(dz, dx):
        return ((s + dz + Z) % Z, (c + dx + 8) % 8)

    def stage_partner(stage, d):
        if stage == 0:
            return (
                z_hi * 16 + y_chip * 2 + (core + d // 4) % 2,
                z_lo * 4 + (x_chip + d % 4) % 4,
            )
        if stage == 1:
            return (z_hi * 16 + ((y_chip + d) % 8) * 2 + core, c)
        z_new = (z_chip + d) % 8
        return ((z_new // 2) * 16 + y_chip * 2 + core, (z_new % 2) * 4 + x_chip)

    stage_index = (core * 4 + x_chip, y_chip, z_chip)

    partners = [shifted(dz, dx) for dz, dx in offsets]
    partners += [shifted(0, d) for d in range(1, 8)]
    partners += [stage_partner(stage, d) for stage in range(3) for d in range(1, 8)]
    barrier = pltpu.get_barrier_semaphore()
    for partner in partners:
        pl.semaphore_signal(barrier, inc=1, device_id=partner, device_id_type=MESH)

    local_copies = [
        pltpu.make_async_copy(maps_hbm.at[:, 0], local_maps, local_sem.at[0]),
        pltpu.make_async_copy(kspace_hbm.at[:, 0], local_kspace, local_sem.at[1]),
        pltpu.make_async_copy(
            maps_hbm.at[:, 0, pl.ds(c * XB, XB)], own_maps.at[pl.ds(c * CL, CL)], local_sem.at[2]
        ),
    ]
    for copy in local_copies:
        copy.start()

    halo[HALO, 8:16] = jnp.zeros((8, YP), F32)
    for x in range(XB):
        halo[HALO, 8 + 2 * x : 10 + 2 * x, 0:Y] = image_ref[0, x]

    pl.semaphore_wait(barrier, len(partners))

    image_copies = []
    for i, (dz, dx) in enumerate(offsets):
        copy = pltpu.make_async_remote_copy(
            src_ref=halo.at[HALO, pl.ds(8, 8)],
            dst_ref=halo.at[HALO - dz, pl.ds(8 - 8 * dx, 8)],
            send_sem=img_send.at[i],
            recv_sem=img_recv.at[i],
            device_id=shifted(dz, dx),
            device_id_type=MESH,
        )
        copy.start()
        image_copies.append(copy)
    map_copies = []
    for d in range(1, 8):
        target = (c + d) % 8
        copy = pltpu.make_async_remote_copy(
            src_ref=maps_hbm.at[:, 0, pl.ds(target * XB, XB)],
            dst_ref=own_maps.at[pl.ds(c * CL, CL)],
            send_sem=map_send.at[d - 1],
            recv_sem=map_recv.at[d - 1],
            device_id=(s, target),
            device_id_type=MESH,
        )
        copy.start()
        map_copies.append(copy)

    def phase_tables():
        lines = jnp.concatenate([lines_ref[...], jnp.full((1, 128 - NS), -1, jnp.int32)], axis=1)
        position = lax.broadcasted_iota(jnp.int32, (YP, 128), 0)
        line = jnp.broadcast_to(lines, (YP, 128))
        inside = (position < Y) & (line >= 0)
        product = (position * line).astype(F32)
        phase = product - Y * jnp.floor((product + 0.5) * (1.0 / Y))
        half = jnp.abs(jnp.where(phase > Y / 2, phase - Y, phase))
        sine_sign = jnp.where(phase > Y / 2, -1.0, 1.0)
        low_half = half <= Y / 4
        angle = jnp.where(low_half, half, Y / 2 - half) * (2.0 * math.pi / Y)
        square = angle * angle
        cosine = jnp.full((YP, 128), 1.0 / math.factorial(14), F32) * -1.0
        sine = jnp.full((YP, 128), 1.0 / math.factorial(13), F32)
        for order in range(6, -1, -1):
            cosine = cosine * square + (-1.0) ** order / math.factorial(2 * order)
            if order < 6:
                sine = sine * square + (-1.0) ** order / math.factorial(2 * order + 1)
        scale = 1.0 / math.sqrt(Y)
        cosine = jnp.where(inside, jnp.where(low_half, cosine, -cosine) * scale, 0.0)
        sine = jnp.where(inside, sine * angle * sine_sign * scale, 0.0)
        for row, column, value in (
            (0, 0, cosine), (0, 128, -sine), (YP, 0, sine), (YP, 128, cosine),
        ):
            high, low = split(value)
            table_hi[row : row + YP, column : column + 128] = high
            table_lo[row : row + YP, column : column + 128] = low
        pick[...] = jnp.where(inside & (position == line), 1.0, 0.0).astype(BF16)

    phase_tables()

    groups = inter.reshape(3, C, 8, 128)
    tiles = ((0, 128), (1, 128), (2, Y - 256))

    def plane_of(ref, start, count):
        return jnp.concatenate([ref[t, pl.ds(start, count, stride=2), :] for t in range(3)], axis=1)

    def load_planes(source):
        def move(group, carry):
            for x in range(XB):
                value = source(group, x)
                for t, width in tiles:
                    groups[t, group, 2 * x : 2 * x + 2, 0:width] = value[:, 128 * t : 128 * t + width]
            return carry

        lax.fori_loop(0, C, move, 0)
        return plane_of(inter, 0, 4 * C), plane_of(inter, 1, 4 * C)

    for copy in local_copies:
        copy.wait()
    inter[...] = jnp.zeros_like(inter)

    def phase_adjoint():
        kspace_re, kspace_im = load_planes(lambda group, x: local_kspace[group // 8, (group % 8) * XB + x])
        spectrum = []
        for plane in (kspace_re, kspace_im):
            high, low = split(plane)
            spectrum.append(dot(high, pick[...]) + dot(low, pick[...]))
        field = dot3(jnp.concatenate(spectrum, axis=1), table_hi, table_lo, dot_t)
        planes[...] = field
        s_re, s_im = load_planes(lambda group, x: local_maps[group // 8, (group % 8) * XB + x])
        energy = s_re * s_re + s_im * s_im
        energy = jnp.sum(energy.reshape(16, 8, YP), axis=0)
        energy_out[...] = energy[:, 0:128] + energy[:, 128:256] + energy[:, 256:384]
        f_re, f_im = planes[:, 0:YP], planes[:, YP : 2 * YP]
        sum_re = jnp.sum((s_re * f_re + s_im * f_im).reshape(CL, XW, YP), axis=0)
        sum_im = jnp.sum((s_re * f_im - s_im * f_re).reshape(CL, XW, YP), axis=0)
        for k in range(8):
            part_send[k, 0:4] = sum_re[4 * k : 4 * k + 4]
            part_send[k, 4:8] = sum_im[4 * k : 4 * k + 4]
        part_recv[c] = part_send[c]

    phase_adjoint()
    rhs_copies = []
    for d in range(1, 8):
        target = (c + d) % 8
        copy = pltpu.make_async_remote_copy(
            src_ref=part_send.at[target],
            dst_ref=part_recv.at[c],
            send_sem=rhs_send.at[d - 1],
            recv_sem=rhs_recv.at[d - 1],
            device_id=(s, target),
            device_id_type=MESH,
        )
        copy.start()
        rhs_copies.append(copy)

    def start_stage(which, stage, value):
        index = stage_index[stage]
        slots[which, stage, index] = value
        copies = []
        for d in range(1, 8):
            copy = pltpu.make_async_remote_copy(
                src_ref=slots.at[which, stage, index],
                dst_ref=slots.at[which, stage, index],
                send_sem=sum_send.at[which, stage, d - 1],
                recv_sem=sum_recv.at[which, stage, d - 1],
                device_id=stage_partner(stage, d),
                device_id_type=MESH,
            )
            copy.start()
            copies.append(copy)
        return copies

    def finish_stage(which, stage, copies):
        for copy in copies:
            copy.wait()
        return jnp.sum(slots[which, stage], axis=0)

    energy_copies = start_stage(0, 0, jnp.concatenate([energy_out[...], jnp.zeros((8, 128), F32)], axis=0))

    def last_all():
        wl[...] = jnp.zeros_like(wl)
        for k in range(27):
            wl[2 * k : 2 * k + 2, 0:CH] = last_ref[k].astype(F32)
        return wl[...]

    def phase_weights():
        wt[...] = jnp.zeros_like(wt)
        for dy in range(3):
            for dz in range(3):
                for dx in range(3):
                    row = 2 * (dy * 9 + dz * 3 + dx)
                    wt[row : row + 2, 0:CH] = first_ref[dz * 9 + dx * 3 + dy].astype(F32)
        w1f[...] = jnp.zeros_like(w1f)
        row8 = lax.broadcasted_iota(jnp.int32, (8, 128), 0)
        for q in range(9):
            low = jnp.where(row8 < 6, wt[6 * q : 6 * q + 8, :], 0.0)
            both = low + lane_roll(pltpu.roll(low, 2, axis=0), CH)
            for x in range(10):
                if x < 9:
                    w1f[24 * q + 2 * x : 24 * q + 2 * x + 8, 128 * x : 128 * x + 128] = both
                else:
                    w1f[24 * q + 18 : 24 * q + 24, 128 * x : 128 * x + 128] = low[0:6]
        w1[...] = w1f[0:256, :].astype(BF16)

        wm[...] = jnp.zeros_like(wm)

        def middle_weights(i, carry):
            layer, dz = i // 3, i % 3
            for dx in range(3):
                taps = [middle_ref[i * 9 + dx * 3 + dy] for dy in range(3)]
                wm[layer, pl.ds(pl.multiple_of(dz * 256 + dx * CH, CH), CH), 0:128] = jnp.concatenate([taps[0], taps[2]], axis=1)
                wm[layer, pl.ds(pl.multiple_of(dz * 256 + dx * CH, CH), CH), 128:256] = jnp.concatenate([taps[1], taps[1]], axis=1)
            return carry

        lax.fori_loop(0, 6, middle_weights, 0)

        w4f[...] = jnp.zeros_like(w4f)
        turned = jnp.transpose(last_all())[0:CH]
        column = lax.broadcasted_iota(jnp.int32, (CH, 128), 1)
        for dz in range(3):
            for dx in range(3):
                merged = None
                for dy in range(3):
                    first_column = 2 * (dz * 9 + dx * 3 + dy)
                    tap = jnp.where((column >= first_column) & (column < first_column + 2), turned, 0.0)
                    tap = lane_roll(tap, 8 * dy - first_column)
                    merged = tap if merged is None else merged + tap
                for x in range(XB):
                    base = dz * 384 + (x + dx) * CH
                    w4f[base : base + CH, :] += merged if x == 0 else lane_roll(merged, 2 * x)
        w4[...] = w4f[...].astype(BF16)

    phase_weights()

    for copy in image_copies:
        copy.wait()
    row24 = lax.broadcasted_iota(jnp.int32, (24, YP), 0) // 8 + (c - 1)

    def feature_slice(zi, carry):
        slice_index = s + zi - HALO
        valid = (row24 >= 0) & (row24 < 8) & (slice_index >= 0) & (slice_index < Z)
        value = jnp.where(valid, halo[zi].astype(BF16).astype(F32), 0.0)
        feats[0, zi] = lane_roll(value, 1)
        feats[1, zi] = value
        feats[2, zi] = lane_roll(value, -1)
        return carry

    def phase_features():
        for zi in range(2 * HALO + 1):
            feature_slice(zi, 0)

    phase_features()

    lane = lax.broadcasted_iota(jnp.int32, (1, 256), 1)

    def first_layer(z, carry):
        slice_index = s + z - 3
        slice_valid = (slice_index >= 0) & (slice_index < Z)
        columns = jnp.concatenate(
            [feats[dy, z : z + 3].reshape(72, YP) for dy in range(3)] + [jnp.zeros((40, YP), F32)],
            axis=0,
        )
        tall = jnp.transpose(columns)[0:Y].astype(BF16)
        for x in range(0, 10, 2):
            at = c * XB - 3 + x + lane // CH - lane // 128
            mask = jnp.where((at >= 0) & (at < XW) & slice_valid, 1.0, 0.0)
            product = dot(tall, w1[:, 128 * x : 128 * x + 256])
            product = (jnp.maximum(product, 0.0) * mask).astype(BF16)
            p1[z, x] = product[:, 0:128]
            p1[z, x + 1] = product[:, 128:256]
        return carry

    def phase_first():
        for z in range(7):
            first_layer(z, 0)

    phase_first()
    energy = finish_stage(0, 0, energy_copies)
    energy_copies = start_stage(0, 1, energy)

    low_lanes = lax.broadcasted_iota(jnp.int32, (Y, 128), 1) < CH

    rowi = lax.broadcasted_iota(jnp.int32, (Y, 128), 0)
    edge = jnp.where((low_lanes & (rowi == 0)) | (jnp.logical_not(low_lanes) & (rowi == Y - 1)), 0.0, 1.0)

    def middle_layer(layer, source, target, slices, rows):
        reach_z, reach_x = slices // 2, (rows - XB) // 2

        def one_slice(z, carry):
            slice_index = s + z - reach_z
            slice_valid = (slice_index >= 0) & (slice_index < Z)
            def finish(x, before):
                at = c * XB - reach_x + x
                mask = jnp.where((at >= 0) & (at < XW) & slice_valid, 1.0, 0.0).astype(F32)
                first_half = products[x][:, 0:128]
                outer = jnp.where(low_lanes, pltpu.roll(first_half, 1, axis=0), pltpu.roll(first_half, Y - 1, axis=0)) * edge
                value = outer + lane_roll(outer, CH) + products[x][:, 128:256]
                value = jnp.maximum(value, 0.0) * mask
                if before is not None:
                    target[z, x - 1] = jnp.where(low_lanes, before, value).astype(BF16)
                return value

            value = None
            products = []
            for x in range(0, rows + CHUNK, CHUNK):
                if x < rows:
                    operand = jnp.concatenate(
                        [
                            source[z + dz, x + 2 * k : x + 2 * k + CHUNK].reshape(CHUNK * Y, 128)
                            for dz in range(3)
                            for k in range(2)
                        ],
                        axis=1,
                    )
                    product = dot(operand, wm[layer])
                    products.append(product)
                if x > 0:
                    for i in range(CHUNK):
                        value = finish(x - CHUNK + i, value)
            target[z, rows - 1] = value.astype(BF16)
            return carry

        lax.fori_loop(0, slices, one_slice, 0)

    def phase_middle0():
        middle_layer(0, p1, p2, 5, 8)

    phase_middle0()
    energy = finish_stage(0, 1, energy_copies)
    energy_copies = start_stage(0, 2, energy)
    def phase_middle1():
        middle_layer(1, p2, p3, 3, 6)

    phase_middle1()
    energy = finish_stage(0, 2, energy_copies)

    def write(ref):
        for x in range(XB):
            for t, width in tiles:
                ref[0, x, :, 128 * t : 128 * t + width] = pair[t, 2 * x : 2 * x + 2, 0:width]

    def phase_last():
        operand = jnp.concatenate([p3[dz, 2 * k] for dz in range(3) for k in range(3)], axis=1)
        w1f[0:YP, 0:128] = jnp.zeros((YP, 128), F32)
        w1f[0:Y, 0:128] = dot(operand, w4[...])
        turned = jnp.transpose(w1f[0:YP, 0:128])
        residual = lane_roll(turned[0:8], 1) + turned[8:16] + lane_roll(turned[16:24], -1)
        lane8 = lax.broadcasted_iota(jnp.int32, (8, YP), 1)
        denoised = halo[HALO, 8:16] + jnp.where(lane8 < Y, residual, 0.0)
        for t in range(3):
            pair[t, 0:8] = denoised[:, 128 * t : 128 * t + 128]
            pair[t, 8:16] = denoised[:, 128 * t : 128 * t + 128]

        write(denoised_ref)

    phase_last()
    den_re, den_im = plane_of(pair, 0, 8), plane_of(pair, 1, 8)

    reg = reg_ref[0]
    for copy in rhs_copies:
        copy.wait()
    adjoint = jnp.sum(part_recv[...], axis=0)
    other = pltpu.roll(adjoint, 4, axis=0)
    first_rows = lax.broadcasted_iota(jnp.int32, (8, YP), 0) < 4
    right = (
        jnp.where(first_rows, adjoint, other) + reg * den_re,
        jnp.where(first_rows, other, adjoint) + reg * den_im,
    )
    for copy in map_copies:
        copy.wait()

    def phase_maps():
        s_re, s_im = load_planes(lambda group, x: own_maps[group, x])
        maps_re[...] = s_re
        maps_im[...] = s_im

    phase_maps()

    mean = jnp.sum(jnp.sum(energy, axis=0, keepdims=True), axis=1, keepdims=True) * (NS / Y / (Z * XW * Y))

    def spectrum_of(vector):
        v_re = jnp.broadcast_to(vector[0][None], (16, 8, YP)).reshape(128, YP)
        v_im = jnp.broadcast_to(vector[1][None], (16, 8, YP)).reshape(128, YP)
        m_re, m_im = maps_re[...], maps_im[...]
        weighted = jnp.concatenate([m_re * v_re - m_im * v_im, m_re * v_im + m_im * v_re], axis=1)
        return dot3(weighted, table_hi, table_lo, dot)

    def gram_map(vector):
        planes[...] = dot3(spectrum_of(vector), table_hi, table_lo, dot_t)
        m_re, m_im = maps_re[...], maps_im[...]
        f_re, f_im = planes[:, 0:YP], planes[:, YP : 2 * YP]
        real = jnp.sum((m_re * f_re + m_im * f_im).reshape(16, 8, YP), axis=0)
        imag = jnp.sum((m_re * f_im - m_im * f_re).reshape(16, 8, YP), axis=0)
        return real + pltpu.roll(real, 4, axis=0), imag + pltpu.roll(imag, 4, axis=0)

    def folded(first, second):
        product = first[0] * second[0] + first[1] * second[1]
        product = product[:, 0:128] + product[:, 128:256] + product[:, 256:384]
        return 0.5 * jnp.sum(product, axis=0, keepdims=True)

    pairs = [(i, j) for i in range(4) for j in range(i, 4)]
    basis = [right]

    def phase_krylov():
        del basis[1:]
        for _ in range(3):
            mapped = gram_map(basis[-1])
            basis.append((mapped[0] - mean * basis[-1][0], mapped[1] - mean * basis[-1][1]))
        last_spectrum = spectrum_of(basis[-1])
        last_energy = jnp.sum((last_spectrum * last_spectrum).reshape(16, 8, 256), axis=0)
        last_energy = last_energy[:, 0:128] + last_energy[:, 128:256]
        rows = [folded(basis[i], basis[j]) for i, j in pairs]
        rows.append(jnp.sum(last_energy, axis=0, keepdims=True))
        rows.append(jnp.zeros((16 - len(rows), 128), F32))
        moments = jnp.concatenate(rows, axis=0)
        return moments

    moments = phase_krylov()
    for stage in range(3):
        moments = finish_stage(1, stage, start_stage(1, stage, moments))
    moments = jnp.sum(moments, axis=1, keepdims=True)
    gram = {}
    for row, (i, j) in enumerate(pairs):
        gram[i, j] = gram[j, i] = moments[row : row + 1]
    shift = mean + reg
    matrix = {}
    for i in range(4):
        for j in range(i, 4):
            value = gram[i + 1, j] + shift * gram[i, j] if i < 3 else moments[10:11] + reg * gram[3, 3]
            matrix[i, j] = matrix[j, i] = value
    norm = [jnp.where(matrix[i, i] > 1e-37, lax.rsqrt(jnp.maximum(matrix[i, i], 1e-37)), 0.0) for i in range(4)]
    side = [gram[0, i] * norm[i] for i in range(4)]
    for i in range(4):
        for j in range(i, 4):
            matrix[i, j] = matrix[j, i] = matrix[i, j] * norm[i] * norm[j]
    inverse = []
    for k in range(4):
        pivot = matrix[k, k]
        inverse.append(jnp.where(pivot > 2e-6, 1.0 / jnp.maximum(pivot, 2e-6), 0.0))
        for i in range(k + 1, 4):
            factor = matrix[i, k] * inverse[k]
            for j in range(i, 4):
                matrix[i, j] = matrix[j, i] = matrix[i, j] - factor * matrix[k, j]
            side[i] = side[i] - factor * side[k]
    weights = [None] * 4
    for k in range(3, -1, -1):
        value = side[k]
        for j in range(k + 1, 4):
            value = value - matrix[k, j] * weights[j]
        weights[k] = value * inverse[k]
    real = sum(weights[k] * norm[k] * basis[k][0] for k in range(4))
    imag = sum(weights[k] * norm[k] * basis[k][1] for k in range(4))
    for t in range(3):
        pair[t, pl.ds(0, 8, stride=2), :] = real[:, 128 * t : 128 * t + 128]
        pair[t, pl.ds(1, 8, stride=2), :] = imag[:, 128 * t : 128 * t + 128]
    write(out_ref)


def local(image, sampled_lines, coil_maps, kspace, reg_weight, conv_first, conv_middle, conv_last):
    vmem = pl.BlockSpec(memory_space=pltpu.VMEM)
    anywhere = pl.BlockSpec(memory_space=pl.ANY)
    block = jax.ShapeDtypeStruct((1, XB, 2, Y), F32)
    dma = pltpu.SemaphoreType.DMA
    return pl.pallas_call(
        kernel,
        out_shape=(block, block),
        in_specs=[vmem, vmem, anywhere, anywhere, pl.BlockSpec(memory_space=pltpu.SMEM), vmem, vmem, vmem],
        out_specs=(vmem, vmem),
        scratch_shapes=[
            pltpu.VMEM((9, 24, YP), F32),
            pltpu.VMEM((3, 9, 24, YP), F32),
            pltpu.VMEM((YP, 1280), F32),
            pltpu.VMEM((256, 1280), BF16),
            pltpu.VMEM((64, 128), F32),
            pltpu.VMEM((128, 128), F32),
            pltpu.VMEM((2, 768, 256), BF16),
            pltpu.VMEM((1152, 128), F32),
            pltpu.VMEM((1152, 128), BF16),
            pltpu.VMEM((7, 10, Y, 128), BF16),
            pltpu.VMEM((5, 8, Y, 128), BF16),
            pltpu.VMEM((3, 6, Y, 128), BF16),
            pltpu.VMEM((2 * YP, 256), BF16),
            pltpu.VMEM((2 * YP, 256), BF16),
            pltpu.VMEM((YP, 128), BF16),
            pltpu.VMEM((CL, XW, 2, Y), F32),
            pltpu.VMEM((CL, XW, 2, Y), F32),
            pltpu.VMEM((C, XB, 2, Y), F32),
            pltpu.VMEM((3, 8 * C, 128), F32),
            pltpu.VMEM((4 * C, 2 * YP), F32),
            pltpu.VMEM((4 * C, YP), F32),
            pltpu.VMEM((4 * C, YP), F32),
            pltpu.VMEM((8, 8, YP), F32),
            pltpu.VMEM((8, 8, YP), F32),
            pltpu.VMEM((3, 16, 128), F32),
            pltpu.VMEM((8, 128), F32),
            pltpu.VMEM((2, 3, 8, 16, 128), F32),
            dma((3,)), dma((26,)), dma((26,)), dma((7,)), dma((7,)), dma((7,)), dma((7,)),
            dma((2, 3, 7)), dma((2, 3, 7)),
        ],
        compiler_params=pltpu.CompilerParams(
            collective_id=0, has_side_effects=True, vmem_limit_bytes=LIMIT
        ),
    )(
        image, sampled_lines, coil_maps, kspace, reg_weight,
        conv_first.reshape(27, 2, CH), conv_middle.reshape(54, CH, CH), conv_last.transpose(0, 1, 2, 4, 3).reshape(27, 2, CH),
    )


def solution(mesh):
    in_specs = (
        P("slab", "coil", None, None),
        P("slab", None),
        P("coil", "slab", None, None, None),
        P("coil", "slab", None, None, None),
        P(),
        P(),
        P(),
        P(),
    )
    out_specs = (P("slab", "coil", None, None), P("slab", "coil", None, None))
    return jax.shard_map(local, mesh=mesh, in_specs=in_specs, out_specs=out_specs, check_vma=False)
```

```python
import functools
import math

import jax
import jax.numpy as jnp
from jax import lax
from jax.experimental import pallas as pl
from jax.experimental.pallas import tpu as pltpu
from jax.sharding import PartitionSpec as P

MESH = pl.DeviceIdType.MESH
F32 = jnp.float32
BF16 = jnp.bfloat16

Y = 320
YP = 384
XB = 4
CH = 64
C = 32
CL = 4
NS = 80
HALO = 4
XW = 32
Z = 64
X_CHIPS = 4
Y_CHIPS = 8
Z_CHIPS = 8
CHUNK = 1
LIMIT = 56 * 2**20


def dot(a, b):
    return jnp.dot(a, b, preferred_element_type=F32)


def dot_t(a, b):
    return lax.dot_general(a, b, (((1,), (1,)), ((), ())), preferred_element_type=F32)


def split(v):
    high = v.astype(BF16)
    return high, (v - high.astype(F32)).astype(BF16)


def dot3(v, high_ref, low_ref, op):
    high, low = split(v)
    rows = v.shape[0]
    both = op(jnp.concatenate([high, low], axis=0), high_ref[...])
    return both[0:rows] + both[rows : 2 * rows] + op(high, low_ref[...])


def lane_roll(v, amount):
    return pltpu.roll(v, amount % v.shape[1], axis=1)


def kernel(
    image_ref, lines_ref, maps_hbm, kspace_hbm, reg_ref, first_ref, middle_ref, last_ref,
    denoised_ref, out_ref,
    halo, own_image, feats, w1f, w1, wt, wl, wm, w4f, w4, p1, p2, p3,
    table_hi, table_lo, pick, local_maps, local_kspace, own_maps, inter, planes, maps_re, maps_im,
    part_send, part_recv, pair, energy_out, slots,
    local_sem, img_send, img_recv, map_send, map_recv, rhs_send, rhs_recv, sum_send, sum_recv,
):
    s = lax.axis_index("slab")
    c = lax.axis_index("coil")
    x_chip, z_lo = c % X_CHIPS, c // X_CHIPS
    core, y_chip, z_hi = s % 2, (s // 2) % Y_CHIPS, s // (2 * Y_CHIPS)
    z_chip = z_hi * 2 + z_lo

    offsets = [(dz, dx) for dz in range(-HALO, HALO + 1) for dx in (-1, 0, 1) if (dz, dx) != (0, 0)]

    def shifted(dz, dx):
        return ((s + dz + Z) % Z, (c + dx + 8) % 8)

    def stage_partner(stage, d):
        if stage == 0:
            return (
                z_hi * 16 + y_chip * 2 + (core + d // 4) % 2,
                z_lo * 4 + (x_chip + d % 4) % 4,
            )
        if stage == 1:
            return (z_hi * 16 + ((y_chip + d) % 8) * 2 + core, c)
        z_new = (z_chip + d) % 8
        return ((z_new // 2) * 16 + y_chip * 2 + core, (z_new % 2) * 4 + x_chip)

    stage_index = (core * 4 + x_chip, y_chip, z_chip)

    partners = [shifted(dz, dx) for dz, dx in offsets]
    partners += [shifted(0, d) for d in range(1, 8)]
    partners += [stage_partner(stage, d) for stage in range(3) for d in range(1, 8)]
    barrier = pltpu.get_barrier_semaphore()
    for partner in partners:
        pl.semaphore_signal(barrier, inc=1, device_id=partner, device_id_type=MESH)

    local_copies = [
        pltpu.make_async_copy(maps_hbm.at[:, 0], local_maps, local_sem.at[0]),
        pltpu.make_async_copy(kspace_hbm.at[:, 0], local_kspace, local_sem.at[1]),
        pltpu.make_async_copy(
            maps_hbm.at[:, 0, pl.ds(c * XB, XB)], own_maps.at[pl.ds(c * CL, CL)], local_sem.at[2]
        ),
    ]
    for copy in local_copies:
        copy.start()

    own_image[...] = jnp.zeros_like(own_image)
    for x in range(XB):
        own_image[2 * x : 2 * x + 2, 0:Y] = image_ref[0, x]
    mine = own_image[...]
    tail = jnp.concatenate([mine[:, 256:384], jnp.zeros((8, 128), F32)], axis=1)
    halo[HALO, 1] = jnp.concatenate([mine[:, 0:256], tail], axis=0).astype(BF16)

    pl.semaphore_wait(barrier, len(partners))

    image_copies = []
    for i, (dz, dx) in enumerate(offsets):
        copy = pltpu.make_async_remote_copy(
            src_ref=halo.at[HALO, 1],
            dst_ref=halo.at[HALO - dz, 1 - dx],
            send_sem=img_send.at[i],
            recv_sem=img_recv.at[i],
            device_id=shifted(dz, dx),
            device_id_type=MESH,
        )
        copy.start()
        image_copies.append(copy)
    def phase_tables():
        lines = jnp.concatenate([lines_ref[...], jnp.full((1, 128 - NS), -1, jnp.int32)], axis=1)
        position = lax.broadcasted_iota(jnp.int32, (YP, 128), 0)
        line = jnp.broadcast_to(lines, (YP, 128))
        inside = (position < Y) & (line >= 0)
        product = (position * line).astype(F32)
        phase = product - Y * jnp.floor((product + 0.5) * (1.0 / Y))
        half = jnp.abs(jnp.where(phase > Y / 2, phase - Y, phase))
        sine_sign = jnp.where(phase > Y / 2, -1.0, 1.0)
        low_half = half <= Y / 4
        angle = jnp.where(low_half, half, Y / 2 - half) * (2.0 * math.pi / Y)
        square = angle * angle
        cosine = jnp.full((YP, 128), 1.0 / math.factorial(14), F32) * -1.0
        sine = jnp.full((YP, 128), 1.0 / math.factorial(13), F32)
        for order in range(6, -1, -1):
            cosine = cosine * square + (-1.0) ** order / math.factorial(2 * order)
            if order < 6:
                sine = sine * square + (-1.0) ** order / math.factorial(2 * order + 1)
        scale = 1.0 / math.sqrt(Y)
        cosine = jnp.where(inside, jnp.where(low_half, cosine, -cosine) * scale, 0.0)
        sine = jnp.where(inside, sine * angle * sine_sign * scale, 0.0)
        for row, column, value in (
            (0, 0, cosine), (0, 128, -sine), (YP, 0, sine), (YP, 128, cosine),
        ):
            high, low = split(value)
            table_hi[row : row + YP, column : column + 128] = high
            table_lo[row : row + YP, column : column + 128] = low
        pick[...] = jnp.where(inside & (position == line), 1.0, 0.0).astype(BF16)

    phase_tables()

    groups = inter.reshape(3, C, 8, 128)
    tiles = ((0, 128), (1, 128), (2, Y - 256))

    def plane_of(ref, start, count):
        return jnp.concatenate([ref[t, pl.ds(start, count, stride=2), :] for t in range(3)], axis=1)

    def load_planes(source):
        def move(group, carry):
            for x in range(XB):
                value = source(group, x)
                for t, width in tiles:
                    groups[t, group, 2 * x : 2 * x + 2, 0:width] = value[:, 128 * t : 128 * t + width]
            return carry

        lax.fori_loop(0, C, move, 0)
        return plane_of(inter, 0, 4 * C), plane_of(inter, 1, 4 * C)

    for copy in local_copies:
        copy.wait()
    inter[...] = jnp.zeros_like(inter)

    def phase_adjoint():
        kspace_re, kspace_im = load_planes(lambda group, x: local_kspace[group // 8, (group % 8) * XB + x])
        spectrum = []
        for plane in (kspace_re, kspace_im):
            high, low = split(plane)
            spectrum.append(dot(high, pick[...]) + dot(low, pick[...]))
        field = dot3(jnp.concatenate(spectrum, axis=1), table_hi, table_lo, dot_t)
        planes[...] = field
        s_re, s_im = load_planes(lambda group, x: local_maps[group // 8, (group % 8) * XB + x])
        energy = s_re * s_re + s_im * s_im
        energy = jnp.sum(energy.reshape(16, 8, YP), axis=0)
        energy_out[...] = energy[:, 0:128] + energy[:, 128:256] + energy[:, 256:384]
        f_re, f_im = planes[:, 0:YP], planes[:, YP : 2 * YP]
        sum_re = jnp.sum((s_re * f_re + s_im * f_im).reshape(CL, XW, YP), axis=0)
        sum_im = jnp.sum((s_re * f_im - s_im * f_re).reshape(CL, XW, YP), axis=0)
        for k in range(8):
            part_send[k, 0:4] = sum_re[4 * k : 4 * k + 4]
            part_send[k, 4:8] = sum_im[4 * k : 4 * k + 4]
        part_recv[c] = part_send[c]

    phase_adjoint()
    def start_stage(which, stage, value):
        index = stage_index[stage]
        slots[which, stage, index] = value
        copies = []
        for d in range(1, 8):
            copy = pltpu.make_async_remote_copy(
                src_ref=slots.at[which, stage, index],
                dst_ref=slots.at[which, stage, index],
                send_sem=sum_send.at[which, stage, d - 1],
                recv_sem=sum_recv.at[which, stage, d - 1],
                device_id=stage_partner(stage, d),
                device_id_type=MESH,
            )
            copy.start()
            copies.append(copy)
        return copies

    def finish_stage(which, stage, copies):
        for copy in copies:
            copy.wait()
        return jnp.sum(slots[which, stage], axis=0)

    energy_copies = start_stage(0, 0, jnp.sum(energy_out[...], axis=0, keepdims=True))

    def last_all():
        wl[...] = jnp.zeros_like(wl)
        for k in range(27):
            wl[2 * k : 2 * k + 2, 0:CH] = last_ref[k].astype(F32)
        return wl[...]

    def phase_weights():
        wt[...] = jnp.zeros_like(wt)
        for dy in range(3):
            for dz in range(3):
                for dx in range(3):
                    row = 2 * (dy * 9 + dz * 3 + dx)
                    wt[row : row + 2, 0:CH] = first_ref[dz * 9 + dx * 3 + dy].astype(F32)
        w1f[...] = jnp.zeros_like(w1f)
        row8 = lax.broadcasted_iota(jnp.int32, (8, 128), 0)
        for q in range(9):
            low = jnp.where(row8 < 6, wt[6 * q : 6 * q + 8, :], 0.0)
            both = low + lane_roll(pltpu.roll(low, 2, axis=0), CH)
            for x in range(10):
                if x < 9:
                    w1f[24 * q + 2 * x : 24 * q + 2 * x + 8, 128 * x : 128 * x + 128] = both
                else:
                    w1f[24 * q + 18 : 24 * q + 24, 128 * x : 128 * x + 128] = low[0:6]
        w1[...] = w1f[0:256, :].astype(BF16)

        wm[...] = jnp.zeros_like(wm)

        def middle_weights(i, carry):
            layer, dz = i // 3, i % 3
            for dx in range(3):
                taps = [middle_ref[i * 9 + dx * 3 + dy] for dy in range(3)]
                wm[layer, pl.ds(pl.multiple_of(dz * 256 + dx * CH, CH), CH), 0:128] = jnp.concatenate([taps[0], taps[2]], axis=1)
                wm[layer, pl.ds(pl.multiple_of(dz * 256 + dx * CH, CH), CH), 128:256] = jnp.concatenate([taps[1], taps[1]], axis=1)
            return carry

        lax.fori_loop(0, 6, middle_weights, 0)

        w4f[...] = jnp.zeros_like(w4f)
        turned = jnp.transpose(last_all())[0:CH]
        column = lax.broadcasted_iota(jnp.int32, (CH, 128), 1)
        for dz in range(3):
            for dx in range(3):
                merged = None
                for dy in range(3):
                    first_column = 2 * (dz * 9 + dx * 3 + dy)
                    tap = jnp.where((column >= first_column) & (column < first_column + 2), turned, 0.0)
                    tap = lane_roll(tap, 8 * dy - first_column)
                    merged = tap if merged is None else merged + tap
                for x in range(XB):
                    base = dz * 384 + (x + dx) * CH
                    w4f[base : base + CH, :] += merged if x == 0 else lane_roll(merged, 2 * x)
        w4[...] = w4f[...].astype(BF16)

    phase_weights()

    for copy in image_copies:
        copy.wait()
    energy_copies = start_stage(0, 1, finish_stage(0, 0, energy_copies))
    map_copies = []
    for d in range(1, 8):
        target = (c + d) % 8
        copy = pltpu.make_async_remote_copy(
            src_ref=maps_hbm.at[:, 0, pl.ds(target * XB, XB)],
            dst_ref=own_maps.at[pl.ds(c * CL, CL)],
            send_sem=map_send.at[d - 1],
            recv_sem=map_recv.at[d - 1],
            device_id=(s, target),
            device_id_type=MESH,
        )
        copy.start()
        map_copies.append(copy)
    rhs_copies = []
    for d in range(1, 8):
        target = (c + d) % 8
        copy = pltpu.make_async_remote_copy(
            src_ref=part_send.at[target],
            dst_ref=part_recv.at[c],
            send_sem=rhs_send.at[d - 1],
            recv_sem=rhs_recv.at[d - 1],
            device_id=(s, target),
            device_id_type=MESH,
        )
        copy.start()
        rhs_copies.append(copy)

    row24 = lax.broadcasted_iota(jnp.int32, (24, YP), 0) // 8 + (c - 1)

    def feature_slice(zi, carry):
        slice_index = s + zi - HALO
        valid = (row24 >= 0) & (row24 < 8) & (slice_index >= 0) & (slice_index < Z)
        blocks = [halo[zi, k].astype(F32) for k in range(3)]
        value = jnp.concatenate(
            [jnp.concatenate([block[0:8], block[8:16, 0:128]], axis=1) for block in blocks], axis=0
        )
        value = jnp.where(valid, value, 0.0)
        feats[0, zi] = lane_roll(value, 1)
        feats[1, zi] = value
        feats[2, zi] = lane_roll(value, -1)
        return carry

    def phase_features():
        for zi in range(2 * HALO + 1):
            feature_slice(zi, 0)

    phase_features()

    lane = lax.broadcasted_iota(jnp.int32, (1, 256), 1)

    def first_layer(z, carry):
        slice_index = s + z - 3
        slice_valid = (slice_index >= 0) & (slice_index < Z)
        columns = jnp.concatenate(
            [feats[dy, z : z + 3].reshape(72, YP) for dy in range(3)] + [jnp.zeros((40, YP), F32)],
            axis=0,
        )
        tall = jnp.transpose(columns)[0:Y].astype(BF16)
        for x in range(0, 10, 2):
            at = c * XB - 3 + x + lane // CH - lane // 128
            mask = jnp.where((at >= 0) & (at < XW) & slice_valid, 1.0, 0.0)
            product = dot(tall, w1[:, 128 * x : 128 * x + 256])
            product = (jnp.maximum(product, 0.0) * mask).astype(BF16)
            p1[z, x] = product[:, 0:128]
            p1[z, x + 1] = product[:, 128:256]
        return carry

    def phase_first():
        for z in range(7):
            first_layer(z, 0)

    phase_first()

    low_lanes = lax.broadcasted_iota(jnp.int32, (Y, 128), 1) < CH

    rowi = lax.broadcasted_iota(jnp.int32, (Y, 128), 0)
    edge = jnp.where((low_lanes & (rowi == 0)) | (jnp.logical_not(low_lanes) & (rowi == Y - 1)), 0.0, 1.0)

    def middle_layer(layer, source, target, slices, rows, begin, end):
        reach_z, reach_x = slices // 2, (rows - XB) // 2

        def one_slice(z, carry):
            slice_index = s + z - reach_z
            slice_valid = (slice_index >= 0) & (slice_index < Z)
            def finish(x, before):
                at = c * XB - reach_x + x
                mask = jnp.where((at >= 0) & (at < XW) & slice_valid, 1.0, 0.0).astype(F32)
                first_half = products[x][:, 0:128]
                outer = jnp.where(low_lanes, pltpu.roll(first_half, 1, axis=0), pltpu.roll(first_half, Y - 1, axis=0)) * edge
                value = outer + lane_roll(outer, CH) + products[x][:, 128:256]
                value = jnp.maximum(value, 0.0) * mask
                if before is not None:
                    target[z, x - 1] = jnp.where(low_lanes, before, value).astype(BF16)
                return value

            value = None
            products = []
            for x in range(0, rows + CHUNK, CHUNK):
                if x < rows:
                    operand = jnp.concatenate(
                        [
                            source[z + dz, x + 2 * k : x + 2 * k + CHUNK].reshape(CHUNK * Y, 128)
                            for dz in range(3)
                            for k in range(2)
                        ],
                        axis=1,
                    )
                    product = dot(operand, wm[layer])
                    products.append(product)
                if x > 0:
                    for i in range(CHUNK):
                        value = finish(x - CHUNK + i, value)
            target[z, rows - 1] = value.astype(BF16)
            return carry

        lax.fori_loop(begin, end, one_slice, 0)

    def phase_middle0():
        middle_layer(0, p1, p2, 5, 8, 0, 3)

    def phase_middle0b():
        middle_layer(0, p1, p2, 5, 8, 3, 5)

    phase_middle0()
    energy_copies = start_stage(0, 2, finish_stage(0, 1, energy_copies))
    phase_middle0b()
    def phase_middle1():
        middle_layer(1, p2, p3, 3, 6, 0, 3)

    phase_middle1()

    def write(ref):
        for x in range(XB):
            for t, width in tiles:
                ref[0, x, :, 128 * t : 128 * t + width] = pair[t, 2 * x : 2 * x + 2, 0:width]

    def phase_last():
        operand = jnp.concatenate([p3[dz, 2 * k] for dz in range(3) for k in range(3)], axis=1)
        w1f[0:YP, 0:128] = jnp.zeros((YP, 128), F32)
        w1f[0:Y, 0:128] = dot(operand, w4[...])
        turned = jnp.transpose(w1f[0:YP, 0:128])
        residual = lane_roll(turned[0:8], 1) + turned[8:16] + lane_roll(turned[16:24], -1)
        lane8 = lax.broadcasted_iota(jnp.int32, (8, YP), 1)
        denoised = own_image[...] + jnp.where(lane8 < Y, residual, 0.0)
        for t in range(3):
            pair[t, 0:8] = denoised[:, 128 * t : 128 * t + 128]
            pair[t, 8:16] = denoised[:, 128 * t : 128 * t + 128]

        write(denoised_ref)

    phase_last()
    den_re, den_im = plane_of(pair, 0, 8), plane_of(pair, 1, 8)

    reg = reg_ref[0]
    for copy in rhs_copies:
        copy.wait()
    adjoint = jnp.sum(part_recv[...], axis=0)
    other = pltpu.roll(adjoint, 4, axis=0)
    first_rows = lax.broadcasted_iota(jnp.int32, (8, YP), 0) < 4
    right = (
        jnp.where(first_rows, adjoint, other) + reg * den_re,
        jnp.where(first_rows, other, adjoint) + reg * den_im,
    )
    for copy in map_copies:
        copy.wait()

    def phase_maps():
        s_re, s_im = load_planes(lambda group, x: own_maps[group, x])
        maps_re[...] = s_re
        maps_im[...] = s_im

    phase_maps()
    energy = finish_stage(0, 2, energy_copies)

    mean = jnp.sum(energy, axis=1, keepdims=True) * (NS / Y / (Z * XW * Y))

    def spectrum_of(vector):
        v_re = jnp.broadcast_to(vector[0][None], (16, 8, YP)).reshape(128, YP)
        v_im = jnp.broadcast_to(vector[1][None], (16, 8, YP)).reshape(128, YP)
        m_re, m_im = maps_re[...], maps_im[...]
        weighted = jnp.concatenate([m_re * v_re - m_im * v_im, m_re * v_im + m_im * v_re], axis=1)
        return dot3(weighted, table_hi, table_lo, dot)

    def gram_map(vector):
        planes[...] = dot3(spectrum_of(vector), table_hi, table_lo, dot_t)
        m_re, m_im = maps_re[...], maps_im[...]
        f_re, f_im = planes[:, 0:YP], planes[:, YP : 2 * YP]
        real = jnp.sum((m_re * f_re + m_im * f_im).reshape(16, 8, YP), axis=0)
        imag = jnp.sum((m_re * f_im - m_im * f_re).reshape(16, 8, YP), axis=0)
        return real + pltpu.roll(real, 4, axis=0), imag + pltpu.roll(imag, 4, axis=0)

    def folded(first, second):
        product = first[0] * second[0] + first[1] * second[1]
        product = product[:, 0:128] + product[:, 128:256] + product[:, 256:384]
        return 0.5 * jnp.sum(product, axis=0, keepdims=True)

    pairs = [(i, j) for i in range(4) for j in range(i, 4)]
    basis = [right]

    def phase_krylov():
        del basis[1:]
        for _ in range(3):
            mapped = gram_map(basis[-1])
            basis.append((mapped[0] - mean * basis[-1][0], mapped[1] - mean * basis[-1][1]))
        last_spectrum = spectrum_of(basis[-1])
        last_energy = jnp.sum((last_spectrum * last_spectrum).reshape(16, 8, 256), axis=0)
        last_energy = last_energy[:, 0:128] + last_energy[:, 128:256]
        rows = [folded(basis[i], basis[j]) for i, j in pairs]
        rows.append(jnp.sum(last_energy, axis=0, keepdims=True))
        rows.append(jnp.zeros((16 - len(rows), 128), F32))
        packed = jnp.concatenate(rows, axis=0)
        for width in (64, 32, 16, 8):
            packed = packed + lane_roll(packed, width)
        place = lax.broadcasted_iota(jnp.int32, (16, 128), 1) // 8
        owner = lax.broadcasted_iota(jnp.int32, (16, 128), 0)
        return jnp.sum(jnp.where(place == owner, packed, 0.0), axis=0, keepdims=True)

    moments = phase_krylov()
    for stage in range(3):
        moments = finish_stage(1, stage, start_stage(1, stage, moments))
    place = lax.broadcasted_iota(jnp.int32, (1, 128), 1) // 8
    values = [
        jnp.sum(jnp.where(place == i, moments, 0.0), axis=1, keepdims=True) for i in range(len(pairs) + 1)
    ]
    gram = {}
    for row, (i, j) in enumerate(pairs):
        gram[i, j] = gram[j, i] = values[row]
    shift = mean + reg
    matrix = {}
    for i in range(4):
        for j in range(i, 4):
            value = gram[i + 1, j] + shift * gram[i, j] if i < 3 else values[10] + reg * gram[3, 3]
            matrix[i, j] = matrix[j, i] = value
    norm = [jnp.where(matrix[i, i] > 1e-37, lax.rsqrt(jnp.maximum(matrix[i, i], 1e-37)), 0.0) for i in range(4)]
    side = [gram[0, i] * norm[i] for i in range(4)]
    for i in range(4):
        for j in range(i, 4):
            matrix[i, j] = matrix[j, i] = matrix[i, j] * norm[i] * norm[j]
    inverse = []
    for k in range(4):
        pivot = matrix[k, k]
        inverse.append(jnp.where(pivot > 2e-6, 1.0 / jnp.maximum(pivot, 2e-6), 0.0))
        for i in range(k + 1, 4):
            factor = matrix[i, k] * inverse[k]
            for j in range(i, 4):
                matrix[i, j] = matrix[j, i] = matrix[i, j] - factor * matrix[k, j]
            side[i] = side[i] - factor * side[k]
    weights = [None] * 4
    for k in range(3, -1, -1):
        value = side[k]
        for j in range(k + 1, 4):
            value = value - matrix[k, j] * weights[j]
        weights[k] = value * inverse[k]
    real = sum(weights[k] * norm[k] * basis[k][0] for k in range(4))
    imag = sum(weights[k] * norm[k] * basis[k][1] for k in range(4))
    for t in range(3):
        pair[t, pl.ds(0, 8, stride=2), :] = real[:, 128 * t : 128 * t + 128]
        pair[t, pl.ds(1, 8, stride=2), :] = imag[:, 128 * t : 128 * t + 128]
    write(out_ref)


def local(image, sampled_lines, coil_maps, kspace, reg_weight, conv_first, conv_middle, conv_last):
    vmem = pl.BlockSpec(memory_space=pltpu.VMEM)
    anywhere = pl.BlockSpec(memory_space=pl.ANY)
    block = jax.ShapeDtypeStruct((1, XB, 2, Y), F32)
    dma = pltpu.SemaphoreType.DMA
    return pl.pallas_call(
        kernel,
        out_shape=(block, block),
        in_specs=[vmem, vmem, anywhere, anywhere, pl.BlockSpec(memory_space=pltpu.SMEM), vmem, vmem, vmem],
        out_specs=(vmem, vmem),
        scratch_shapes=[
            pltpu.VMEM((9, 3, 16, 256), BF16),
            pltpu.VMEM((8, YP), F32),
            pltpu.VMEM((3, 9, 24, YP), F32),
            pltpu.VMEM((YP, 1280), F32),
            pltpu.VMEM((256, 1280), BF16),
            pltpu.VMEM((64, 128), F32),
            pltpu.VMEM((128, 128), F32),
            pltpu.VMEM((2, 768, 256), BF16),
            pltpu.VMEM((1152, 128), F32),
            pltpu.VMEM((1152, 128), BF16),
            pltpu.VMEM((7, 10, Y, 128), BF16),
            pltpu.VMEM((5, 8, Y, 128), BF16),
            pltpu.VMEM((3, 6, Y, 128), BF16),
            pltpu.VMEM((2 * YP, 256), BF16),
            pltpu.VMEM((2 * YP, 256), BF16),
            pltpu.VMEM((YP, 128), BF16),
            pltpu.VMEM((CL, XW, 2, Y), F32),
            pltpu.VMEM((CL, XW, 2, Y), F32),
            pltpu.VMEM((C, XB, 2, Y), F32),
            pltpu.VMEM((3, 8 * C, 128), F32),
            pltpu.VMEM((4 * C, 2 * YP), F32),
            pltpu.VMEM((4 * C, YP), F32),
            pltpu.VMEM((4 * C, YP), F32),
            pltpu.VMEM((8, 8, YP), F32),
            pltpu.VMEM((8, 8, YP), F32),
            pltpu.VMEM((3, 16, 128), F32),
            pltpu.VMEM((8, 128), F32),
            pltpu.VMEM((2, 3, 8, 1, 128), F32),
            dma((3,)), dma((26,)), dma((26,)), dma((7,)), dma((7,)), dma((7,)), dma((7,)),
            dma((2, 3, 7)), dma((2, 3, 7)),
        ],
        compiler_params=pltpu.CompilerParams(
            collective_id=0, has_side_effects=True, vmem_limit_bytes=LIMIT
        ),
    )(
        image, sampled_lines, coil_maps, kspace, reg_weight,
        conv_first.reshape(27, 2, CH), conv_middle.reshape(54, CH, CH), conv_last.transpose(0, 1, 2, 4, 3).reshape(27, 2, CH),
    )


def solution(mesh):
    in_specs = (
        P("slab", "coil", None, None),
        P("slab", None),
        P("coil", "slab", None, None, None),
        P("coil", "slab", None, None, None),
        P(),
        P(),
        P(),
        P(),
    )
    out_specs = (P("slab", "coil", None, None), P("slab", "coil", None, None))
    return jax.shard_map(local, mesh=mesh, in_specs=in_specs, out_specs=out_specs, check_vma=False)
```

```python
import functools
import math

import jax
import jax.numpy as jnp
from jax import lax
from jax.experimental import pallas as pl
from jax.experimental.pallas import tpu as pltpu
from jax.sharding import PartitionSpec as P

MESH = pl.DeviceIdType.MESH
F32 = jnp.float32
BF16 = jnp.bfloat16

Y = 320
YP = 384
XB = 4
CH = 64
C = 32
CL = 4
NS = 80
HALO = 4
XW = 32
Z = 64
X_CHIPS = 4
Y_CHIPS = 8
Z_CHIPS = 8
LIMIT = 56 * 2**20


def dot(a, b):
    return jnp.dot(a, b, preferred_element_type=F32)


def dot_t(a, b):
    return lax.dot_general(a, b, (((1,), (1,)), ((), ())), preferred_element_type=F32)


def split(v):
    high = v.astype(BF16)
    return high, (v - high.astype(F32)).astype(BF16)


def dot3(v, high_ref, low_ref, op):
    high, low = split(v)
    rows = v.shape[0]
    both = op(jnp.concatenate([high, low], axis=0), high_ref[...])
    return both[0:rows] + both[rows : 2 * rows] + op(high, low_ref[...])


def lane_roll(v, amount):
    return pltpu.roll(v, amount % v.shape[1], axis=1)


def kernel(
    image_ref, lines_ref, maps_hbm, kspace_hbm, reg_ref, first_ref, middle_ref, last_ref,
    denoised_ref, out_ref,
    halo, own_image, feats, w1f, w1, wt, wl, wm, w4f, w4, p1, p2, p3,
    table_hi, table_lo, pick, local_maps, local_kspace, own_maps, inter, planes, maps_re, maps_im,
    part_send, part_recv, pair, energy_out, slots,
    local_sem, img_send, img_recv, map_send, map_recv, rhs_send, rhs_recv, sum_send, sum_recv,
    core_send, core_recv,
):
    s = lax.axis_index("slab")
    c = lax.axis_index("coil")
    x_chip, z_lo = c % X_CHIPS, c // X_CHIPS
    core, y_chip, z_hi = s % 2, (s // 2) % Y_CHIPS, s // (2 * Y_CHIPS)
    z_chip = z_hi * 2 + z_lo

    outward = 2 * core - 1
    offsets = [(r, dx) for r in range(-1, HALO + 1) for dx in (-1, 0, 1) if (r, dx) != (0, 0)]

    def needing(r, dx):
        away = r if r % 2 == 0 else -r
        return ((s - outward * away + Z) % Z, (c + dx + 8) % 8)

    def stage_partner(stage, d):
        if stage == 0:
            return (
                z_hi * 16 + y_chip * 2 + (core + d // 4) % 2,
                z_lo * 4 + (x_chip + d % 4) % 4,
            )
        if stage == 1:
            return (z_hi * 16 + ((y_chip + d) % 8) * 2 + core, c)
        z_new = (z_chip + d) % 8
        return ((z_new // 2) * 16 + y_chip * 2 + core, (z_new % 2) * 4 + x_chip)

    stage_index = (core * 4 + x_chip, y_chip, z_chip)

    partners = [((s + outward * r + Z) % Z, (c + dx + 8) % 8) for r, dx in offsets]
    partners += [(s, (c + d) % 8) for d in range(1, 8)]
    partners += [stage_partner(stage, d) for stage in range(3) for d in range(1, 8)]
    barrier = pltpu.get_barrier_semaphore()
    for partner in partners:
        pl.semaphore_signal(barrier, inc=1, device_id=partner, device_id_type=MESH)

    local_copies = [
        pltpu.make_async_copy(maps_hbm.at[:, 0], local_maps, local_sem.at[0]),
        pltpu.make_async_copy(kspace_hbm.at[:, 0], local_kspace, local_sem.at[1]),
        pltpu.make_async_copy(
            maps_hbm.at[:, 0, pl.ds(c * XB, XB)], own_maps.at[pl.ds(c * CL, CL)], local_sem.at[2]
        ),
    ]
    for copy in local_copies:
        copy.start()

    own_image[...] = jnp.zeros_like(own_image)
    for x in range(XB):
        own_image[2 * x : 2 * x + 2, 0:Y] = image_ref[0, x]
    mine = own_image[...]
    tail = jnp.concatenate([mine[:, 256:384], jnp.zeros((8, 128), F32)], axis=1)
    halo[1, 1] = jnp.concatenate([mine[:, 0:256], tail], axis=0).astype(BF16)

    pl.semaphore_wait(barrier, len(partners))

    image_copies = {}
    for i, (r, dx) in enumerate(offsets):
        copy = pltpu.make_async_remote_copy(
            src_ref=halo.at[1, 1],
            dst_ref=halo.at[r + 1, 1 - dx],
            send_sem=img_send.at[i],
            recv_sem=img_recv.at[i],
            device_id=needing(r, dx),
            device_id_type=MESH,
        )
        copy.start()
        image_copies[r, dx] = copy
    def phase_tables():
        lines = jnp.concatenate([lines_ref[...], jnp.full((1, 128 - NS), -1, jnp.int32)], axis=1)
        position = lax.broadcasted_iota(jnp.int32, (YP, 128), 0)
        line = jnp.broadcast_to(lines, (YP, 128))
        inside = (position < Y) & (line >= 0)
        product = (position * line).astype(F32)
        phase = product - Y * jnp.floor((product + 0.5) * (1.0 / Y))
        half = jnp.abs(jnp.where(phase > Y / 2, phase - Y, phase))
        sine_sign = jnp.where(phase > Y / 2, -1.0, 1.0)
        low_half = half <= Y / 4
        angle = jnp.where(low_half, half, Y / 2 - half) * (2.0 * math.pi / Y)
        square = angle * angle
        cosine = jnp.full((YP, 128), 1.0 / math.factorial(14), F32) * -1.0
        sine = jnp.full((YP, 128), 1.0 / math.factorial(13), F32)
        for order in range(6, -1, -1):
            cosine = cosine * square + (-1.0) ** order / math.factorial(2 * order)
            if order < 6:
                sine = sine * square + (-1.0) ** order / math.factorial(2 * order + 1)
        scale = 1.0 / math.sqrt(Y)
        cosine = jnp.where(inside, jnp.where(low_half, cosine, -cosine) * scale, 0.0)
        sine = jnp.where(inside, sine * angle * sine_sign * scale, 0.0)
        for row, column, value in (
            (0, 0, cosine), (0, 128, -sine), (YP, 0, sine), (YP, 128, cosine),
        ):
            high, low = split(value)
            table_hi[row : row + YP, column : column + 128] = high
            table_lo[row : row + YP, column : column + 128] = low
        pick[...] = jnp.where(inside & (position == line), 1.0, 0.0).astype(BF16)

    phase_tables()

    groups = inter.reshape(3, C, 8, 128)
    tiles = ((0, 128), (1, 128), (2, Y - 256))

    def plane_of(ref, start, count):
        return jnp.concatenate([ref[t, pl.ds(start, count, stride=2), :] for t in range(3)], axis=1)

    def load_planes(source):
        def move(group, carry):
            for x in range(XB):
                value = source(group, x)
                for t, width in tiles:
                    groups[t, group, 2 * x : 2 * x + 2, 0:width] = value[:, 128 * t : 128 * t + width]
            return carry

        lax.fori_loop(0, C, move, 0)
        return plane_of(inter, 0, 4 * C), plane_of(inter, 1, 4 * C)

    for copy in local_copies:
        copy.wait()
    inter[...] = jnp.zeros_like(inter)

    def phase_adjoint():
        kspace_re, kspace_im = load_planes(lambda group, x: local_kspace[group // 8, (group % 8) * XB + x])
        spectrum = []
        for plane in (kspace_re, kspace_im):
            high, low = split(plane)
            spectrum.append(dot(high, pick[...]) + dot(low, pick[...]))
        field = dot3(jnp.concatenate(spectrum, axis=1), table_hi, table_lo, dot_t)
        planes[...] = field
        s_re, s_im = load_planes(lambda group, x: local_maps[group // 8, (group % 8) * XB + x])
        energy = s_re * s_re + s_im * s_im
        energy = jnp.sum(energy.reshape(16, 8, YP), axis=0)
        energy_out[...] = energy[:, 0:128] + energy[:, 128:256] + energy[:, 256:384]
        f_re, f_im = planes[:, 0:YP], planes[:, YP : 2 * YP]
        sum_re = jnp.sum((s_re * f_re + s_im * f_im).reshape(CL, XW, YP), axis=0)
        sum_im = jnp.sum((s_re * f_im - s_im * f_re).reshape(CL, XW, YP), axis=0)
        for k in range(8):
            part_send[k, 0:4] = sum_re[4 * k : 4 * k + 4]
            part_send[k, 4:8] = sum_im[4 * k : 4 * k + 4]
        part_recv[c] = part_send[c]

    phase_adjoint()
    def start_stage(which, stage, value):
        index = stage_index[stage]
        slots[which, stage, index] = value
        copies = []
        for d in range(1, 8):
            copy = pltpu.make_async_remote_copy(
                src_ref=slots.at[which, stage, index],
                dst_ref=slots.at[which, stage, index],
                send_sem=sum_send.at[which, stage, d - 1],
                recv_sem=sum_recv.at[which, stage, d - 1],
                device_id=stage_partner(stage, d),
                device_id_type=MESH,
            )
            copy.start()
            copies.append(copy)
        return copies

    def finish_stage(which, stage, copies):
        for copy in copies:
            copy.wait()
        return jnp.sum(slots[which, stage], axis=0)

    energy_copies = start_stage(0, 0, jnp.sum(energy_out[...], axis=0, keepdims=True))

    def tap_slice(dz):
        return dz * core + (2 - dz) * (1 - core)

    def last_all():
        wl[...] = jnp.zeros_like(wl)
        for k in range(27):
            wl[2 * k : 2 * k + 2, 0:CH] = last_ref[tap_slice(k // 9) * 9 + k % 9].astype(F32)
        return wl[...]

    def phase_weights():
        wt[...] = jnp.zeros_like(wt)
        for dy in range(3):
            for dz in range(3):
                for dx in range(3):
                    row = 2 * (dy * 9 + dz * 3 + dx)
                    wt[row : row + 2, 0:CH] = first_ref[tap_slice(dz) * 9 + dx * 3 + dy].astype(F32)
        w1f[...] = jnp.zeros_like(w1f)
        row8 = lax.broadcasted_iota(jnp.int32, (8, 128), 0)
        for q in range(9):
            low = jnp.where(row8 < 6, wt[6 * q : 6 * q + 8, :], 0.0)
            both = low + lane_roll(pltpu.roll(low, 2, axis=0), CH)
            for x in range(10):
                if x < 9:
                    w1f[24 * q + 2 * x : 24 * q + 2 * x + 8, 128 * x : 128 * x + 128] = both
                else:
                    w1f[24 * q + 18 : 24 * q + 24, 128 * x : 128 * x + 128] = low[0:6]
        w1[...] = w1f[0:256, :].astype(BF16)

        wm[...] = jnp.zeros_like(wm)

        def middle_weights(i, carry):
            layer, dz = i // 3, i % 3
            for dx in range(3):
                taps = [middle_ref[layer * 27 + tap_slice(dz) * 9 + dx * 3 + dy] for dy in range(3)]
                wm[layer, pl.ds(pl.multiple_of(dz * 256 + dx * CH, CH), CH), 0:128] = jnp.concatenate([taps[0], taps[2]], axis=1)
                wm[layer, pl.ds(pl.multiple_of(dz * 256 + dx * CH, CH), CH), 128:256] = jnp.concatenate([taps[1], taps[1]], axis=1)
            return carry

        lax.fori_loop(0, 6, middle_weights, 0)

        w4f[...] = jnp.zeros_like(w4f)
        turned = jnp.transpose(last_all())[0:CH]
        column = lax.broadcasted_iota(jnp.int32, (CH, 128), 1)
        for dz in range(3):
            for dx in range(3):
                merged = None
                for dy in range(3):
                    first_column = 2 * (dz * 9 + dx * 3 + dy)
                    tap = jnp.where((column >= first_column) & (column < first_column + 2), turned, 0.0)
                    tap = lane_roll(tap, 8 * dy - first_column)
                    merged = tap if merged is None else merged + tap
                for x in range(XB):
                    base = dz * 384 + (x + dx) * CH
                    w4f[base : base + CH, :] += merged if x == 0 else lane_roll(merged, 2 * x)
        w4[...] = w4f[...].astype(BF16)

    phase_weights()

    for (r, _), copy in image_copies.items():
        if r <= 1:
            copy.wait()
    energy_copies = start_stage(0, 1, finish_stage(0, 0, energy_copies))
    row24 = lax.broadcasted_iota(jnp.int32, (24, YP), 0) // 8 + (c - 1)

    def feature_slice(zi):
        slice_index = s + outward * (zi - 1)
        valid = (row24 >= 0) & (row24 < 8) & (slice_index >= 0) & (slice_index < Z)
        blocks = [halo[zi, k].astype(F32) for k in range(3)]
        value = jnp.concatenate(
            [jnp.concatenate([block[0:8], block[8:16, 0:128]], axis=1) for block in blocks], axis=0
        )
        value = jnp.where(valid, value, 0.0)
        feats[0, zi] = lane_roll(value, 1)
        feats[1, zi] = value
        feats[2, zi] = lane_roll(value, -1)

    lane = lax.broadcasted_iota(jnp.int32, (1, 256), 1)

    def first_layer(z):
        slice_index = s + outward * z
        slice_valid = (slice_index >= 0) & (slice_index < Z)
        columns = jnp.concatenate(
            [feats[dy, z : z + 3].reshape(72, YP) for dy in range(3)] + [jnp.zeros((40, YP), F32)],
            axis=0,
        )
        tall = jnp.transpose(columns)[0:Y].astype(BF16)
        for x in range(0, 10, 2):
            at = c * XB - 3 + x + lane // CH - lane // 128
            mask = jnp.where((at >= 0) & (at < XW) & slice_valid, 1.0, 0.0)
            product = dot(tall, w1[:, 128 * x : 128 * x + 256])
            product = (jnp.maximum(product, 0.0) * mask).astype(BF16)
            p1[z + 1, x] = product[:, 0:128]
            p1[z + 1, x + 1] = product[:, 128:256]

    low_lanes = lax.broadcasted_iota(jnp.int32, (Y, 128), 1) < CH

    rowi = lax.broadcasted_iota(jnp.int32, (Y, 128), 0)
    edge = jnp.where((low_lanes & (rowi == 0)) | (jnp.logical_not(low_lanes) & (rowi == Y - 1)), 0.0, 1.0)

    def middle_slice(layer, source, target, rows, z, sent=()):
        reach_x = (rows - XB) // 2
        slice_index = s + outward * z
        slice_valid = (slice_index >= 0) & (slice_index < Z)
        before = None
        for x in range(rows):
            operand = jnp.concatenate(
                [source[z + dz, x + 2 * k] for dz in range(3) for k in range(2)], axis=1
            )
            product = dot(operand, wm[layer])
            at = c * XB - reach_x + x
            mask = jnp.where((at >= 0) & (at < XW) & slice_valid, 1.0, 0.0).astype(F32)
            first_half = product[:, 0:128]
            outer = jnp.where(
                low_lanes, pltpu.roll(first_half, 1, axis=0), pltpu.roll(first_half, Y - 1, axis=0)
            )
            outer = outer * edge
            value = outer + lane_roll(outer, CH) + product[:, 128:256]
            value = jnp.maximum(value, 0.0) * mask
            if before is not None:
                target[z + 1, x - 1] = jnp.where(low_lanes, before, value).astype(BF16)
            before = value
            for count, copy in sent:
                if count == x:
                    copy.start()
        target[z + 1, rows - 1] = before.astype(BF16)
        for count, copy in sent:
            if count == rows:
                copy.start()

    def to_other_core(ref, blocks, index):
        return pltpu.make_async_remote_copy(
            src_ref=ref.at[1, blocks],
            dst_ref=ref.at[0, blocks],
            send_sem=core_send.at[index],
            recv_sem=core_recv.at[index],
            device_id=(s + 1 - 2 * core, c),
            device_id_type=MESH,
        )

    first_copy = to_other_core(p1, pl.ds(0, 10), 0)
    middle_copies = [(4, to_other_core(p2, pl.ds(0, 4), 1)), (8, to_other_core(p2, pl.ds(4, 4), 2))]
    hidden_copies = [(x + 1, to_other_core(p3, pl.ds(x, 1), 3 + x // 2)) for x in (0, 2, 4)]

    def phase_firstA():
        for zi in range(3):
            feature_slice(zi)
        first_layer(0)

    phase_firstA()
    first_copy.start()
    map_copies = []
    for d in range(1, 8):
        target = (c + d) % 8
        copy = pltpu.make_async_remote_copy(
            src_ref=maps_hbm.at[:, 0, pl.ds(target * XB, XB)],
            dst_ref=own_maps.at[pl.ds(c * CL, CL)],
            send_sem=map_send.at[d - 1],
            recv_sem=map_recv.at[d - 1],
            device_id=(s, target),
            device_id_type=MESH,
        )
        copy.start()
        map_copies.append(copy)
    rhs_copies = []
    for d in range(1, 8):
        target = (c + d) % 8
        copy = pltpu.make_async_remote_copy(
            src_ref=part_send.at[target],
            dst_ref=part_recv.at[c],
            send_sem=rhs_send.at[d - 1],
            recv_sem=rhs_recv.at[d - 1],
            device_id=(s, target),
            device_id_type=MESH,
        )
        copy.start()
        rhs_copies.append(copy)
    for z in range(1, 4):
        for dx in (-1, 0, 1):
            image_copies[z + 1, dx].wait()
        feature_slice(z + 2)
        first_layer(z)

    def phase_middleA():
        middle_slice(0, p1, p2, 8, 2)

    phase_middleA()
    first_copy.wait()

    def phase_middleB():
        middle_slice(0, p1, p2, 8, 0, middle_copies)

    phase_middleB()
    energy_copies = start_stage(0, 2, finish_stage(0, 1, energy_copies))

    def phase_middleC():
        middle_slice(0, p1, p2, 8, 1)

    phase_middleC()
    for _, copy in middle_copies:
        copy.wait()

    def phase_hiddenA():
        middle_slice(1, p2, p3, 6, 0, hidden_copies)

    phase_hiddenA()

    def phase_hiddenB():
        middle_slice(1, p2, p3, 6, 1)

    phase_hiddenB()

    def write(ref):
        for x in range(XB):
            for t, width in tiles:
                ref[0, x, :, 128 * t : 128 * t + width] = pair[t, 2 * x : 2 * x + 2, 0:width]

    for copy in map_copies:
        copy.wait()

    def phase_maps():
        s_re, s_im = load_planes(lambda group, x: own_maps[group, x])
        maps_re[...] = s_re
        maps_im[...] = s_im

    phase_maps()
    for _, copy in hidden_copies:
        copy.wait()

    def phase_last():
        operand = jnp.concatenate([p3[dz, 2 * k] for dz in range(3) for k in range(3)], axis=1)
        w1f[0:YP, 0:128] = jnp.zeros((YP, 128), F32)
        w1f[0:Y, 0:128] = dot(operand, w4[...])
        turned = jnp.transpose(w1f[0:YP, 0:128])
        residual = lane_roll(turned[0:8], 1) + turned[8:16] + lane_roll(turned[16:24], -1)
        lane8 = lax.broadcasted_iota(jnp.int32, (8, YP), 1)
        denoised = own_image[...] + jnp.where(lane8 < Y, residual, 0.0)
        for t in range(3):
            pair[t, 0:8] = denoised[:, 128 * t : 128 * t + 128]
            pair[t, 8:16] = denoised[:, 128 * t : 128 * t + 128]

        write(denoised_ref)

    phase_last()
    den_re, den_im = plane_of(pair, 0, 8), plane_of(pair, 1, 8)

    reg = reg_ref[0]
    for copy in rhs_copies:
        copy.wait()
    adjoint = jnp.sum(part_recv[...], axis=0)
    other = pltpu.roll(adjoint, 4, axis=0)
    first_rows = lax.broadcasted_iota(jnp.int32, (8, YP), 0) < 4
    right = (
        jnp.where(first_rows, adjoint, other) + reg * den_re,
        jnp.where(first_rows, other, adjoint) + reg * den_im,
    )
    energy = finish_stage(0, 2, energy_copies)

    mean = jnp.sum(energy, axis=1, keepdims=True) * (NS / Y / (Z * XW * Y))

    def spectrum_of(vector):
        v_re = jnp.broadcast_to(vector[0][None], (16, 8, YP)).reshape(128, YP)
        v_im = jnp.broadcast_to(vector[1][None], (16, 8, YP)).reshape(128, YP)
        m_re, m_im = maps_re[...], maps_im[...]
        weighted = jnp.concatenate([m_re * v_re - m_im * v_im, m_re * v_im + m_im * v_re], axis=1)
        return dot3(weighted, table_hi, table_lo, dot)

    def gram_map(vector):
        planes[...] = dot3(spectrum_of(vector), table_hi, table_lo, dot_t)
        m_re, m_im = maps_re[...], maps_im[...]
        f_re, f_im = planes[:, 0:YP], planes[:, YP : 2 * YP]
        real = jnp.sum((m_re * f_re + m_im * f_im).reshape(16, 8, YP), axis=0)
        imag = jnp.sum((m_re * f_im - m_im * f_re).reshape(16, 8, YP), axis=0)
        return real + pltpu.roll(real, 4, axis=0), imag + pltpu.roll(imag, 4, axis=0)

    def folded(first, second):
        product = first[0] * second[0] + first[1] * second[1]
        product = product[:, 0:128] + product[:, 128:256] + product[:, 256:384]
        return 0.5 * jnp.sum(product, axis=0, keepdims=True)

    pairs = [(i, j) for i in range(4) for j in range(i, 4)]
    basis = [right]

    def phase_krylov():
        del basis[1:]
        for _ in range(3):
            mapped = gram_map(basis[-1])
            basis.append((mapped[0] - mean * basis[-1][0], mapped[1] - mean * basis[-1][1]))
        last_spectrum = spectrum_of(basis[-1])
        last_energy = jnp.sum((last_spectrum * last_spectrum).reshape(16, 8, 256), axis=0)
        last_energy = last_energy[:, 0:128] + last_energy[:, 128:256]
        rows = [folded(basis[i], basis[j]) for i, j in pairs]
        rows.append(jnp.sum(last_energy, axis=0, keepdims=True))
        rows.append(jnp.zeros((16 - len(rows), 128), F32))
        packed = jnp.concatenate(rows, axis=0)
        for width in (64, 32, 16, 8):
            packed = packed + lane_roll(packed, width)
        place = lax.broadcasted_iota(jnp.int32, (16, 128), 1) // 8
        owner = lax.broadcasted_iota(jnp.int32, (16, 128), 0)
        return jnp.sum(jnp.where(place == owner, packed, 0.0), axis=0, keepdims=True)

    moments = phase_krylov()
    for stage in range(3):
        moments = finish_stage(1, stage, start_stage(1, stage, moments))
    place = lax.broadcasted_iota(jnp.int32, (1, 128), 1) // 8
    values = [
        jnp.sum(jnp.where(place == i, moments, 0.0), axis=1, keepdims=True) for i in range(len(pairs) + 1)
    ]
    gram = {}
    for row, (i, j) in enumerate(pairs):
        gram[i, j] = gram[j, i] = values[row]
    shift = mean + reg
    matrix = {}
    for i in range(4):
        for j in range(i, 4):
            value = gram[i + 1, j] + shift * gram[i, j] if i < 3 else values[10] + reg * gram[3, 3]
            matrix[i, j] = matrix[j, i] = value
    norm = [jnp.where(matrix[i, i] > 1e-37, lax.rsqrt(jnp.maximum(matrix[i, i], 1e-37)), 0.0) for i in range(4)]
    side = [gram[0, i] * norm[i] for i in range(4)]
    for i in range(4):
        for j in range(i, 4):
            matrix[i, j] = matrix[j, i] = matrix[i, j] * norm[i] * norm[j]
    inverse = []
    for k in range(4):
        pivot = matrix[k, k]
        inverse.append(jnp.where(pivot > 2e-6, 1.0 / jnp.maximum(pivot, 2e-6), 0.0))
        for i in range(k + 1, 4):
            factor = matrix[i, k] * inverse[k]
            for j in range(i, 4):
                matrix[i, j] = matrix[j, i] = matrix[i, j] - factor * matrix[k, j]
            side[i] = side[i] - factor * side[k]
    weights = [None] * 4
    for k in range(3, -1, -1):
        value = side[k]
        for j in range(k + 1, 4):
            value = value - matrix[k, j] * weights[j]
        weights[k] = value * inverse[k]
    real = sum(weights[k] * norm[k] * basis[k][0] for k in range(4))
    imag = sum(weights[k] * norm[k] * basis[k][1] for k in range(4))
    for t in range(3):
        pair[t, pl.ds(0, 8, stride=2), :] = real[:, 128 * t : 128 * t + 128]
        pair[t, pl.ds(1, 8, stride=2), :] = imag[:, 128 * t : 128 * t + 128]
    write(out_ref)


def local(image, sampled_lines, coil_maps, kspace, reg_weight, conv_first, conv_middle, conv_last):
    vmem = pl.BlockSpec(memory_space=pltpu.VMEM)
    anywhere = pl.BlockSpec(memory_space=pl.ANY)
    block = jax.ShapeDtypeStruct((1, XB, 2, Y), F32)
    dma = pltpu.SemaphoreType.DMA
    return pl.pallas_call(
        kernel,
        out_shape=(block, block),
        in_specs=[vmem, vmem, anywhere, anywhere, pl.BlockSpec(memory_space=pltpu.SMEM), vmem, vmem, vmem],
        out_specs=(vmem, vmem),
        scratch_shapes=[
            pltpu.VMEM((6, 3, 16, 256), BF16),
            pltpu.VMEM((8, YP), F32),
            pltpu.VMEM((3, 6, 24, YP), F32),
            pltpu.VMEM((YP, 1280), F32),
            pltpu.VMEM((256, 1280), BF16),
            pltpu.VMEM((64, 128), F32),
            pltpu.VMEM((128, 128), F32),
            pltpu.VMEM((2, 768, 256), BF16),
            pltpu.VMEM((1152, 128), F32),
            pltpu.VMEM((1152, 128), BF16),
            pltpu.VMEM((5, 10, Y, 128), BF16),
            pltpu.VMEM((4, 8, Y, 128), BF16),
            pltpu.VMEM((3, 6, Y, 128), BF16),
            pltpu.VMEM((2 * YP, 256), BF16),
            pltpu.VMEM((2 * YP, 256), BF16),
            pltpu.VMEM((YP, 128), BF16),
            pltpu.VMEM((CL, XW, 2, Y), F32),
            pltpu.VMEM((CL, XW, 2, Y), F32),
            pltpu.VMEM((C, XB, 2, Y), F32),
            pltpu.VMEM((3, 8 * C, 128), F32),
            pltpu.VMEM((4 * C, 2 * YP), F32),
            pltpu.VMEM((4 * C, YP), F32),
            pltpu.VMEM((4 * C, YP), F32),
            pltpu.VMEM((8, 8, YP), F32),
            pltpu.VMEM((8, 8, YP), F32),
            pltpu.VMEM((3, 16, 128), F32),
            pltpu.VMEM((8, 128), F32),
            pltpu.VMEM((2, 3, 8, 1, 128), F32),
            dma((3,)), dma((17,)), dma((17,)), dma((7,)), dma((7,)), dma((7,)), dma((7,)),
            dma((2, 3, 7)), dma((2, 3, 7)), dma((6,)), dma((6,)),
        ],
        compiler_params=pltpu.CompilerParams(
            collective_id=0, has_side_effects=True, vmem_limit_bytes=LIMIT
        ),
    )(
        image, sampled_lines, coil_maps, kspace, reg_weight,
        conv_first.reshape(27, 2, CH), conv_middle.reshape(54, CH, CH), conv_last.transpose(0, 1, 2, 4, 3).reshape(27, 2, CH),
    )


def solution(mesh):
    in_specs = (
        P("slab", "coil", None, None),
        P("slab", None),
        P("coil", "slab", None, None, None),
        P("coil", "slab", None, None, None),
        P(),
        P(),
        P(),
        P(),
    )
    out_specs = (P("slab", "coil", None, None), P("slab", "coil", None, None))
    return jax.shard_map(local, mesh=mesh, in_specs=in_specs, out_specs=out_specs, check_vma=False)
```

```python
import functools
import math

import jax
import jax.numpy as jnp
from jax import lax
from jax.experimental import pallas as pl
from jax.experimental.pallas import tpu as pltpu
from jax.sharding import PartitionSpec as P

MESH = pl.DeviceIdType.MESH
F32 = jnp.float32
BF16 = jnp.bfloat16

Y = 320
YP = 384
XB = 4
CH = 64
C = 32
CL = 4
NS = 80
HALO = 4
XW = 32
Z = 64
X_CHIPS = 4
Y_CHIPS = 8
Z_CHIPS = 8
LIMIT = 56 * 2**20


def dot(a, b):
    return jnp.dot(a, b, preferred_element_type=F32)


def dot_t(a, b):
    return lax.dot_general(a, b, (((1,), (1,)), ((), ())), preferred_element_type=F32)


def split(v):
    high = v.astype(BF16)
    return high, (v - high.astype(F32)).astype(BF16)


def dot3(v, high_ref, low_ref, op):
    high, low = split(v)
    rows = v.shape[0]
    both = op(jnp.concatenate([high, low], axis=0), high_ref[...])
    return both[0:rows] + both[rows : 2 * rows] + op(high, low_ref[...])


def lane_roll(v, amount):
    return pltpu.roll(v, amount % v.shape[1], axis=1)


def kernel(
    image_hbm, lines_hbm, maps_hbm, kspace_hbm, reg_hbm, first_hbm, middle_hbm, last_hbm,
    denoised_ref, out_ref,
    image_ref, lines_ref, reg_ref, first_ref, middle_ref, last_ref,
    halo, own_image, feats, w1f, w1, wt, wl, wm, w4f, w4, p1, p2, p3,
    table_hi, table_lo, pick, local_maps, local_kspace, own_maps, inter, planes, maps_re, maps_im,
    part_send, part_recv, pair, energy_out, slots,
    local_sem, img_send, img_recv, map_send, map_recv, rhs_send, rhs_recv, sum_send, sum_recv,
    core_send, core_recv,
):
    s = lax.axis_index("slab")
    c = lax.axis_index("coil")
    x_chip, z_lo = c % X_CHIPS, c // X_CHIPS
    core, y_chip, z_hi = s % 2, (s // 2) % Y_CHIPS, s // (2 * Y_CHIPS)
    z_chip = z_hi * 2 + z_lo

    outward = 2 * core - 1
    offsets = [(r, dx) for r in range(-1, HALO + 1) for dx in (-1, 0, 1) if (r, dx) != (0, 0)]

    def needing(r, dx):
        away = r if r % 2 == 0 else -r
        return ((s - outward * away + Z) % Z, (c + dx + 8) % 8)

    def stage_partner(stage, d):
        if stage == 0:
            return (
                z_hi * 16 + y_chip * 2 + (core + d // 4) % 2,
                z_lo * 4 + (x_chip + d % 4) % 4,
            )
        if stage == 1:
            return (z_hi * 16 + ((y_chip + d) % 8) * 2 + core, c)
        z_new = (z_chip + d) % 8
        return ((z_new // 2) * 16 + y_chip * 2 + core, (z_new % 2) * 4 + x_chip)

    stage_index = (core * 4 + x_chip, y_chip, z_chip)

    partners = [((s + outward * r + Z) % Z, (c + dx + 8) % 8) for r, dx in offsets]
    partners += [(s, (c + d) % 8) for d in range(1, 8)]
    partners += [stage_partner(stage, d) for stage in range(3) for d in range(1, 8)]
    barrier = pltpu.get_barrier_semaphore()
    for partner in partners:
        pl.semaphore_signal(barrier, inc=1, device_id=partner, device_id_type=MESH)

    image_in, lines_in, reg_in, first_in, middle_in, last_in = [
        pltpu.make_async_copy(source, target, local_sem.at[3 + i])
        for i, (source, target) in enumerate(
            (
                (image_hbm, image_ref),
                (lines_hbm, lines_ref),
                (reg_hbm, reg_ref),
                (first_hbm, first_ref),
                (middle_hbm, middle_ref),
                (last_hbm, last_ref),
            )
        )
    ]
    for copy in (image_in, lines_in, first_in, last_in, reg_in):
        copy.start()
    local_copies = [
        pltpu.make_async_copy(maps_hbm.at[:, 0], local_maps, local_sem.at[0]),
        pltpu.make_async_copy(kspace_hbm.at[:, 0], local_kspace, local_sem.at[1]),
        pltpu.make_async_copy(
            maps_hbm.at[:, 0, pl.ds(c * XB, XB)], own_maps.at[pl.ds(c * CL, CL)], local_sem.at[2]
        ),
    ]
    for copy in local_copies:
        copy.start()
    middle_in.start()

    own_image[...] = jnp.zeros_like(own_image)
    image_in.wait()
    for x in range(XB):
        own_image[2 * x : 2 * x + 2, 0:Y] = image_ref[0, x]
    mine = own_image[...]
    tail = jnp.concatenate([mine[:, 256:384], jnp.zeros((8, 128), F32)], axis=1)
    halo[1, 1] = jnp.concatenate([mine[:, 0:256], tail], axis=0).astype(BF16)

    pl.semaphore_wait(barrier, len(partners))

    image_copies = {}
    for i, (r, dx) in enumerate(offsets):
        copy = pltpu.make_async_remote_copy(
            src_ref=halo.at[1, 1],
            dst_ref=halo.at[r + 1, 1 - dx],
            send_sem=img_send.at[i],
            recv_sem=img_recv.at[i],
            device_id=needing(r, dx),
            device_id_type=MESH,
        )
        copy.start()
        image_copies[r, dx] = copy
    lines_in.wait()

    def phase_tables():
        lines = jnp.concatenate([lines_ref[...], jnp.full((1, 128 - NS), -1, jnp.int32)], axis=1)
        position = lax.broadcasted_iota(jnp.int32, (YP, 128), 0)
        line = jnp.broadcast_to(lines, (YP, 128))
        inside = (position < Y) & (line >= 0)
        product = (position * line).astype(F32)
        phase = product - Y * jnp.floor((product + 0.5) * (1.0 / Y))
        half = jnp.abs(jnp.where(phase > Y / 2, phase - Y, phase))
        sine_sign = jnp.where(phase > Y / 2, -1.0, 1.0)
        low_half = half <= Y / 4
        angle = jnp.where(low_half, half, Y / 2 - half) * (2.0 * math.pi / Y)
        square = angle * angle
        cosine = jnp.full((YP, 128), 1.0 / math.factorial(14), F32) * -1.0
        sine = jnp.full((YP, 128), 1.0 / math.factorial(13), F32)
        for order in range(6, -1, -1):
            cosine = cosine * square + (-1.0) ** order / math.factorial(2 * order)
            if order < 6:
                sine = sine * square + (-1.0) ** order / math.factorial(2 * order + 1)
        scale = 1.0 / math.sqrt(Y)
        cosine = jnp.where(inside, jnp.where(low_half, cosine, -cosine) * scale, 0.0)
        sine = jnp.where(inside, sine * angle * sine_sign * scale, 0.0)
        for row, column, value in (
            (0, 0, cosine), (0, 128, -sine), (YP, 0, sine), (YP, 128, cosine),
        ):
            high, low = split(value)
            table_hi[row : row + YP, column : column + 128] = high
            table_lo[row : row + YP, column : column + 128] = low
        pick[...] = jnp.where(inside & (position == line), 1.0, 0.0).astype(BF16)

    phase_tables()

    groups = inter.reshape(3, C, 8, 128)
    tiles = ((0, 128), (1, 128), (2, Y - 256))

    def plane_of(ref, start, count):
        return jnp.concatenate([ref[t, pl.ds(start, count, stride=2), :] for t in range(3)], axis=1)

    def load_planes(source):
        def move(group, carry):
            for x in range(XB):
                value = source(group, x)
                for t, width in tiles:
                    groups[t, group, 2 * x : 2 * x + 2, 0:width] = value[:, 128 * t : 128 * t + width]
            return carry

        lax.fori_loop(0, C, move, 0)
        return plane_of(inter, 0, 4 * C), plane_of(inter, 1, 4 * C)

    for copy in local_copies:
        copy.wait()
    inter[...] = jnp.zeros_like(inter)

    def phase_adjoint():
        kspace_re, kspace_im = load_planes(lambda group, x: local_kspace[group // 8, (group % 8) * XB + x])
        spectrum = []
        for plane in (kspace_re, kspace_im):
            high, low = split(plane)
            spectrum.append(dot(high, pick[...]) + dot(low, pick[...]))
        field = dot3(jnp.concatenate(spectrum, axis=1), table_hi, table_lo, dot_t)
        planes[...] = field
        s_re, s_im = load_planes(lambda group, x: local_maps[group // 8, (group % 8) * XB + x])
        energy = s_re * s_re + s_im * s_im
        energy = jnp.sum(energy.reshape(16, 8, YP), axis=0)
        energy_out[...] = energy[:, 0:128] + energy[:, 128:256] + energy[:, 256:384]
        f_re, f_im = planes[:, 0:YP], planes[:, YP : 2 * YP]
        sum_re = jnp.sum((s_re * f_re + s_im * f_im).reshape(CL, XW, YP), axis=0)
        sum_im = jnp.sum((s_re * f_im - s_im * f_re).reshape(CL, XW, YP), axis=0)
        for k in range(8):
            part_send[k, 0:4] = sum_re[4 * k : 4 * k + 4]
            part_send[k, 4:8] = sum_im[4 * k : 4 * k + 4]
        part_recv[c] = part_send[c]

    phase_adjoint()
    def start_stage(which, stage, value):
        index = stage_index[stage]
        slots[which, stage, index] = value
        copies = []
        for d in range(1, 8):
            copy = pltpu.make_async_remote_copy(
                src_ref=slots.at[which, stage, index],
                dst_ref=slots.at[which, stage, index],
                send_sem=sum_send.at[which, stage, d - 1],
                recv_sem=sum_recv.at[which, stage, d - 1],
                device_id=stage_partner(stage, d),
                device_id_type=MESH,
            )
            copy.start()
            copies.append(copy)
        return copies

    def finish_stage(which, stage, copies):
        for copy in copies:
            copy.wait()
        return jnp.sum(slots[which, stage], axis=0)

    energy_copies = start_stage(0, 0, jnp.sum(energy_out[...], axis=0, keepdims=True))

    def tap_slice(dz):
        return dz * core + (2 - dz) * (1 - core)

    def last_all():
        wl[...] = jnp.zeros_like(wl)
        for k in range(27):
            wl[2 * k : 2 * k + 2, 0:CH] = last_ref[tap_slice(k // 9) * 9 + k % 9].astype(F32)
        return wl[...]

    for copy in (first_in, middle_in, last_in, reg_in):
        copy.wait()

    def phase_weights():
        wt[...] = jnp.zeros_like(wt)
        for dy in range(3):
            for dz in range(3):
                for dx in range(3):
                    row = 2 * (dy * 9 + dz * 3 + dx)
                    wt[row : row + 2, 0:CH] = first_ref[tap_slice(dz) * 9 + dx * 3 + dy].astype(F32)
        w1f[...] = jnp.zeros_like(w1f)
        row8 = lax.broadcasted_iota(jnp.int32, (8, 128), 0)
        for q in range(9):
            low = jnp.where(row8 < 6, wt[6 * q : 6 * q + 8, :], 0.0)
            both = low + lane_roll(pltpu.roll(low, 2, axis=0), CH)
            for x in range(10):
                if x < 9:
                    w1f[24 * q + 2 * x : 24 * q + 2 * x + 8, 128 * x : 128 * x + 128] = both
                else:
                    w1f[24 * q + 18 : 24 * q + 24, 128 * x : 128 * x + 128] = low[0:6]
        w1[...] = w1f[0:256, :].astype(BF16)

        wm[...] = jnp.zeros_like(wm)

        def middle_weights(i, carry):
            layer, dz = i // 3, i % 3
            for dx in range(3):
                taps = [middle_ref[layer * 27 + tap_slice(dz) * 9 + dx * 3 + dy] for dy in range(3)]
                wm[layer, pl.ds(pl.multiple_of(dz * 256 + dx * CH, CH), CH), 0:128] = jnp.concatenate([taps[0], taps[2]], axis=1)
                wm[layer, pl.ds(pl.multiple_of(dz * 256 + dx * CH, CH), CH), 128:256] = jnp.concatenate([taps[1], taps[1]], axis=1)
            return carry

        lax.fori_loop(0, 6, middle_weights, 0)

        w4f[...] = jnp.zeros_like(w4f)
        turned = jnp.transpose(last_all())[0:CH]
        column = lax.broadcasted_iota(jnp.int32, (CH, 128), 1)
        for dz in range(3):
            for dx in range(3):
                merged = None
                for dy in range(3):
                    first_column = 2 * (dz * 9 + dx * 3 + dy)
                    tap = jnp.where((column >= first_column) & (column < first_column + 2), turned, 0.0)
                    tap = lane_roll(tap, 8 * dy - first_column)
                    merged = tap if merged is None else merged + tap
                for x in range(XB):
                    base = dz * 384 + (x + dx) * CH
                    w4f[base : base + CH, :] += merged if x == 0 else lane_roll(merged, 2 * x)
        w4[...] = w4f[...].astype(BF16)

    phase_weights()

    for (r, _), copy in image_copies.items():
        if r <= 1:
            copy.wait()
    energy_copies = start_stage(0, 1, finish_stage(0, 0, energy_copies))
    row24 = lax.broadcasted_iota(jnp.int32, (24, YP), 0) // 8 + (c - 1)

    def feature_slice(zi):
        slice_index = s + outward * (zi - 1)
        valid = (row24 >= 0) & (row24 < 8) & (slice_index >= 0) & (slice_index < Z)
        blocks = [halo[zi, k].astype(F32) for k in range(3)]
        value = jnp.concatenate(
            [jnp.concatenate([block[0:8], block[8:16, 0:128]], axis=1) for block in blocks], axis=0
        )
        value = jnp.where(valid, value, 0.0)
        feats[0, zi] = lane_roll(value, 1)
        feats[1, zi] = value
        feats[2, zi] = lane_roll(value, -1)

    lane = lax.broadcasted_iota(jnp.int32, (1, 256), 1)

    def first_layer(z):
        slice_index = s + outward * z
        slice_valid = (slice_index >= 0) & (slice_index < Z)
        columns = jnp.concatenate(
            [feats[dy, z : z + 3].reshape(72, YP) for dy in range(3)] + [jnp.zeros((40, YP), F32)],
            axis=0,
        )
        tall = jnp.transpose(columns)[0:Y].astype(BF16)
        for x in range(0, 10, 2):
            at = c * XB - 3 + x + lane // CH - lane // 128
            mask = jnp.where((at >= 0) & (at < XW) & slice_valid, 1.0, 0.0)
            product = dot(tall, w1[:, 128 * x : 128 * x + 256])
            product = (jnp.maximum(product, 0.0) * mask).astype(BF16)
            p1[z + 1, x] = product[:, 0:128]
            p1[z + 1, x + 1] = product[:, 128:256]

    low_lanes = lax.broadcasted_iota(jnp.int32, (Y, 128), 1) < CH

    rowi = lax.broadcasted_iota(jnp.int32, (Y, 128), 0)
    edge = jnp.where((low_lanes & (rowi == 0)) | (jnp.logical_not(low_lanes) & (rowi == Y - 1)), 0.0, 1.0)

    def middle_slice(layer, source, target, rows, z, sent=()):
        reach_x = (rows - XB) // 2
        slice_index = s + outward * z
        slice_valid = (slice_index >= 0) & (slice_index < Z)
        before = None
        for x in range(rows):
            operand = jnp.concatenate(
                [source[z + dz, x + 2 * k] for dz in range(3) for k in range(2)], axis=1
            )
            product = dot(operand, wm[layer])
            at = c * XB - reach_x + x
            mask = jnp.where((at >= 0) & (at < XW) & slice_valid, 1.0, 0.0).astype(F32)
            first_half = product[:, 0:128]
            outer = jnp.where(
                low_lanes, pltpu.roll(first_half, 1, axis=0), pltpu.roll(first_half, Y - 1, axis=0)
            )
            outer = outer * edge
            value = outer + lane_roll(outer, CH) + product[:, 128:256]
            value = jnp.maximum(value, 0.0) * mask
            if before is not None:
                target[z + 1, x - 1] = jnp.where(low_lanes, before, value).astype(BF16)
            before = value
            for count, copy in sent:
                if count == x:
                    copy.start()
        target[z + 1, rows - 1] = before.astype(BF16)
        for count, copy in sent:
            if count == rows:
                copy.start()

    def to_other_core(ref, blocks, index):
        return pltpu.make_async_remote_copy(
            src_ref=ref.at[1, blocks],
            dst_ref=ref.at[0, blocks],
            send_sem=core_send.at[index],
            recv_sem=core_recv.at[index],
            device_id=(s + 1 - 2 * core, c),
            device_id_type=MESH,
        )

    first_copy = to_other_core(p1, pl.ds(0, 10), 0)
    middle_copies = [(4, to_other_core(p2, pl.ds(0, 4), 1)), (8, to_other_core(p2, pl.ds(4, 4), 2))]
    hidden_copies = [(x + 1, to_other_core(p3, pl.ds(x, 1), 3 + x // 2)) for x in (0, 2, 4)]

    def phase_firstA():
        for zi in range(3):
            feature_slice(zi)
        first_layer(0)

    phase_firstA()
    first_copy.start()
    map_copies = []
    for d in range(1, 8):
        target = (c + d) % 8
        copy = pltpu.make_async_remote_copy(
            src_ref=maps_hbm.at[:, 0, pl.ds(target * XB, XB)],
            dst_ref=own_maps.at[pl.ds(c * CL, CL)],
            send_sem=map_send.at[d - 1],
            recv_sem=map_recv.at[d - 1],
            device_id=(s, target),
            device_id_type=MESH,
        )
        copy.start()
        map_copies.append(copy)
    rhs_copies = []
    for d in range(1, 8):
        target = (c + d) % 8
        copy = pltpu.make_async_remote_copy(
            src_ref=part_send.at[target],
            dst_ref=part_recv.at[c],
            send_sem=rhs_send.at[d - 1],
            recv_sem=rhs_recv.at[d - 1],
            device_id=(s, target),
            device_id_type=MESH,
        )
        copy.start()
        rhs_copies.append(copy)
    for z in range(1, 4):
        for dx in (-1, 0, 1):
            image_copies[z + 1, dx].wait()
        feature_slice(z + 2)
        first_layer(z)

    def phase_middleA():
        middle_slice(0, p1, p2, 8, 2)

    phase_middleA()
    first_copy.wait()

    def phase_middleB():
        middle_slice(0, p1, p2, 8, 0, middle_copies)

    phase_middleB()
    energy_copies = start_stage(0, 2, finish_stage(0, 1, energy_copies))

    def phase_middleC():
        middle_slice(0, p1, p2, 8, 1)

    phase_middleC()
    for _, copy in middle_copies:
        copy.wait()

    def phase_hiddenA():
        middle_slice(1, p2, p3, 6, 0, hidden_copies)

    phase_hiddenA()

    def phase_hiddenB():
        middle_slice(1, p2, p3, 6, 1)

    phase_hiddenB()

    def write(ref):
        for x in range(XB):
            for t, width in tiles:
                ref[0, x, :, 128 * t : 128 * t + width] = pair[t, 2 * x : 2 * x + 2, 0:width]

    for copy in map_copies:
        copy.wait()

    def phase_maps():
        s_re, s_im = load_planes(lambda group, x: own_maps[group, x])
        maps_re[...] = s_re
        maps_im[...] = s_im

    phase_maps()
    for _, copy in hidden_copies:
        copy.wait()

    def phase_last():
        operand = jnp.concatenate([p3[dz, 2 * k] for dz in range(3) for k in range(3)], axis=1)
        w1f[0:YP, 0:128] = jnp.zeros((YP, 128), F32)
        w1f[0:Y, 0:128] = dot(operand, w4[...])
        turned = jnp.transpose(w1f[0:YP, 0:128])
        residual = lane_roll(turned[0:8], 1) + turned[8:16] + lane_roll(turned[16:24], -1)
        lane8 = lax.broadcasted_iota(jnp.int32, (8, YP), 1)
        denoised = own_image[...] + jnp.where(lane8 < Y, residual, 0.0)
        for t in range(3):
            pair[t, 0:8] = denoised[:, 128 * t : 128 * t + 128]
            pair[t, 8:16] = denoised[:, 128 * t : 128 * t + 128]

        write(denoised_ref)

    phase_last()
    den_re, den_im = plane_of(pair, 0, 8), plane_of(pair, 1, 8)

    reg = reg_ref[0]
    for copy in rhs_copies:
        copy.wait()
    adjoint = jnp.sum(part_recv[...], axis=0)
    other = pltpu.roll(adjoint, 4, axis=0)
    first_rows = lax.broadcasted_iota(jnp.int32, (8, YP), 0) < 4
    right = (
        jnp.where(first_rows, adjoint, other) + reg * den_re,
        jnp.where(first_rows, other, adjoint) + reg * den_im,
    )
    energy = finish_stage(0, 2, energy_copies)

    mean = jnp.sum(energy, axis=1, keepdims=True) * (NS / Y / (Z * XW * Y))

    def spectrum_of(vector):
        v_re = jnp.broadcast_to(vector[0][None], (16, 8, YP)).reshape(128, YP)
        v_im = jnp.broadcast_to(vector[1][None], (16, 8, YP)).reshape(128, YP)
        m_re, m_im = maps_re[...], maps_im[...]
        weighted = jnp.concatenate([m_re * v_re - m_im * v_im, m_re * v_im + m_im * v_re], axis=1)
        return dot3(weighted, table_hi, table_lo, dot)

    def gram_map(vector):
        planes[...] = dot3(spectrum_of(vector), table_hi, table_lo, dot_t)
        m_re, m_im = maps_re[...], maps_im[...]
        f_re, f_im = planes[:, 0:YP], planes[:, YP : 2 * YP]
        real = jnp.sum((m_re * f_re + m_im * f_im).reshape(16, 8, YP), axis=0)
        imag = jnp.sum((m_re * f_im - m_im * f_re).reshape(16, 8, YP), axis=0)
        return real + pltpu.roll(real, 4, axis=0), imag + pltpu.roll(imag, 4, axis=0)

    def folded(first, second):
        product = first[0] * second[0] + first[1] * second[1]
        product = product[:, 0:128] + product[:, 128:256] + product[:, 256:384]
        return 0.5 * jnp.sum(product, axis=0, keepdims=True)

    pairs = [(i, j) for i in range(4) for j in range(i, 4)]
    basis = [right]

    def phase_krylov():
        del basis[1:]
        for _ in range(3):
            mapped = gram_map(basis[-1])
            basis.append((mapped[0] - mean * basis[-1][0], mapped[1] - mean * basis[-1][1]))
        last_spectrum = spectrum_of(basis[-1])
        last_energy = jnp.sum((last_spectrum * last_spectrum).reshape(16, 8, 256), axis=0)
        last_energy = last_energy[:, 0:128] + last_energy[:, 128:256]
        rows = [folded(basis[i], basis[j]) for i, j in pairs]
        rows.append(jnp.sum(last_energy, axis=0, keepdims=True))
        rows.append(jnp.zeros((16 - len(rows), 128), F32))
        packed = jnp.concatenate(rows, axis=0)
        for width in (64, 32, 16, 8):
            packed = packed + lane_roll(packed, width)
        place = lax.broadcasted_iota(jnp.int32, (16, 128), 1) // 8
        owner = lax.broadcasted_iota(jnp.int32, (16, 128), 0)
        return jnp.sum(jnp.where(place == owner, packed, 0.0), axis=0, keepdims=True)

    moments = phase_krylov()
    for stage in range(3):
        moments = finish_stage(1, stage, start_stage(1, stage, moments))
    def phase_solve():
        place = lax.broadcasted_iota(jnp.int32, (1, 128), 1) // 8
        values = [
            jnp.sum(jnp.where(place == i, moments, 0.0), axis=1, keepdims=True) for i in range(len(pairs) + 1)
        ]
        gram = {}
        for row, (i, j) in enumerate(pairs):
            gram[i, j] = gram[j, i] = values[row]
        shift = mean + reg
        matrix = {}
        for i in range(4):
            for j in range(i, 4):
                value = gram[i + 1, j] + shift * gram[i, j] if i < 3 else values[10] + reg * gram[3, 3]
                matrix[i, j] = matrix[j, i] = value
        norm = [jnp.where(matrix[i, i] > 1e-37, lax.rsqrt(jnp.maximum(matrix[i, i], 1e-37)), 0.0) for i in range(4)]
        side = [gram[0, i] * norm[i] for i in range(4)]
        for i in range(4):
            for j in range(i, 4):
                matrix[i, j] = matrix[j, i] = matrix[i, j] * norm[i] * norm[j]
        inverse = []
        for k in range(4):
            pivot = matrix[k, k]
            inverse.append(jnp.where(pivot > 2e-6, 1.0 / jnp.maximum(pivot, 2e-6), 0.0))
            for i in range(k + 1, 4):
                factor = matrix[i, k] * inverse[k]
                for j in range(i, 4):
                    matrix[i, j] = matrix[j, i] = matrix[i, j] - factor * matrix[k, j]
                side[i] = side[i] - factor * side[k]
        weights = [None] * 4
        for k in range(3, -1, -1):
            value = side[k]
            for j in range(k + 1, 4):
                value = value - matrix[k, j] * weights[j]
            weights[k] = value * inverse[k]
        real = sum(weights[k] * norm[k] * basis[k][0] for k in range(4))
        imag = sum(weights[k] * norm[k] * basis[k][1] for k in range(4))
        for t in range(3):
            pair[t, pl.ds(0, 8, stride=2), :] = real[:, 128 * t : 128 * t + 128]
            pair[t, pl.ds(1, 8, stride=2), :] = imag[:, 128 * t : 128 * t + 128]
        write(out_ref)

    phase_solve()


def local(image, sampled_lines, coil_maps, kspace, reg_weight, conv_first, conv_middle, conv_last):
    vmem = pl.BlockSpec(memory_space=pltpu.VMEM)
    anywhere = pl.BlockSpec(memory_space=pltpu.HBM)
    block = pltpu.VMEM((1, XB, 2, Y), F32)
    dma = pltpu.SemaphoreType.DMA
    return pl.pallas_call(
        kernel,
        out_shape=(block, block),
        in_specs=[anywhere] * 8,
        out_specs=(vmem, vmem),
        scratch_shapes=[
            pltpu.VMEM((1, XB, 2, Y), F32),
            pltpu.VMEM((1, NS), jnp.int32),
            pltpu.SMEM((1,), F32),
            pltpu.VMEM((27, 2, CH), BF16),
            pltpu.VMEM((54, CH, CH), BF16),
            pltpu.VMEM((27, 2, CH), BF16),
            pltpu.VMEM((6, 3, 16, 256), BF16),
            pltpu.VMEM((8, YP), F32),
            pltpu.VMEM((3, 6, 24, YP), F32),
            pltpu.VMEM((YP, 1280), F32),
            pltpu.VMEM((256, 1280), BF16),
            pltpu.VMEM((64, 128), F32),
            pltpu.VMEM((128, 128), F32),
            pltpu.VMEM((2, 768, 256), BF16),
            pltpu.VMEM((1152, 128), F32),
            pltpu.VMEM((1152, 128), BF16),
            pltpu.VMEM((5, 10, Y, 128), BF16),
            pltpu.VMEM((4, 8, Y, 128), BF16),
            pltpu.VMEM((3, 6, Y, 128), BF16),
            pltpu.VMEM((2 * YP, 256), BF16),
            pltpu.VMEM((2 * YP, 256), BF16),
            pltpu.VMEM((YP, 128), BF16),
            pltpu.VMEM((CL, XW, 2, Y), F32),
            pltpu.VMEM((CL, XW, 2, Y), F32),
            pltpu.VMEM((C, XB, 2, Y), F32),
            pltpu.VMEM((3, 8 * C, 128), F32),
            pltpu.VMEM((4 * C, 2 * YP), F32),
            pltpu.VMEM((4 * C, YP), F32),
            pltpu.VMEM((4 * C, YP), F32),
            pltpu.VMEM((8, 8, YP), F32),
            pltpu.VMEM((8, 8, YP), F32),
            pltpu.VMEM((3, 16, 128), F32),
            pltpu.VMEM((8, 128), F32),
            pltpu.VMEM((2, 3, 8, 1, 128), F32),
            dma((9,)), dma((17,)), dma((17,)), dma((7,)), dma((7,)), dma((7,)), dma((7,)),
            dma((2, 3, 7)), dma((2, 3, 7)), dma((6,)), dma((6,)),
        ],
        compiler_params=pltpu.CompilerParams(
            collective_id=0, has_side_effects=True, vmem_limit_bytes=LIMIT
        ),
    )(
        image, sampled_lines, coil_maps, kspace, reg_weight,
        conv_first.reshape(27, 2, CH), conv_middle.reshape(54, CH, CH), conv_last.transpose(0, 1, 2, 4, 3).reshape(27, 2, CH),
    )


def solution(mesh):
    in_specs = (
        P("slab", "coil", None, None),
        P("slab", None),
        P("coil", "slab", None, None, None),
        P("coil", "slab", None, None, None),
        P(),
        P(),
        P(),
        P(),
    )
    out_specs = (P("slab", "coil", None, None), P("slab", "coil", None, None))
    return jax.shard_map(local, mesh=mesh, in_specs=in_specs, out_specs=out_specs, check_vma=False)
```

```python
import functools
import math

import jax
import jax.numpy as jnp
from jax import lax
from jax.experimental import pallas as pl
from jax.experimental.pallas import tpu as pltpu
from jax.sharding import PartitionSpec as P

MESH = pl.DeviceIdType.MESH
F32 = jnp.float32
BF16 = jnp.bfloat16

Y = 320
YP = 384
XB = 4
CH = 64
C = 32
CL = 4
NS = 80
HALO = 4
XW = 32
Z = 64
X_CHIPS = 4
Y_CHIPS = 8
Z_CHIPS = 8
LIMIT = 56 * 2**20


def dot(a, b):
    return jnp.dot(a, b, preferred_element_type=F32)


def dot_t(a, b):
    return lax.dot_general(a, b, (((1,), (1,)), ((), ())), preferred_element_type=F32)


def split(v):
    high = v.astype(BF16)
    return high, (v - high.astype(F32)).astype(BF16)


def dot3(v, high_ref, low_ref, op):
    high, low = split(v)
    rows = v.shape[0]
    both = op(jnp.concatenate([high, low], axis=0), high_ref[...])
    return both[0:rows] + both[rows : 2 * rows] + op(high, low_ref[...])


def lane_roll(v, amount):
    return pltpu.roll(v, amount % v.shape[1], axis=1)


def kernel(
    image_hbm, lines_hbm, maps_hbm, kspace_hbm, reg_hbm, first_hbm, middle_hbm, last_hbm,
    denoised_ref, out_ref,
    image_ref, lines_ref, reg_ref, first_ref, middle_ref, last_ref,
    halo, own_image, feats, w1f, w1, wt, wl, wm, w4f, w4, p1, p2, p3,
    table_hi, table_lo, pick, local_maps, local_kspace, own_maps, inter, planes, maps_re, maps_im,
    part_send, part_recv, pair, energy_out, slots,
    local_sem, img_send, img_recv, map_send, map_recv, rhs_send, rhs_recv, sum_send, sum_recv,
    core_send, core_recv,
):
    s = lax.axis_index("slab")
    c = lax.axis_index("coil")
    x_chip, z_lo = c % X_CHIPS, c // X_CHIPS
    core, y_chip, z_hi = s % 2, (s // 2) % Y_CHIPS, s // (2 * Y_CHIPS)
    z_chip = z_hi * 2 + z_lo

    outward = 2 * core - 1
    offsets = [(r, dx) for r in (4, 3, 1, 2, 0, -1) for dx in (-1, 1, 0) if (r, dx) != (0, 0)]

    def needing(r, dx):
        away = r if r % 2 == 0 else -r
        return ((s - outward * away + Z) % Z, (c + dx + 8) % 8)

    def stage_partner(stage, d):
        if stage == 0:
            return (
                z_hi * 16 + y_chip * 2 + (core + d // 4) % 2,
                z_lo * 4 + (x_chip + d % 4) % 4,
            )
        if stage == 1:
            return (z_hi * 16 + ((y_chip + d) % 8) * 2 + core, c)
        z_new = (z_chip + d) % 8
        return ((z_new // 2) * 16 + y_chip * 2 + core, (z_new % 2) * 4 + x_chip)

    stage_index = (core * 4 + x_chip, y_chip, z_chip)

    image_in, lines_in, reg_in, first_in, middle_in, last_in = [
        pltpu.make_async_copy(source, target, local_sem.at[3 + i])
        for i, (source, target) in enumerate(
            (
                (image_hbm, image_ref),
                (lines_hbm, lines_ref),
                (reg_hbm, reg_ref),
                (first_hbm, first_ref),
                (middle_hbm, middle_ref),
                (last_hbm, last_ref),
            )
        )
    ]
    image_in.start()

    partners = [((s + outward * r + Z) % Z, (c + dx + 8) % 8) for r, dx in offsets]
    partners += [(s, (c + d) % 8) for d in range(1, 8)]
    partners += [stage_partner(stage, d) for stage in range(3) for d in range(1, 8)]
    barrier = pltpu.get_barrier_semaphore()
    for partner in partners:
        pl.semaphore_signal(barrier, inc=1, device_id=partner, device_id_type=MESH)

    for copy in (lines_in, first_in, last_in, reg_in):
        copy.start()
    local_copies = [
        pltpu.make_async_copy(maps_hbm.at[:, 0], local_maps, local_sem.at[0]),
        pltpu.make_async_copy(kspace_hbm.at[:, 0], local_kspace, local_sem.at[1]),
        pltpu.make_async_copy(
            maps_hbm.at[:, 0, pl.ds(c * XB, XB)], own_maps.at[pl.ds(c * CL, CL)], local_sem.at[2]
        ),
    ]
    for copy in local_copies:
        copy.start()
    middle_in.start()

    own_image[...] = jnp.zeros_like(own_image)
    image_in.wait()
    for x in range(XB):
        own_image[2 * x : 2 * x + 2, 0:Y] = image_ref[0, x]
    mine = own_image[...]
    tail = jnp.concatenate([mine[:, 256:384], jnp.zeros((8, 128), F32)], axis=1)
    halo[1, 1] = jnp.concatenate([mine[:, 0:256], tail], axis=0).astype(BF16)

    pl.semaphore_wait(barrier, len(partners))

    image_copies = {}
    for i, (r, dx) in enumerate(offsets):
        copy = pltpu.make_async_remote_copy(
            src_ref=halo.at[1, 1],
            dst_ref=halo.at[r + 1, 1 - dx],
            send_sem=img_send.at[i],
            recv_sem=img_recv.at[i],
            device_id=needing(r, dx),
            device_id_type=MESH,
        )
        copy.start()
        image_copies[r, dx] = copy
    lines_in.wait()

    def phase_tables():
        lines = jnp.concatenate([lines_ref[...], jnp.full((1, 128 - NS), -1, jnp.int32)], axis=1)
        position = lax.broadcasted_iota(jnp.int32, (YP, 128), 0)
        line = jnp.broadcast_to(lines, (YP, 128))
        inside = (position < Y) & (line >= 0)
        product = (position * line).astype(F32)
        phase = product - Y * jnp.floor((product + 0.5) * (1.0 / Y))
        half = jnp.abs(jnp.where(phase > Y / 2, phase - Y, phase))
        sine_sign = jnp.where(phase > Y / 2, -1.0, 1.0)
        low_half = half <= Y / 4
        angle = jnp.where(low_half, half, Y / 2 - half) * (2.0 * math.pi / Y)
        square = angle * angle
        cosine = jnp.full((YP, 128), 1.0 / math.factorial(14), F32) * -1.0
        sine = jnp.full((YP, 128), 1.0 / math.factorial(13), F32)
        for order in range(6, -1, -1):
            cosine = cosine * square + (-1.0) ** order / math.factorial(2 * order)
            if order < 6:
                sine = sine * square + (-1.0) ** order / math.factorial(2 * order + 1)
        scale = 1.0 / math.sqrt(Y)
        cosine = jnp.where(inside, jnp.where(low_half, cosine, -cosine) * scale, 0.0)
        sine = jnp.where(inside, sine * angle * sine_sign * scale, 0.0)
        for row, column, value in (
            (0, 0, cosine), (0, 128, -sine), (YP, 0, sine), (YP, 128, cosine),
        ):
            high, low = split(value)
            table_hi[row : row + YP, column : column + 128] = high
            table_lo[row : row + YP, column : column + 128] = low
        pick[...] = jnp.where(inside & (position == line), 1.0, 0.0).astype(BF16)

    phase_tables()

    groups = inter.reshape(3, C, 8, 128)
    tiles = ((0, 128), (1, 128), (2, Y - 256))

    def plane_of(ref, start, count):
        return jnp.concatenate([ref[t, pl.ds(start, count, stride=2), :] for t in range(3)], axis=1)

    def load_planes(source):
        def move(group, carry):
            for x in range(XB):
                value = source(group, x)
                for t, width in tiles:
                    groups[t, group, 2 * x : 2 * x + 2, 0:width] = value[:, 128 * t : 128 * t + width]
            return carry

        lax.fori_loop(0, C, move, 0)
        return plane_of(inter, 0, 4 * C), plane_of(inter, 1, 4 * C)

    for copy in local_copies:
        copy.wait()
    inter[...] = jnp.zeros_like(inter)

    def phase_adjoint():
        kspace_re, kspace_im = load_planes(lambda group, x: local_kspace[group // 8, (group % 8) * XB + x])
        spectrum = []
        for plane in (kspace_re, kspace_im):
            high, low = split(plane)
            spectrum.append(dot(high, pick[...]) + dot(low, pick[...]))
        field = dot3(jnp.concatenate(spectrum, axis=1), table_hi, table_lo, dot_t)
        planes[...] = field
        s_re, s_im = load_planes(lambda group, x: local_maps[group // 8, (group % 8) * XB + x])
        energy = s_re * s_re + s_im * s_im
        energy = jnp.sum(energy.reshape(16, 8, YP), axis=0)
        energy_out[...] = energy[:, 0:128] + energy[:, 128:256] + energy[:, 256:384]
        f_re, f_im = planes[:, 0:YP], planes[:, YP : 2 * YP]
        sum_re = jnp.sum((s_re * f_re + s_im * f_im).reshape(CL, XW, YP), axis=0)
        sum_im = jnp.sum((s_re * f_im - s_im * f_re).reshape(CL, XW, YP), axis=0)
        for k in range(8):
            part_send[k, 0:4] = sum_re[4 * k : 4 * k + 4]
            part_send[k, 4:8] = sum_im[4 * k : 4 * k + 4]
        part_recv[c] = part_send[c]

    phase_adjoint()
    def start_stage(which, stage, value):
        index = stage_index[stage]
        slots[which, stage, index] = value
        copies = []
        for d in range(1, 8):
            copy = pltpu.make_async_remote_copy(
                src_ref=slots.at[which, stage, index],
                dst_ref=slots.at[which, stage, index],
                send_sem=sum_send.at[which, stage, d - 1],
                recv_sem=sum_recv.at[which, stage, d - 1],
                device_id=stage_partner(stage, d),
                device_id_type=MESH,
            )
            copy.start()
            copies.append(copy)
        return copies

    def finish_stage(which, stage, copies):
        for copy in copies:
            copy.wait()
        return jnp.sum(slots[which, stage], axis=0)

    energy_copies = start_stage(0, 0, jnp.sum(energy_out[...], axis=0, keepdims=True))

    def tap_slice(dz):
        return dz * core + (2 - dz) * (1 - core)

    def last_all():
        wl[...] = jnp.zeros_like(wl)
        for k in range(27):
            wl[2 * k : 2 * k + 2, 0:CH] = last_ref[tap_slice(k // 9) * 9 + k % 9].astype(F32)
        return wl[...]

    for copy in (first_in, middle_in, last_in, reg_in):
        copy.wait()

    def phase_weights():
        wt[...] = jnp.zeros_like(wt)
        for dy in range(3):
            for dz in range(3):
                for dx in range(3):
                    row = 2 * (dy * 9 + dz * 3 + dx)
                    wt[row : row + 2, 0:CH] = first_ref[tap_slice(dz) * 9 + dx * 3 + dy].astype(F32)
        w1f[...] = jnp.zeros_like(w1f)
        row8 = lax.broadcasted_iota(jnp.int32, (8, 128), 0)
        for q in range(9):
            low = jnp.where(row8 < 6, wt[6 * q : 6 * q + 8, :], 0.0)
            both = low + lane_roll(pltpu.roll(low, 2, axis=0), CH)
            for x in range(10):
                if x < 9:
                    w1f[24 * q + 2 * x : 24 * q + 2 * x + 8, 128 * x : 128 * x + 128] = both
                else:
                    w1f[24 * q + 18 : 24 * q + 24, 128 * x : 128 * x + 128] = low[0:6]
        w1[...] = w1f[0:256, :].astype(BF16)

        wm[...] = jnp.zeros_like(wm)

        def middle_weights(i, carry):
            layer, dz = i // 3, i % 3
            for dx in range(3):
                taps = [middle_ref[layer * 27 + tap_slice(dz) * 9 + dx * 3 + dy] for dy in range(3)]
                wm[layer, pl.ds(pl.multiple_of(dz * 256 + dx * CH, CH), CH), 0:128] = jnp.concatenate([taps[0], taps[2]], axis=1)
                wm[layer, pl.ds(pl.multiple_of(dz * 256 + dx * CH, CH), CH), 128:256] = jnp.concatenate([taps[1], taps[1]], axis=1)
            return carry

        lax.fori_loop(0, 6, middle_weights, 0)

        w4f[...] = jnp.zeros_like(w4f)
        turned = jnp.transpose(last_all())[0:CH]
        column = lax.broadcasted_iota(jnp.int32, (CH, 128), 1)
        for dz in range(3):
            for dx in range(3):
                merged = None
                for dy in range(3):
                    first_column = 2 * (dz * 9 + dx * 3 + dy)
                    tap = jnp.where((column >= first_column) & (column < first_column + 2), turned, 0.0)
                    tap = lane_roll(tap, 8 * dy - first_column)
                    merged = tap if merged is None else merged + tap
                for x in range(XB):
                    base = dz * 384 + (x + dx) * CH
                    w4f[base : base + CH, :] += merged if x == 0 else lane_roll(merged, 2 * x)
        w4[...] = w4f[...].astype(BF16)

    phase_weights()

    for (r, _), copy in image_copies.items():
        if r <= 1:
            copy.wait()
    energy_copies = start_stage(0, 1, finish_stage(0, 0, energy_copies))
    row24 = lax.broadcasted_iota(jnp.int32, (24, YP), 0) // 8 + (c - 1)

    def feature_slice(zi):
        slice_index = s + outward * (zi - 1)
        valid = (row24 >= 0) & (row24 < 8) & (slice_index >= 0) & (slice_index < Z)
        blocks = [halo[zi, k].astype(F32) for k in range(3)]
        value = jnp.concatenate(
            [jnp.concatenate([block[0:8], block[8:16, 0:128]], axis=1) for block in blocks], axis=0
        )
        value = jnp.where(valid, value, 0.0)
        feats[0, zi] = lane_roll(value, 1)
        feats[1, zi] = value
        feats[2, zi] = lane_roll(value, -1)

    lane = lax.broadcasted_iota(jnp.int32, (1, 256), 1)

    def first_layer(z):
        slice_index = s + outward * z
        slice_valid = (slice_index >= 0) & (slice_index < Z)
        columns = jnp.concatenate(
            [feats[dy, z : z + 3].reshape(72, YP) for dy in range(3)] + [jnp.zeros((40, YP), F32)],
            axis=0,
        )
        tall = jnp.transpose(columns)[0:Y].astype(BF16)
        for x in range(0, 10, 2):
            at = c * XB - 3 + x + lane // CH - lane // 128
            mask = jnp.where((at >= 0) & (at < XW) & slice_valid, 1.0, 0.0)
            product = dot(tall, w1[:, 128 * x : 128 * x + 256])
            product = (jnp.maximum(product, 0.0) * mask).astype(BF16)
            p1[z + 1, x] = product[:, 0:128]
            p1[z + 1, x + 1] = product[:, 128:256]

    low_lanes = lax.broadcasted_iota(jnp.int32, (Y, 128), 1) < CH

    rowi = lax.broadcasted_iota(jnp.int32, (Y, 128), 0)
    edge = jnp.where((low_lanes & (rowi == 0)) | (jnp.logical_not(low_lanes) & (rowi == Y - 1)), 0.0, 1.0)

    def middle_slice(layer, source, target, rows, z, sent=()):
        reach_x = (rows - XB) // 2
        slice_index = s + outward * z
        slice_valid = (slice_index >= 0) & (slice_index < Z)
        before = None
        for x in range(rows):
            operand = jnp.concatenate(
                [source[z + dz, x + 2 * k] for dz in range(3) for k in range(2)], axis=1
            )
            product = dot(operand, wm[layer])
            at = c * XB - reach_x + x
            mask = jnp.where((at >= 0) & (at < XW) & slice_valid, 1.0, 0.0).astype(F32)
            first_half = product[:, 0:128]
            outer = jnp.where(
                low_lanes, pltpu.roll(first_half, 1, axis=0), pltpu.roll(first_half, Y - 1, axis=0)
            )
            outer = outer * edge
            value = outer + lane_roll(outer, CH) + product[:, 128:256]
            value = jnp.maximum(value, 0.0) * mask
            if before is not None:
                target[z + 1, x - 1] = jnp.where(low_lanes, before, value).astype(BF16)
            before = value
            for count, copy in sent:
                if count == x:
                    copy.start()
        target[z + 1, rows - 1] = before.astype(BF16)
        for count, copy in sent:
            if count == rows:
                copy.start()

    def to_other_core(ref, blocks, index):
        return pltpu.make_async_remote_copy(
            src_ref=ref.at[1, blocks],
            dst_ref=ref.at[0, blocks],
            send_sem=core_send.at[index],
            recv_sem=core_recv.at[index],
            device_id=(s + 1 - 2 * core, c),
            device_id_type=MESH,
        )

    first_copy = to_other_core(p1, pl.ds(0, 10), 0)
    middle_copies = [(4, to_other_core(p2, pl.ds(0, 4), 1)), (8, to_other_core(p2, pl.ds(4, 4), 2))]
    hidden_copies = [(x + 1, to_other_core(p3, pl.ds(x, 1), 3 + x // 2)) for x in (0, 2, 4)]

    def phase_firstA():
        for zi in range(3):
            feature_slice(zi)
        first_layer(0)

    phase_firstA()
    first_copy.start()
    map_copies = []
    for d in range(1, 8):
        target = (c + d) % 8
        copy = pltpu.make_async_remote_copy(
            src_ref=maps_hbm.at[:, 0, pl.ds(target * XB, XB)],
            dst_ref=own_maps.at[pl.ds(c * CL, CL)],
            send_sem=map_send.at[d - 1],
            recv_sem=map_recv.at[d - 1],
            device_id=(s, target),
            device_id_type=MESH,
        )
        copy.start()
        map_copies.append(copy)
    rhs_copies = []
    for d in range(1, 8):
        target = (c + d) % 8
        copy = pltpu.make_async_remote_copy(
            src_ref=part_send.at[target],
            dst_ref=part_recv.at[c],
            send_sem=rhs_send.at[d - 1],
            recv_sem=rhs_recv.at[d - 1],
            device_id=(s, target),
            device_id_type=MESH,
        )
        copy.start()
        rhs_copies.append(copy)
    for z in range(1, 4):
        for dx in (-1, 0, 1):
            image_copies[z + 1, dx].wait()
        feature_slice(z + 2)
        first_layer(z)

    def phase_middleA():
        middle_slice(0, p1, p2, 8, 2)

    phase_middleA()
    first_copy.wait()

    def phase_middleB():
        middle_slice(0, p1, p2, 8, 0, middle_copies)

    phase_middleB()
    energy_copies = start_stage(0, 2, finish_stage(0, 1, energy_copies))

    def phase_middleC():
        middle_slice(0, p1, p2, 8, 1)

    phase_middleC()
    for _, copy in middle_copies:
        copy.wait()

    def phase_hiddenA():
        middle_slice(1, p2, p3, 6, 0, hidden_copies)

    phase_hiddenA()

    def phase_hiddenB():
        middle_slice(1, p2, p3, 6, 1)

    phase_hiddenB()

    def write(ref):
        for x in range(XB):
            for t, width in tiles:
                ref[0, x, :, 128 * t : 128 * t + width] = pair[t, 2 * x : 2 * x + 2, 0:width]

    for copy in map_copies:
        copy.wait()

    def phase_maps():
        s_re, s_im = load_planes(lambda group, x: own_maps[group, x])
        maps_re[...] = s_re
        maps_im[...] = s_im

    phase_maps()
    for _, copy in hidden_copies:
        copy.wait()

    def phase_last():
        operand = jnp.concatenate([p3[dz, 2 * k] for dz in range(3) for k in range(3)], axis=1)
        w1f[0:YP, 0:128] = jnp.zeros((YP, 128), F32)
        w1f[0:Y, 0:128] = dot(operand, w4[...])
        turned = jnp.transpose(w1f[0:YP, 0:128])
        residual = lane_roll(turned[0:8], 1) + turned[8:16] + lane_roll(turned[16:24], -1)
        lane8 = lax.broadcasted_iota(jnp.int32, (8, YP), 1)
        denoised = own_image[...] + jnp.where(lane8 < Y, residual, 0.0)
        for t in range(3):
            pair[t, 0:8] = denoised[:, 128 * t : 128 * t + 128]
            pair[t, 8:16] = denoised[:, 128 * t : 128 * t + 128]

        write(denoised_ref)

    phase_last()
    den_re, den_im = plane_of(pair, 0, 8), plane_of(pair, 1, 8)

    reg = reg_ref[0]
    for copy in rhs_copies:
        copy.wait()
    adjoint = jnp.sum(part_recv[...], axis=0)
    other = pltpu.roll(adjoint, 4, axis=0)
    first_rows = lax.broadcasted_iota(jnp.int32, (8, YP), 0) < 4
    right = (
        jnp.where(first_rows, adjoint, other) + reg * den_re,
        jnp.where(first_rows, other, adjoint) + reg * den_im,
    )
    energy = finish_stage(0, 2, energy_copies)

    mean = jnp.sum(energy, axis=1, keepdims=True) * (NS / Y / (Z * XW * Y))

    def spectrum_of(vector):
        v_re = jnp.broadcast_to(vector[0][None], (16, 8, YP)).reshape(128, YP)
        v_im = jnp.broadcast_to(vector[1][None], (16, 8, YP)).reshape(128, YP)
        m_re, m_im = maps_re[...], maps_im[...]
        weighted = jnp.concatenate([m_re * v_re - m_im * v_im, m_re * v_im + m_im * v_re], axis=1)
        return dot3(weighted, table_hi, table_lo, dot)

    def gram_map(vector):
        planes[...] = dot3(spectrum_of(vector), table_hi, table_lo, dot_t)
        m_re, m_im = maps_re[...], maps_im[...]
        f_re, f_im = planes[:, 0:YP], planes[:, YP : 2 * YP]
        real = jnp.sum((m_re * f_re + m_im * f_im).reshape(16, 8, YP), axis=0)
        imag = jnp.sum((m_re * f_im - m_im * f_re).reshape(16, 8, YP), axis=0)
        return real + pltpu.roll(real, 4, axis=0), imag + pltpu.roll(imag, 4, axis=0)

    def folded(first, second):
        product = first[0] * second[0] + first[1] * second[1]
        product = product[:, 0:128] + product[:, 128:256] + product[:, 256:384]
        return 0.5 * jnp.sum(product, axis=0, keepdims=True)

    pairs = [(i, j) for i in range(4) for j in range(i, 4)]
    basis = [right]

    def phase_krylov():
        del basis[1:]
        for _ in range(3):
            mapped = gram_map(basis[-1])
            basis.append((mapped[0] - mean * basis[-1][0], mapped[1] - mean * basis[-1][1]))
        last_spectrum = spectrum_of(basis[-1])
        last_energy = jnp.sum((last_spectrum * last_spectrum).reshape(16, 8, 256), axis=0)
        last_energy = last_energy[:, 0:128] + last_energy[:, 128:256]
        rows = [folded(basis[i], basis[j]) for i, j in pairs]
        rows.append(jnp.sum(last_energy, axis=0, keepdims=True))
        rows.append(jnp.zeros((16 - len(rows), 128), F32))
        packed = jnp.concatenate(rows, axis=0)
        for width in (64, 32, 16, 8):
            packed = packed + lane_roll(packed, width)
        place = lax.broadcasted_iota(jnp.int32, (16, 128), 1) // 8
        owner = lax.broadcasted_iota(jnp.int32, (16, 128), 0)
        return jnp.sum(jnp.where(place == owner, packed, 0.0), axis=0, keepdims=True)

    moments = phase_krylov()
    for stage in range(3):
        moments = finish_stage(1, stage, start_stage(1, stage, moments))
    def phase_solve():
        place = lax.broadcasted_iota(jnp.int32, (1, 128), 1) // 8
        values = [
            jnp.sum(jnp.where(place == i, moments, 0.0), axis=1, keepdims=True) for i in range(len(pairs) + 1)
        ]
        gram = {}
        for row, (i, j) in enumerate(pairs):
            gram[i, j] = gram[j, i] = values[row]
        shift = mean + reg
        matrix = {}
        for i in range(4):
            for j in range(i, 4):
                value = gram[i + 1, j] + shift * gram[i, j] if i < 3 else values[10] + reg * gram[3, 3]
                matrix[i, j] = matrix[j, i] = value
        norm = [jnp.where(matrix[i, i] > 1e-37, lax.rsqrt(jnp.maximum(matrix[i, i], 1e-37)), 0.0) for i in range(4)]
        side = [gram[0, i] * norm[i] for i in range(4)]
        for i in range(4):
            for j in range(i, 4):
                matrix[i, j] = matrix[j, i] = matrix[i, j] * norm[i] * norm[j]
        inverse = []
        for k in range(4):
            pivot = matrix[k, k]
            inverse.append(jnp.where(pivot > 2e-6, 1.0 / jnp.maximum(pivot, 2e-6), 0.0))
            for i in range(k + 1, 4):
                factor = matrix[i, k] * inverse[k]
                for j in range(i, 4):
                    matrix[i, j] = matrix[j, i] = matrix[i, j] - factor * matrix[k, j]
                side[i] = side[i] - factor * side[k]
        weights = [None] * 4
        for k in range(3, -1, -1):
            value = side[k]
            for j in range(k + 1, 4):
                value = value - matrix[k, j] * weights[j]
            weights[k] = value * inverse[k]
        real = sum(weights[k] * norm[k] * basis[k][0] for k in range(4))
        imag = sum(weights[k] * norm[k] * basis[k][1] for k in range(4))
        for t in range(3):
            pair[t, pl.ds(0, 8, stride=2), :] = real[:, 128 * t : 128 * t + 128]
            pair[t, pl.ds(1, 8, stride=2), :] = imag[:, 128 * t : 128 * t + 128]
        write(out_ref)

    phase_solve()


def write_out(first, second, first_out, second_out, sems):
    copies = [
        pltpu.make_async_copy(first, first_out, sems.at[0]),
        pltpu.make_async_copy(second, second_out, sems.at[1]),
    ]
    for copy in copies:
        copy.start()
    for copy in copies:
        copy.wait()


def local(image, sampled_lines, coil_maps, kspace, reg_weight, conv_first, conv_middle, conv_last):
    vmem = pl.BlockSpec(memory_space=pltpu.VMEM)
    anywhere = pl.BlockSpec(memory_space=pltpu.HBM)
    block = pltpu.VMEM((1, XB, 2, Y), F32)
    dma = pltpu.SemaphoreType.DMA
    results = pl.pallas_call(
        kernel,
        out_shape=(block, block),
        in_specs=[anywhere] * 8,
        out_specs=(vmem, vmem),
        scratch_shapes=[
            pltpu.VMEM((1, XB, 2, Y), F32),
            pltpu.VMEM((1, NS), jnp.int32),
            pltpu.SMEM((1,), F32),
            pltpu.VMEM((27, 2, CH), BF16),
            pltpu.VMEM((54, CH, CH), BF16),
            pltpu.VMEM((27, 2, CH), BF16),
            pltpu.VMEM((6, 3, 16, 256), BF16),
            pltpu.VMEM((8, YP), F32),
            pltpu.VMEM((3, 6, 24, YP), F32),
            pltpu.VMEM((YP, 1280), F32),
            pltpu.VMEM((256, 1280), BF16),
            pltpu.VMEM((64, 128), F32),
            pltpu.VMEM((128, 128), F32),
            pltpu.VMEM((2, 768, 256), BF16),
            pltpu.VMEM((1152, 128), F32),
            pltpu.VMEM((1152, 128), BF16),
            pltpu.VMEM((5, 10, Y, 128), BF16),
            pltpu.VMEM((4, 8, Y, 128), BF16),
            pltpu.VMEM((3, 6, Y, 128), BF16),
            pltpu.VMEM((2 * YP, 256), BF16),
            pltpu.VMEM((2 * YP, 256), BF16),
            pltpu.VMEM((YP, 128), BF16),
            pltpu.VMEM((CL, XW, 2, Y), F32),
            pltpu.VMEM((CL, XW, 2, Y), F32),
            pltpu.VMEM((C, XB, 2, Y), F32),
            pltpu.VMEM((3, 8 * C, 128), F32),
            pltpu.VMEM((4 * C, 2 * YP), F32),
            pltpu.VMEM((4 * C, YP), F32),
            pltpu.VMEM((4 * C, YP), F32),
            pltpu.VMEM((8, 8, YP), F32),
            pltpu.VMEM((8, 8, YP), F32),
            pltpu.VMEM((3, 16, 128), F32),
            pltpu.VMEM((8, 128), F32),
            pltpu.VMEM((2, 3, 8, 1, 128), F32),
            dma((9,)), dma((17,)), dma((17,)), dma((7,)), dma((7,)), dma((7,)), dma((7,)),
            dma((2, 3, 7)), dma((2, 3, 7)), dma((6,)), dma((6,)),
        ],
        compiler_params=pltpu.CompilerParams(
            collective_id=0, has_side_effects=True, vmem_limit_bytes=LIMIT
        ),
    )(
        image, sampled_lines, coil_maps, kspace, reg_weight,
        conv_first.reshape(27, 2, CH), conv_middle.reshape(54, CH, CH), conv_last.transpose(0, 1, 2, 4, 3).reshape(27, 2, CH),
    )
    hbm = pl.BlockSpec(memory_space=pltpu.HBM)
    return pl.pallas_call(
        write_out,
        out_shape=(jax.ShapeDtypeStruct((1, XB, 2, Y), F32),) * 2,
        in_specs=[vmem, vmem],
        out_specs=(hbm, hbm),
        scratch_shapes=[dma((2,))],
    )(*results)


def solution(mesh):
    in_specs = (
        P("slab", "coil", None, None),
        P("slab", None),
        P("coil", "slab", None, None, None),
        P("coil", "slab", None, None, None),
        P(),
        P(),
        P(),
        P(),
    )
    out_specs = (P("slab", "coil", None, None), P("slab", "coil", None, None))
    return jax.shard_map(local, mesh=mesh, in_specs=in_specs, out_specs=out_specs, check_vma=False)
```

```python
import functools
import math

import jax
import jax.numpy as jnp
from jax import lax
from jax.experimental import pallas as pl
from jax.experimental.pallas import tpu as pltpu
from jax.sharding import PartitionSpec as P

MESH = pl.DeviceIdType.MESH
F32 = jnp.float32
BF16 = jnp.bfloat16

Y = 320
YP = 384
XB = 4
CH = 64
C = 32
CL = 4
NS = 80
HALO = 4
XW = 32
Z = 64
X_CHIPS = 4
Y_CHIPS = 8
Z_CHIPS = 8
LIMIT = 56 * 2**20


def dot(a, b):
    return jnp.dot(a, b, preferred_element_type=F32)


def dot_t(a, b):
    return lax.dot_general(a, b, (((1,), (1,)), ((), ())), preferred_element_type=F32)


def split(v):
    high = v.astype(BF16)
    return high, (v - high.astype(F32)).astype(BF16)


def dot3(v, high_ref, low_ref, op):
    high, low = split(v)
    rows = v.shape[0]
    both = op(jnp.concatenate([high, low], axis=0), high_ref[...])
    return both[0:rows] + both[rows : 2 * rows] + op(high, low_ref[...])


def lane_roll(v, amount):
    return pltpu.roll(v, amount % v.shape[1], axis=1)


def kernel(
    image_hbm, lines_hbm, maps_hbm, kspace_hbm, reg_hbm, first_hbm, middle_hbm, last_hbm,
    denoised_ref, out_ref,
    image_ref, lines_ref, reg_ref, first_ref, middle_ref, last_ref,
    halo, own_image, feats, w1f, w1, wt, wl, wm, w4f, w4, p1, p2, p3,
    table_hi, table_lo, back_hi, back_lo, pick, local_maps, local_kspace, own_maps, inter, planes, maps_re, maps_im,
    part_send, part_recv, pair, energy_out, slots,
    local_sem, img_send, img_recv, map_send, map_recv, rhs_send, rhs_recv, sum_send, sum_recv,
    core_send, core_recv,
):
    s = lax.axis_index("slab")
    c = lax.axis_index("coil")
    x_chip, z_lo = c % X_CHIPS, c // X_CHIPS
    core, y_chip, z_hi = s % 2, (s // 2) % Y_CHIPS, s // (2 * Y_CHIPS)
    z_chip = z_hi * 2 + z_lo

    outward = 2 * core - 1
    offsets = [(r, dx) for r in (4, 3, 1, 2, 0, -1) for dx in (-1, 1, 0) if (r, dx) != (0, 0)]

    def needing(r, dx):
        away = r if r % 2 == 0 else -r
        return ((s - outward * away + Z) % Z, (c + dx + 8) % 8)

    def stage_partner(stage, d):
        if stage == 0:
            return (
                z_hi * 16 + y_chip * 2 + (core + d // 4) % 2,
                z_lo * 4 + (x_chip + d % 4) % 4,
            )
        if stage == 1:
            return (z_hi * 16 + ((y_chip + d) % 8) * 2 + core, c)
        z_new = (z_chip + d) % 8
        return ((z_new // 2) * 16 + y_chip * 2 + core, (z_new % 2) * 4 + x_chip)

    stage_index = (core * 4 + x_chip, y_chip, z_chip)

    image_in, lines_in, reg_in, first_in, middle_in, last_in = [
        pltpu.make_async_copy(source, target, local_sem.at[3 + i])
        for i, (source, target) in enumerate(
            (
                (image_hbm, image_ref),
                (lines_hbm, lines_ref),
                (reg_hbm, reg_ref),
                (first_hbm, first_ref),
                (middle_hbm, middle_ref),
                (last_hbm, last_ref),
            )
        )
    ]
    image_in.start()

    partners = [((s + outward * r + Z) % Z, (c + dx + 8) % 8) for r, dx in offsets]
    partners += [(s, (c + d) % 8) for d in range(1, 8)]
    partners += [stage_partner(stage, d) for stage in range(3) for d in range(1, 8)]
    barrier = pltpu.get_barrier_semaphore()
    for partner in partners:
        pl.semaphore_signal(barrier, inc=1, device_id=partner, device_id_type=MESH)

    for copy in (lines_in, first_in, last_in, reg_in):
        copy.start()
    local_copies = [
        pltpu.make_async_copy(maps_hbm.at[:, 0], local_maps, local_sem.at[0]),
        pltpu.make_async_copy(kspace_hbm.at[:, 0], local_kspace, local_sem.at[1]),
        pltpu.make_async_copy(
            maps_hbm.at[:, 0, pl.ds(c * XB, XB)], own_maps.at[pl.ds(c * CL, CL)], local_sem.at[2]
        ),
    ]
    for copy in local_copies:
        copy.start()
    middle_in.start()

    own_image[...] = jnp.zeros_like(own_image)
    image_in.wait()
    for x in range(XB):
        own_image[2 * x : 2 * x + 2, 0:Y] = image_ref[0, x]
    mine = own_image[...]
    tail = jnp.concatenate([mine[:, 256:384], jnp.zeros((8, 128), F32)], axis=1)
    halo[1, 1] = jnp.concatenate([mine[:, 0:256], tail], axis=0).astype(BF16)

    pl.semaphore_wait(barrier, len(partners))

    image_copies = {}
    for i, (r, dx) in enumerate(offsets):
        copy = pltpu.make_async_remote_copy(
            src_ref=halo.at[1, 1],
            dst_ref=halo.at[r + 1, 1 - dx],
            send_sem=img_send.at[i],
            recv_sem=img_recv.at[i],
            device_id=needing(r, dx),
            device_id_type=MESH,
        )
        copy.start()
        image_copies[r, dx] = copy
    lines_in.wait()

    def phase_tables():
        lines = jnp.concatenate([lines_ref[...], jnp.full((1, 128 - NS), -1, jnp.int32)], axis=1)
        position = lax.broadcasted_iota(jnp.int32, (YP, 128), 0)
        line = jnp.broadcast_to(lines, (YP, 128))
        inside = (position < Y) & (line >= 0)
        product = (position * line).astype(F32)
        phase = product - Y * jnp.floor((product + 0.5) * (1.0 / Y))
        half = jnp.abs(jnp.where(phase > Y / 2, phase - Y, phase))
        sine_sign = jnp.where(phase > Y / 2, -1.0, 1.0)
        low_half = half <= Y / 4
        angle = jnp.where(low_half, half, Y / 2 - half) * (2.0 * math.pi / Y)
        square = angle * angle
        cosine = jnp.full((YP, 128), 1.0 / math.factorial(14), F32) * -1.0
        sine = jnp.full((YP, 128), 1.0 / math.factorial(13), F32)
        for order in range(6, -1, -1):
            cosine = cosine * square + (-1.0) ** order / math.factorial(2 * order)
            if order < 6:
                sine = sine * square + (-1.0) ** order / math.factorial(2 * order + 1)
        scale = 1.0 / math.sqrt(Y)
        cosine = jnp.where(inside, jnp.where(low_half, cosine, -cosine) * scale, 0.0)
        sine = jnp.where(inside, sine * angle * sine_sign * scale, 0.0)
        for row, column, value in (
            (0, 0, cosine), (0, 128, -sine), (YP, 0, sine), (YP, 128, cosine),
        ):
            high, low = split(value)
            table_hi[row : row + YP, column : column + 128] = high
            table_lo[row : row + YP, column : column + 128] = low
        for row, column, value in (
            (0, 0, cosine), (128, 0, -sine), (0, YP, sine), (128, YP, cosine),
        ):
            high, low = split(jnp.transpose(value))
            back_hi[row : row + 128, column : column + YP] = high
            back_lo[row : row + 128, column : column + YP] = low
        pick[...] = jnp.where(inside & (position == line), 1.0, 0.0).astype(BF16)

    phase_tables()

    groups = inter.reshape(3, C, 8, 128)
    tiles = ((0, 128), (1, 128), (2, Y - 256))

    def plane_of(ref, start, count):
        return jnp.concatenate([ref[t, pl.ds(start, count, stride=2), :] for t in range(3)], axis=1)

    def load_planes(source):
        def move(group, carry):
            for x in range(XB):
                value = source(group, x)
                for t, width in tiles:
                    groups[t, group, 2 * x : 2 * x + 2, 0:width] = value[:, 128 * t : 128 * t + width]
            return carry

        lax.fori_loop(0, C, move, 0)
        return plane_of(inter, 0, 4 * C), plane_of(inter, 1, 4 * C)

    for copy in local_copies:
        copy.wait()
    inter[...] = jnp.zeros_like(inter)

    def phase_adjoint():
        kspace_re, kspace_im = load_planes(lambda group, x: local_kspace[group // 8, (group % 8) * XB + x])
        spectrum = []
        for plane in (kspace_re, kspace_im):
            high, low = split(plane)
            spectrum.append(dot(high, pick[...]) + dot(low, pick[...]))
        field = dot3(jnp.concatenate(spectrum, axis=1), back_hi, back_lo, dot)
        planes[...] = field
        s_re, s_im = load_planes(lambda group, x: local_maps[group // 8, (group % 8) * XB + x])
        energy = s_re * s_re + s_im * s_im
        energy = jnp.sum(energy.reshape(16, 8, YP), axis=0)
        energy_out[...] = energy[:, 0:128] + energy[:, 128:256] + energy[:, 256:384]
        f_re, f_im = planes[:, 0:YP], planes[:, YP : 2 * YP]
        sum_re = jnp.sum((s_re * f_re + s_im * f_im).reshape(CL, XW, YP), axis=0)
        sum_im = jnp.sum((s_re * f_im - s_im * f_re).reshape(CL, XW, YP), axis=0)
        for k in range(8):
            part_send[k, 0:4] = sum_re[4 * k : 4 * k + 4]
            part_send[k, 4:8] = sum_im[4 * k : 4 * k + 4]
        part_recv[c] = part_send[c]

    phase_adjoint()
    def start_stage(which, stage, value):
        index = stage_index[stage]
        slots[which, stage, index] = value
        copies = []
        for d in range(1, 8):
            copy = pltpu.make_async_remote_copy(
                src_ref=slots.at[which, stage, index],
                dst_ref=slots.at[which, stage, index],
                send_sem=sum_send.at[which, stage, d - 1],
                recv_sem=sum_recv.at[which, stage, d - 1],
                device_id=stage_partner(stage, d),
                device_id_type=MESH,
            )
            copy.start()
            copies.append(copy)
        return copies

    def finish_stage(which, stage, copies):
        for copy in copies:
            copy.wait()
        return jnp.sum(slots[which, stage], axis=0)

    energy_copies = start_stage(0, 0, jnp.sum(energy_out[...], axis=0, keepdims=True))

    def tap_slice(dz):
        return dz * core + (2 - dz) * (1 - core)

    def last_all():
        wl[...] = jnp.zeros_like(wl)
        for k in range(27):
            wl[2 * k : 2 * k + 2, 0:CH] = last_ref[tap_slice(k // 9) * 9 + k % 9].astype(F32)
        return wl[...]

    for copy in (first_in, middle_in, last_in, reg_in):
        copy.wait()

    def phase_weights():
        wt[...] = jnp.zeros_like(wt)
        for dy in range(3):
            for dz in range(3):
                for dx in range(3):
                    row = 2 * (dy * 9 + dz * 3 + dx)
                    wt[row : row + 2, 0:CH] = first_ref[tap_slice(dz) * 9 + dx * 3 + dy].astype(F32)
        w1f[...] = jnp.zeros_like(w1f)
        row8 = lax.broadcasted_iota(jnp.int32, (8, 128), 0)
        for q in range(9):
            low = jnp.where(row8 < 6, wt[6 * q : 6 * q + 8, :], 0.0)
            both = low + lane_roll(pltpu.roll(low, 2, axis=0), CH)
            for x in range(10):
                if x < 9:
                    w1f[24 * q + 2 * x : 24 * q + 2 * x + 8, 128 * x : 128 * x + 128] = both
                else:
                    w1f[24 * q + 18 : 24 * q + 24, 128 * x : 128 * x + 128] = low[0:6]
        w1[...] = w1f[0:256, :].astype(BF16)

        wm[...] = jnp.zeros_like(wm)

        def middle_weights(i, carry):
            layer, dz = i // 3, i % 3
            for dx in range(3):
                taps = [middle_ref[layer * 27 + tap_slice(dz) * 9 + dx * 3 + dy] for dy in range(3)]
                wm[layer, pl.ds(pl.multiple_of(dz * 256 + dx * CH, CH), CH), 0:128] = jnp.concatenate([taps[0], taps[2]], axis=1)
                wm[layer, pl.ds(pl.multiple_of(dz * 256 + dx * CH, CH), CH), 128:256] = jnp.concatenate([taps[1], taps[1]], axis=1)
            return carry

        lax.fori_loop(0, 6, middle_weights, 0)

        w4f[...] = jnp.zeros_like(w4f)
        turned = jnp.transpose(last_all())[0:CH]
        column = lax.broadcasted_iota(jnp.int32, (CH, 128), 1)
        for dz in range(3):
            for dx in range(3):
                merged = None
                for dy in range(3):
                    first_column = 2 * (dz * 9 + dx * 3 + dy)
                    tap = jnp.where((column >= first_column) & (column < first_column + 2), turned, 0.0)
                    tap = lane_roll(tap, 8 * dy - first_column)
                    merged = tap if merged is None else merged + tap
                for x in range(XB):
                    base = dz * 384 + (x + dx) * CH
                    w4f[base : base + CH, :] += merged if x == 0 else lane_roll(merged, 2 * x)
        w4[...] = w4f[...].astype(BF16)

    phase_weights()
    rhs_copies = []
    for d in range(1, 8):
        target = (c + d) % 8
        copy = pltpu.make_async_remote_copy(
            src_ref=part_send.at[target],
            dst_ref=part_recv.at[c],
            send_sem=rhs_send.at[d - 1],
            recv_sem=rhs_recv.at[d - 1],
            device_id=(s, target),
            device_id_type=MESH,
        )
        copy.start()
        rhs_copies.append(copy)
    energy_copies = start_stage(0, 1, finish_stage(0, 0, energy_copies))

    for (r, _), copy in image_copies.items():
        if r <= 1:
            copy.wait()
    map_copies = []
    for d in range(1, 8):
        target = (c + d) % 8
        copy = pltpu.make_async_remote_copy(
            src_ref=maps_hbm.at[:, 0, pl.ds(target * XB, XB)],
            dst_ref=own_maps.at[pl.ds(c * CL, CL)],
            send_sem=map_send.at[d - 1],
            recv_sem=map_recv.at[d - 1],
            device_id=(s, target),
            device_id_type=MESH,
        )
        copy.start()
        map_copies.append(copy)
    row24 = lax.broadcasted_iota(jnp.int32, (24, YP), 0) // 8 + (c - 1)

    def feature_slice(zi):
        slice_index = s + outward * (zi - 1)
        valid = (row24 >= 0) & (row24 < 8) & (slice_index >= 0) & (slice_index < Z)
        blocks = [halo[zi, k].astype(F32) for k in range(3)]
        value = jnp.concatenate(
            [jnp.concatenate([block[0:8], block[8:16, 0:128]], axis=1) for block in blocks], axis=0
        )
        value = jnp.where(valid, value, 0.0)
        feats[0, zi] = lane_roll(value, 1)
        feats[1, zi] = value
        feats[2, zi] = lane_roll(value, -1)

    lane = lax.broadcasted_iota(jnp.int32, (1, 256), 1)

    def first_layer(z):
        slice_index = s + outward * z
        slice_valid = (slice_index >= 0) & (slice_index < Z)
        columns = jnp.concatenate(
            [feats[dy, z : z + 3].reshape(72, YP) for dy in range(3)] + [jnp.zeros((40, YP), F32)],
            axis=0,
        )
        tall = jnp.transpose(columns)[0:Y].astype(BF16)
        for x in range(0, 10, 2):
            at = c * XB - 3 + x + lane // CH - lane // 128
            mask = jnp.where((at >= 0) & (at < XW) & slice_valid, 1.0, 0.0)
            product = dot(tall, w1[:, 128 * x : 128 * x + 256])
            product = (jnp.maximum(product, 0.0) * mask).astype(BF16)
            p1[z + 1, x] = product[:, 0:128]
            p1[z + 1, x + 1] = product[:, 128:256]

    low_lanes = lax.broadcasted_iota(jnp.int32, (Y, 128), 1) < CH

    rowi = lax.broadcasted_iota(jnp.int32, (Y, 128), 0)
    edge = jnp.where((low_lanes & (rowi == 0)) | (jnp.logical_not(low_lanes) & (rowi == Y - 1)), 0.0, 1.0)

    def middle_slice(layer, source, target, rows, z, sent=()):
        reach_x = (rows - XB) // 2
        slice_index = s + outward * z
        slice_valid = (slice_index >= 0) & (slice_index < Z)
        before = None
        for x in range(rows):
            operand = jnp.concatenate(
                [source[z + dz, x + 2 * k] for dz in range(3) for k in range(2)], axis=1
            )
            product = dot(operand, wm[layer])
            at = c * XB - reach_x + x
            mask = jnp.where((at >= 0) & (at < XW) & slice_valid, 1.0, 0.0).astype(F32)
            first_half = product[:, 0:128]
            outer = jnp.where(
                low_lanes, pltpu.roll(first_half, 1, axis=0), pltpu.roll(first_half, Y - 1, axis=0)
            )
            outer = outer * edge
            value = outer + lane_roll(outer, CH) + product[:, 128:256]
            value = jnp.maximum(value, 0.0) * mask
            if before is not None:
                target[z + 1, x - 1] = jnp.where(low_lanes, before, value).astype(BF16)
            before = value
            for count, copy in sent:
                if count == x:
                    copy.start()
        target[z + 1, rows - 1] = before.astype(BF16)
        for count, copy in sent:
            if count == rows:
                copy.start()

    def to_other_core(ref, blocks, index):
        return pltpu.make_async_remote_copy(
            src_ref=ref.at[1, blocks],
            dst_ref=ref.at[0, blocks],
            send_sem=core_send.at[index],
            recv_sem=core_recv.at[index],
            device_id=(s + 1 - 2 * core, c),
            device_id_type=MESH,
        )

    first_copy = to_other_core(p1, pl.ds(0, 10), 0)
    middle_copies = [(4, to_other_core(p2, pl.ds(0, 4), 1)), (8, to_other_core(p2, pl.ds(4, 4), 2))]
    hidden_copies = [(x + 1, to_other_core(p3, pl.ds(x, 1), 3 + x // 2)) for x in (0, 2, 4)]

    def phase_firstA():
        for zi in range(3):
            feature_slice(zi)
        first_layer(0)

    phase_firstA()
    first_copy.start()
    for z in range(1, 4):
        for dx in (-1, 0, 1):
            image_copies[z + 1, dx].wait()
        feature_slice(z + 2)
        first_layer(z)
    energy_copies = start_stage(0, 2, finish_stage(0, 1, energy_copies))

    def phase_middleA():
        middle_slice(0, p1, p2, 8, 2)

    phase_middleA()
    first_copy.wait()

    def phase_middleB():
        middle_slice(0, p1, p2, 8, 0, middle_copies)

    phase_middleB()

    def phase_middleC():
        middle_slice(0, p1, p2, 8, 1)

    phase_middleC()
    for _, copy in middle_copies:
        copy.wait()

    def phase_hiddenA():
        middle_slice(1, p2, p3, 6, 0, hidden_copies)

    phase_hiddenA()

    def phase_hiddenB():
        middle_slice(1, p2, p3, 6, 1)

    phase_hiddenB()

    def write(ref):
        for x in range(XB):
            for t, width in tiles:
                ref[0, x, :, 128 * t : 128 * t + width] = pair[t, 2 * x : 2 * x + 2, 0:width]

    for copy in map_copies:
        copy.wait()

    def phase_maps():
        s_re, s_im = load_planes(lambda group, x: own_maps[group, x])
        maps_re[...] = s_re
        maps_im[...] = s_im

    phase_maps()
    for _, copy in hidden_copies:
        copy.wait()

    def phase_last():
        operand = jnp.concatenate([p3[dz, 2 * k] for dz in range(3) for k in range(3)], axis=1)
        w1f[0:YP, 0:128] = jnp.zeros((YP, 128), F32)
        w1f[0:Y, 0:128] = dot(operand, w4[...])
        turned = jnp.transpose(w1f[0:YP, 0:128])
        residual = lane_roll(turned[0:8], 1) + turned[8:16] + lane_roll(turned[16:24], -1)
        lane8 = lax.broadcasted_iota(jnp.int32, (8, YP), 1)
        denoised = own_image[...] + jnp.where(lane8 < Y, residual, 0.0)
        for t in range(3):
            pair[t, 0:8] = denoised[:, 128 * t : 128 * t + 128]
            pair[t, 8:16] = denoised[:, 128 * t : 128 * t + 128]

        write(denoised_ref)

    phase_last()
    den_re, den_im = plane_of(pair, 0, 8), plane_of(pair, 1, 8)

    reg = reg_ref[0]
    for copy in rhs_copies:
        copy.wait()
    adjoint = jnp.sum(part_recv[...], axis=0)
    other = pltpu.roll(adjoint, 4, axis=0)
    first_rows = lax.broadcasted_iota(jnp.int32, (8, YP), 0) < 4
    right = (
        jnp.where(first_rows, adjoint, other) + reg * den_re,
        jnp.where(first_rows, other, adjoint) + reg * den_im,
    )
    energy = finish_stage(0, 2, energy_copies)

    mean = jnp.sum(energy, axis=1, keepdims=True) * (NS / Y / (Z * XW * Y))

    def spectrum_of(vector):
        v_re = jnp.broadcast_to(vector[0][None], (16, 8, YP)).reshape(128, YP)
        v_im = jnp.broadcast_to(vector[1][None], (16, 8, YP)).reshape(128, YP)
        m_re, m_im = maps_re[...], maps_im[...]
        weighted = jnp.concatenate([m_re * v_re - m_im * v_im, m_re * v_im + m_im * v_re], axis=1)
        return dot3(weighted, table_hi, table_lo, dot)

    def gram_map(vector):
        planes[...] = dot3(spectrum_of(vector), back_hi, back_lo, dot)
        m_re, m_im = maps_re[...], maps_im[...]
        f_re, f_im = planes[:, 0:YP], planes[:, YP : 2 * YP]
        real = jnp.sum((m_re * f_re + m_im * f_im).reshape(16, 8, YP), axis=0)
        imag = jnp.sum((m_re * f_im - m_im * f_re).reshape(16, 8, YP), axis=0)
        return real + pltpu.roll(real, 4, axis=0), imag + pltpu.roll(imag, 4, axis=0)

    def folded(first, second):
        product = first[0] * second[0] + first[1] * second[1]
        product = product[:, 0:128] + product[:, 128:256] + product[:, 256:384]
        return 0.5 * jnp.sum(product, axis=0, keepdims=True)

    pairs = [(i, j) for i in range(4) for j in range(i, 4)]
    basis = [right]

    def phase_krylov():
        del basis[1:]
        for _ in range(3):
            mapped = gram_map(basis[-1])
            basis.append((mapped[0] - mean * basis[-1][0], mapped[1] - mean * basis[-1][1]))
        last_spectrum = spectrum_of(basis[-1])
        last_energy = jnp.sum((last_spectrum * last_spectrum).reshape(16, 8, 256), axis=0)
        last_energy = last_energy[:, 0:128] + last_energy[:, 128:256]
        rows = [folded(basis[i], basis[j]) for i, j in pairs]
        rows.append(jnp.sum(last_energy, axis=0, keepdims=True))
        rows.append(jnp.zeros((16 - len(rows), 128), F32))
        packed = jnp.concatenate(rows, axis=0)
        for width in (64, 32, 16, 8):
            packed = packed + lane_roll(packed, width)
        place = lax.broadcasted_iota(jnp.int32, (16, 128), 1) // 8
        owner = lax.broadcasted_iota(jnp.int32, (16, 128), 0)
        return jnp.sum(jnp.where(place == owner, packed, 0.0), axis=0, keepdims=True)

    moments = phase_krylov()
    for stage in range(3):
        moments = finish_stage(1, stage, start_stage(1, stage, moments))
    def phase_solve():
        place = lax.broadcasted_iota(jnp.int32, (1, 128), 1) // 8
        values = [
            jnp.sum(jnp.where(place == i, moments, 0.0), axis=1, keepdims=True) for i in range(len(pairs) + 1)
        ]
        gram = {}
        for row, (i, j) in enumerate(pairs):
            gram[i, j] = gram[j, i] = values[row]
        shift = mean + reg
        matrix = {}
        for i in range(4):
            for j in range(i, 4):
                value = gram[i + 1, j] + shift * gram[i, j] if i < 3 else values[10] + reg * gram[3, 3]
                matrix[i, j] = matrix[j, i] = value
        norm = [jnp.where(matrix[i, i] > 1e-37, lax.rsqrt(jnp.maximum(matrix[i, i], 1e-37)), 0.0) for i in range(4)]
        side = [gram[0, i] * norm[i] for i in range(4)]
        for i in range(4):
            for j in range(i, 4):
                matrix[i, j] = matrix[j, i] = matrix[i, j] * norm[i] * norm[j]
        inverse = []
        for k in range(4):
            pivot = matrix[k, k]
            inverse.append(jnp.where(pivot > 2e-6, 1.0 / jnp.maximum(pivot, 2e-6), 0.0))
            for i in range(k + 1, 4):
                factor = matrix[i, k] * inverse[k]
                for j in range(i, 4):
                    matrix[i, j] = matrix[j, i] = matrix[i, j] - factor * matrix[k, j]
                side[i] = side[i] - factor * side[k]
        weights = [None] * 4
        for k in range(3, -1, -1):
            value = side[k]
            for j in range(k + 1, 4):
                value = value - matrix[k, j] * weights[j]
            weights[k] = value * inverse[k]
        real = sum(weights[k] * norm[k] * basis[k][0] for k in range(4))
        imag = sum(weights[k] * norm[k] * basis[k][1] for k in range(4))
        for t in range(3):
            pair[t, pl.ds(0, 8, stride=2), :] = real[:, 128 * t : 128 * t + 128]
            pair[t, pl.ds(1, 8, stride=2), :] = imag[:, 128 * t : 128 * t + 128]
        write(out_ref)

    phase_solve()


def local(image, sampled_lines, coil_maps, kspace, reg_weight, conv_first, conv_middle, conv_last):
    vmem = pl.BlockSpec(memory_space=pltpu.VMEM)
    anywhere = pl.BlockSpec(memory_space=pltpu.HBM)
    block = pltpu.VMEM((1, XB, 2, Y), F32)
    dma = pltpu.SemaphoreType.DMA
    return pl.pallas_call(
        kernel,
        out_shape=(block, block),
        in_specs=[anywhere] * 8,
        out_specs=(vmem, vmem),
        scratch_shapes=[
            pltpu.VMEM((1, XB, 2, Y), F32),
            pltpu.VMEM((1, NS), jnp.int32),
            pltpu.SMEM((1,), F32),
            pltpu.VMEM((27, 2, CH), BF16),
            pltpu.VMEM((54, CH, CH), BF16),
            pltpu.VMEM((27, 2, CH), BF16),
            pltpu.VMEM((6, 3, 16, 256), BF16),
            pltpu.VMEM((8, YP), F32),
            pltpu.VMEM((3, 6, 24, YP), F32),
            pltpu.VMEM((YP, 1280), F32),
            pltpu.VMEM((256, 1280), BF16),
            pltpu.VMEM((64, 128), F32),
            pltpu.VMEM((128, 128), F32),
            pltpu.VMEM((2, 768, 256), BF16),
            pltpu.VMEM((1152, 128), F32),
            pltpu.VMEM((1152, 128), BF16),
            pltpu.VMEM((5, 10, Y, 128), BF16),
            pltpu.VMEM((4, 8, Y, 128), BF16),
            pltpu.VMEM((3, 6, Y, 128), BF16),
            pltpu.VMEM((2 * YP, 256), BF16),
            pltpu.VMEM((2 * YP, 256), BF16),
            pltpu.VMEM((256, 2 * YP), BF16),
            pltpu.VMEM((256, 2 * YP), BF16),
            pltpu.VMEM((YP, 128), BF16),
            pltpu.VMEM((CL, XW, 2, Y), F32),
            pltpu.VMEM((CL, XW, 2, Y), F32),
            pltpu.VMEM((C, XB, 2, Y), F32),
            pltpu.VMEM((3, 8 * C, 128), F32),
            pltpu.VMEM((4 * C, 2 * YP), F32),
            pltpu.VMEM((4 * C, YP), F32),
            pltpu.VMEM((4 * C, YP), F32),
            pltpu.VMEM((8, 8, YP), F32),
            pltpu.VMEM((8, 8, YP), F32),
            pltpu.VMEM((3, 16, 128), F32),
            pltpu.VMEM((8, 128), F32),
            pltpu.VMEM((2, 3, 8, 1, 128), F32),
            dma((9,)), dma((17,)), dma((17,)), dma((7,)), dma((7,)), dma((7,)), dma((7,)),
            dma((2, 3, 7)), dma((2, 3, 7)), dma((6,)), dma((6,)),
        ],
        compiler_params=pltpu.CompilerParams(
            collective_id=0, has_side_effects=True, vmem_limit_bytes=LIMIT
        ),
    )(
        image, sampled_lines, coil_maps, kspace, reg_weight,
        conv_first.reshape(27, 2, CH), conv_middle.reshape(54, CH, CH), conv_last.transpose(0, 1, 2, 4, 3).reshape(27, 2, CH),
    )


def solution(mesh):
    in_specs = (
        P("slab", "coil", None, None),
        P("slab", None),
        P("coil", "slab", None, None, None),
        P("coil", "slab", None, None, None),
        P(),
        P(),
        P(),
        P(),
    )
    out_specs = (P("slab", "coil", None, None), P("slab", "coil", None, None))
    return jax.shard_map(local, mesh=mesh, in_specs=in_specs, out_specs=out_specs, check_vma=False)
```

```python
import functools
import math

import jax
import jax.numpy as jnp
from jax import lax
from jax.experimental import pallas as pl
from jax.experimental.pallas import tpu as pltpu
from jax.sharding import PartitionSpec as P

MESH = pl.DeviceIdType.MESH
F32 = jnp.float32
BF16 = jnp.bfloat16

Y = 320
YP = 384
XB = 4
CH = 64
C = 32
CL = 4
NS = 80
HALO = 4
XW = 32
Z = 64
X_CHIPS = 4
Y_CHIPS = 8
Z_CHIPS = 8
LIMIT = 56 * 2**20


def dot(a, b):
    return jnp.dot(a, b, preferred_element_type=F32)


def dot_t(a, b):
    return lax.dot_general(a, b, (((1,), (1,)), ((), ())), preferred_element_type=F32)


def split(v):
    high = v.astype(BF16)
    return high, (v - high.astype(F32)).astype(BF16)


def dot3(v, high_ref, low_ref, op):
    high, low = split(v)
    rows = v.shape[0]
    both = op(jnp.concatenate([high, low], axis=0), high_ref[...])
    return both[0:rows] + both[rows : 2 * rows] + op(high, low_ref[...])


def lane_roll(v, amount):
    return pltpu.roll(v, amount % v.shape[1], axis=1)


def kernel(
    image_hbm, lines_hbm, maps_hbm, kspace_hbm, reg_hbm, first_hbm, middle_hbm, last_hbm,
    denoised_ref, out_ref,
    image_ref, lines_ref, reg_ref, first_ref, middle_ref, last_ref,
    halo, own_image, feats, w1f, w1, wt, wl, wm, w4f, w4, p1, p2, p3,
    table_hi, table_lo, back_hi, back_lo, pick, local_maps, local_kspace, own_maps, inter, planes, maps_re, maps_im,
    part_send, part_recv, pair, energy_out, slots,
    local_sem, img_send, img_recv, map_send, map_recv, rhs_send, rhs_recv, sum_send, sum_recv,
    core_send, core_recv,
):
    s = lax.axis_index("slab")
    c = lax.axis_index("coil")
    x_chip, z_lo = c % X_CHIPS, c // X_CHIPS
    core, y_chip, z_hi = s % 2, (s // 2) % Y_CHIPS, s // (2 * Y_CHIPS)
    z_chip = z_hi * 2 + z_lo

    outward = 2 * core - 1
    offsets = [(r, dx) for r in (4, 3, 1, 2, 0, -1) for dx in (-1, 1, 0) if (r, dx) != (0, 0)]

    def needing(r, dx):
        away = r if r % 2 == 0 else -r
        return ((s - outward * away + Z) % Z, (c + dx + 8) % 8)

    def stage_partner(stage, d):
        if stage == 0:
            return (
                z_hi * 16 + y_chip * 2 + (core + d // 4) % 2,
                z_lo * 4 + (x_chip + d % 4) % 4,
            )
        if stage == 1:
            return (z_hi * 16 + ((y_chip + d) % 8) * 2 + core, c)
        z_new = (z_chip + d) % 8
        return ((z_new // 2) * 16 + y_chip * 2 + core, (z_new % 2) * 4 + x_chip)

    stage_index = (core * 4 + x_chip, y_chip, z_chip)

    image_in, lines_in, reg_in, first_in, middle_in, last_in = [
        pltpu.make_async_copy(source, target, local_sem.at[3 + i])
        for i, (source, target) in enumerate(
            (
                (image_hbm, image_ref),
                (lines_hbm, lines_ref),
                (reg_hbm, reg_ref),
                (first_hbm, first_ref),
                (middle_hbm, middle_ref),
                (last_hbm, last_ref),
            )
        )
    ]
    image_in.start()

    partners = [((s + outward * r + Z) % Z, (c + dx + 8) % 8) for r, dx in offsets]
    partners += [(s, (c + d) % 8) for d in range(1, 8)]
    partners += [stage_partner(stage, d) for stage in range(3) for d in range(1, 8)]
    barrier = pltpu.get_barrier_semaphore()
    for partner in partners:
        pl.semaphore_signal(barrier, inc=1, device_id=partner, device_id_type=MESH)

    for copy in (lines_in, first_in, last_in, reg_in):
        copy.start()
    local_copies = [
        pltpu.make_async_copy(maps_hbm.at[:, 0], local_maps, local_sem.at[0]),
        pltpu.make_async_copy(kspace_hbm.at[:, 0], local_kspace, local_sem.at[1]),
        pltpu.make_async_copy(
            maps_hbm.at[:, 0, pl.ds(c * XB, XB)], own_maps.at[pl.ds(c * CL, CL)], local_sem.at[2]
        ),
    ]
    for copy in local_copies:
        copy.start()
    middle_in.start()

    own_image[...] = jnp.zeros_like(own_image)
    image_in.wait()
    for x in range(XB):
        own_image[2 * x : 2 * x + 2, 0:Y] = image_ref[0, x]
    mine = own_image[...]
    tail = jnp.concatenate([mine[:, 256:384], jnp.zeros((8, 128), F32)], axis=1)
    halo[1, 1] = jnp.concatenate([mine[:, 0:256], tail], axis=0).astype(BF16)

    pl.semaphore_wait(barrier, len(partners))

    image_copies = {}
    for i, (r, dx) in enumerate(offsets):
        copy = pltpu.make_async_remote_copy(
            src_ref=halo.at[1, 1],
            dst_ref=halo.at[r + 1, 1 - dx],
            send_sem=img_send.at[i],
            recv_sem=img_recv.at[i],
            device_id=needing(r, dx),
            device_id_type=MESH,
        )
        copy.start()
        image_copies[r, dx] = copy
    lines_in.wait()

    def phase_tables():
        lines = jnp.concatenate([lines_ref[...], jnp.full((1, 128 - NS), -1, jnp.int32)], axis=1)
        position = lax.broadcasted_iota(jnp.int32, (YP, 128), 0)
        line = jnp.broadcast_to(lines, (YP, 128))
        inside = (position < Y) & (line >= 0)
        product = (position * line).astype(F32)
        phase = product - Y * jnp.floor((product + 0.5) * (1.0 / Y))
        half = jnp.abs(jnp.where(phase > Y / 2, phase - Y, phase))
        sine_sign = jnp.where(phase > Y / 2, -1.0, 1.0)
        low_half = half <= Y / 4
        angle = jnp.where(low_half, half, Y / 2 - half) * (2.0 * math.pi / Y)
        square = angle * angle
        cosine = jnp.full((YP, 128), 1.0 / math.factorial(14), F32) * -1.0
        sine = jnp.full((YP, 128), 1.0 / math.factorial(13), F32)
        for order in range(6, -1, -1):
            cosine = cosine * square + (-1.0) ** order / math.factorial(2 * order)
            if order < 6:
                sine = sine * square + (-1.0) ** order / math.factorial(2 * order + 1)
        scale = 1.0 / math.sqrt(Y)
        cosine = jnp.where(inside, jnp.where(low_half, cosine, -cosine) * scale, 0.0)
        sine = jnp.where(inside, sine * angle * sine_sign * scale, 0.0)
        for row, column, value in (
            (0, 0, cosine), (0, 128, -sine), (YP, 0, sine), (YP, 128, cosine),
        ):
            high, low = split(value)
            table_hi[row : row + YP, column : column + 128] = high
            table_lo[row : row + YP, column : column + 128] = low
        for row, column, value in (
            (0, 0, cosine), (128, 0, -sine), (0, YP, sine), (128, YP, cosine),
        ):
            high, low = split(jnp.transpose(value))
            back_hi[row : row + 128, column : column + YP] = high
            back_lo[row : row + 128, column : column + YP] = low
        pick[...] = jnp.where(inside & (position == line), 1.0, 0.0).astype(BF16)

    phase_tables()

    groups = inter.reshape(3, C, 8, 128)
    tiles = ((0, 128), (1, 128), (2, Y - 256))

    def plane_of(ref, start, count):
        return jnp.concatenate([ref[t, pl.ds(start, count, stride=2), :] for t in range(3)], axis=1)

    def load_planes(source):
        def move(group, carry):
            for x in range(XB):
                value = source(group, x)
                for t, width in tiles:
                    groups[t, group, 2 * x : 2 * x + 2, 0:width] = value[:, 128 * t : 128 * t + width]
            return carry

        lax.fori_loop(0, C, move, 0)
        return plane_of(inter, 0, 4 * C), plane_of(inter, 1, 4 * C)

    for copy in local_copies:
        copy.wait()
    inter[...] = jnp.zeros_like(inter)

    def phase_adjoint():
        kspace_re, kspace_im = load_planes(lambda group, x: local_kspace[group // 8, (group % 8) * XB + x])
        spectrum = []
        for plane in (kspace_re, kspace_im):
            high, low = split(plane)
            spectrum.append(dot(high, pick[...]) + dot(low, pick[...]))
        field = dot3(jnp.concatenate(spectrum, axis=1), back_hi, back_lo, dot)
        planes[...] = field
        s_re, s_im = load_planes(lambda group, x: local_maps[group // 8, (group % 8) * XB + x])
        energy = s_re * s_re + s_im * s_im
        energy = jnp.sum(energy.reshape(16, 8, YP), axis=0)
        energy_out[...] = energy[:, 0:128] + energy[:, 128:256] + energy[:, 256:384]
        f_re, f_im = planes[:, 0:YP], planes[:, YP : 2 * YP]
        sum_re = jnp.sum((s_re * f_re + s_im * f_im).reshape(CL, XW, YP), axis=0)
        sum_im = jnp.sum((s_re * f_im - s_im * f_re).reshape(CL, XW, YP), axis=0)
        for k in range(8):
            part_send[k, 0:4] = sum_re[4 * k : 4 * k + 4]
            part_send[k, 4:8] = sum_im[4 * k : 4 * k + 4]
        part_recv[c] = part_send[c]

    phase_adjoint()
    def start_stage(which, stage, value):
        index = stage_index[stage]
        slots[which, stage, index] = value
        copies = []
        for d in range(1, 8):
            copy = pltpu.make_async_remote_copy(
                src_ref=slots.at[which, stage, index],
                dst_ref=slots.at[which, stage, index],
                send_sem=sum_send.at[which, stage, d - 1],
                recv_sem=sum_recv.at[which, stage, d - 1],
                device_id=stage_partner(stage, d),
                device_id_type=MESH,
            )
            copy.start()
            copies.append(copy)
        return copies

    def finish_stage(which, stage, copies):
        for copy in copies:
            copy.wait()
        return jnp.sum(slots[which, stage], axis=0)

    energy_copies = start_stage(0, 0, jnp.sum(energy_out[...], axis=0, keepdims=True))

    def tap_slice(dz):
        return dz * core + (2 - dz) * (1 - core)

    def last_all():
        wl[...] = jnp.zeros_like(wl)
        for k in range(27):
            wl[2 * k : 2 * k + 2, 0:CH] = last_ref[tap_slice(k // 9) * 9 + k % 9].astype(F32)
        return wl[...]

    for copy in (first_in, middle_in, last_in, reg_in):
        copy.wait()

    def phase_weights():
        wt[...] = jnp.zeros_like(wt)
        for dy in range(3):
            for dz in range(3):
                for dx in range(3):
                    row = 2 * (dy * 9 + dz * 3 + dx)
                    wt[row : row + 2, 0:CH] = first_ref[tap_slice(dz) * 9 + dx * 3 + dy].astype(F32)
        w1f[...] = jnp.zeros_like(w1f)
        row8 = lax.broadcasted_iota(jnp.int32, (8, 128), 0)
        for q in range(9):
            low = jnp.where(row8 < 6, wt[6 * q : 6 * q + 8, :], 0.0)
            both = low + lane_roll(pltpu.roll(low, 2, axis=0), CH)
            for x in range(10):
                if x < 9:
                    w1f[24 * q + 2 * x : 24 * q + 2 * x + 8, 128 * x : 128 * x + 128] = both
                else:
                    w1f[24 * q + 18 : 24 * q + 24, 128 * x : 128 * x + 128] = low[0:6]
        w1[...] = w1f[0:256, :].astype(BF16)

        wm[...] = jnp.zeros_like(wm)

        def middle_weights(i, carry):
            layer, dz = i // 3, i % 3
            for dx in range(3):
                taps = [middle_ref[layer * 27 + tap_slice(dz) * 9 + dx * 3 + dy] for dy in range(3)]
                wm[layer, pl.ds(pl.multiple_of(dz * 256 + dx * CH, CH), CH), 0:128] = jnp.concatenate([taps[0], taps[2]], axis=1)
                wm[layer, pl.ds(pl.multiple_of(dz * 256 + dx * CH, CH), CH), 128:256] = jnp.concatenate([taps[1], taps[1]], axis=1)
            return carry

        lax.fori_loop(0, 6, middle_weights, 0)

        w4f[...] = jnp.zeros_like(w4f)
        turned = jnp.transpose(last_all())[0:CH]
        column = lax.broadcasted_iota(jnp.int32, (CH, 128), 1)
        for dz in range(3):
            for dx in range(3):
                merged = None
                for dy in range(3):
                    first_column = 2 * (dz * 9 + dx * 3 + dy)
                    tap = jnp.where((column >= first_column) & (column < first_column + 2), turned, 0.0)
                    tap = lane_roll(tap, 8 * dy - first_column)
                    merged = tap if merged is None else merged + tap
                for x in range(XB):
                    base = dz * 384 + (x + dx) * CH
                    w4f[base : base + CH, :] += merged if x == 0 else lane_roll(merged, 2 * x)
        w4[...] = w4f[...].astype(BF16)

    phase_weights()

    for (r, _), copy in image_copies.items():
        if r <= 1:
            copy.wait()
    energy_copies = start_stage(0, 1, finish_stage(0, 0, energy_copies))
    row24 = lax.broadcasted_iota(jnp.int32, (24, YP), 0) // 8 + (c - 1)

    def feature_slice(zi):
        slice_index = s + outward * (zi - 1)
        valid = (row24 >= 0) & (row24 < 8) & (slice_index >= 0) & (slice_index < Z)
        blocks = [halo[zi, k].astype(F32) for k in range(3)]
        value = jnp.concatenate(
            [jnp.concatenate([block[0:8], block[8:16, 0:128]], axis=1) for block in blocks], axis=0
        )
        value = jnp.where(valid, value, 0.0)
        feats[0, zi] = lane_roll(value, 1)
        feats[1, zi] = value
        feats[2, zi] = lane_roll(value, -1)

    lane = lax.broadcasted_iota(jnp.int32, (1, 256), 1)

    def first_layer(z):
        slice_index = s + outward * z
        slice_valid = (slice_index >= 0) & (slice_index < Z)
        columns = jnp.concatenate(
            [feats[dy, z : z + 3].reshape(72, YP) for dy in range(3)] + [jnp.zeros((40, YP), F32)],
            axis=0,
        )
        tall = jnp.transpose(columns)[0:Y].astype(BF16)
        for x in range(0, 10, 2):
            at = c * XB - 3 + x + lane // CH - lane // 128
            mask = jnp.where((at >= 0) & (at < XW) & slice_valid, 1.0, 0.0)
            product = dot(tall, w1[:, 128 * x : 128 * x + 256])
            product = (jnp.maximum(product, 0.0) * mask).astype(BF16)
            p1[z + 1, x] = product[:, 0:128]
            p1[z + 1, x + 1] = product[:, 128:256]

    low_lanes = lax.broadcasted_iota(jnp.int32, (Y, 128), 1) < CH

    rowi = lax.broadcasted_iota(jnp.int32, (Y, 128), 0)
    edge = jnp.where((low_lanes & (rowi == 0)) | (jnp.logical_not(low_lanes) & (rowi == Y - 1)), 0.0, 1.0)

    def middle_slice(layer, source, target, rows, z, sent=()):
        reach_x = (rows - XB) // 2
        slice_index = s + outward * z
        slice_valid = (slice_index >= 0) & (slice_index < Z)
        before = None
        for x in range(rows):
            operand = jnp.concatenate(
                [source[z + dz, x + 2 * k] for dz in range(3) for k in range(2)], axis=1
            )
            product = dot(operand, wm[layer])
            at = c * XB - reach_x + x
            mask = jnp.where((at >= 0) & (at < XW) & slice_valid, 1.0, 0.0).astype(F32)
            first_half = product[:, 0:128]
            outer = jnp.where(
                low_lanes, pltpu.roll(first_half, 1, axis=0), pltpu.roll(first_half, Y - 1, axis=0)
            )
            outer = outer * edge
            value = outer + lane_roll(outer, CH) + product[:, 128:256]
            value = jnp.maximum(value, 0.0) * mask
            if before is not None:
                target[z + 1, x - 1] = jnp.where(low_lanes, before, value).astype(BF16)
            before = value
            for count, copy in sent:
                if count == x:
                    copy.start()
        target[z + 1, rows - 1] = before.astype(BF16)
        for count, copy in sent:
            if count == rows:
                copy.start()

    def to_other_core(ref, blocks, index):
        return pltpu.make_async_remote_copy(
            src_ref=ref.at[1, blocks],
            dst_ref=ref.at[0, blocks],
            send_sem=core_send.at[index],
            recv_sem=core_recv.at[index],
            device_id=(s + 1 - 2 * core, c),
            device_id_type=MESH,
        )

    first_copy = to_other_core(p1, pl.ds(0, 10), 0)
    middle_copies = [(4, to_other_core(p2, pl.ds(0, 4), 1)), (8, to_other_core(p2, pl.ds(4, 4), 2))]
    hidden_copies = [(x + 1, to_other_core(p3, pl.ds(x, 1), 3 + x // 2)) for x in (0, 2, 4)]

    def phase_firstA():
        for zi in range(3):
            feature_slice(zi)
        first_layer(0)

    phase_firstA()
    first_copy.start()
    map_copies = []
    for d in range(1, 8):
        target = (c + d) % 8
        copy = pltpu.make_async_remote_copy(
            src_ref=maps_hbm.at[:, 0, pl.ds(target * XB, XB)],
            dst_ref=own_maps.at[pl.ds(c * CL, CL)],
            send_sem=map_send.at[d - 1],
            recv_sem=map_recv.at[d - 1],
            device_id=(s, target),
            device_id_type=MESH,
        )
        copy.start()
        map_copies.append(copy)
    rhs_copies = []
    for d in range(1, 8):
        target = (c + d) % 8
        copy = pltpu.make_async_remote_copy(
            src_ref=part_send.at[target],
            dst_ref=part_recv.at[c],
            send_sem=rhs_send.at[d - 1],
            recv_sem=rhs_recv.at[d - 1],
            device_id=(s, target),
            device_id_type=MESH,
        )
        copy.start()
        rhs_copies.append(copy)
    for z in range(1, 4):
        for dx in (-1, 0, 1):
            image_copies[z + 1, dx].wait()
        feature_slice(z + 2)
        first_layer(z)

    def phase_middleA():
        middle_slice(0, p1, p2, 8, 2)

    phase_middleA()
    first_copy.wait()

    def phase_middleB():
        middle_slice(0, p1, p2, 8, 0, middle_copies)

    phase_middleB()
    energy_copies = start_stage(0, 2, finish_stage(0, 1, energy_copies))

    def phase_middleC():
        middle_slice(0, p1, p2, 8, 1)

    phase_middleC()
    for _, copy in middle_copies:
        copy.wait()

    def phase_hiddenA():
        middle_slice(1, p2, p3, 6, 0, hidden_copies)

    phase_hiddenA()

    def phase_hiddenB():
        middle_slice(1, p2, p3, 6, 1)

    phase_hiddenB()

    def write(ref):
        for x in range(XB):
            for t, width in tiles:
                ref[0, x, :, 128 * t : 128 * t + width] = pair[t, 2 * x : 2 * x + 2, 0:width]

    for copy in map_copies:
        copy.wait()

    def phase_maps():
        s_re, s_im = load_planes(lambda group, x: own_maps[group, x])
        maps_re[...] = s_re
        maps_im[...] = s_im

    phase_maps()
    for _, copy in hidden_copies:
        copy.wait()

    def phase_last():
        operand = jnp.concatenate([p3[dz, 2 * k] for dz in range(3) for k in range(3)], axis=1)
        w1f[0:YP, 0:128] = jnp.zeros((YP, 128), F32)
        w1f[0:Y, 0:128] = dot(operand, w4[...])
        turned = jnp.transpose(w1f[0:YP, 0:128])
        residual = lane_roll(turned[0:8], 1) + turned[8:16] + lane_roll(turned[16:24], -1)
        lane8 = lax.broadcasted_iota(jnp.int32, (8, YP), 1)
        denoised = own_image[...] + jnp.where(lane8 < Y, residual, 0.0)
        for t in range(3):
            pair[t, 0:8] = denoised[:, 128 * t : 128 * t + 128]
            pair[t, 8:16] = denoised[:, 128 * t : 128 * t + 128]

        write(denoised_ref)

    phase_last()
    den_re, den_im = plane_of(pair, 0, 8), plane_of(pair, 1, 8)

    reg = reg_ref[0]
    for copy in rhs_copies:
        copy.wait()
    adjoint = jnp.sum(part_recv[...], axis=0)
    other = pltpu.roll(adjoint, 4, axis=0)
    first_rows = lax.broadcasted_iota(jnp.int32, (8, YP), 0) < 4
    right = (
        jnp.where(first_rows, adjoint, other) + reg * den_re,
        jnp.where(first_rows, other, adjoint) + reg * den_im,
    )
    energy = finish_stage(0, 2, energy_copies)

    mean = jnp.sum(energy, axis=1, keepdims=True) * (NS / Y / (Z * XW * Y))

    def spectrum_of(vector):
        v_re = jnp.broadcast_to(vector[0][None], (16, 8, YP)).reshape(128, YP)
        v_im = jnp.broadcast_to(vector[1][None], (16, 8, YP)).reshape(128, YP)
        m_re, m_im = maps_re[...], maps_im[...]
        weighted = jnp.concatenate([m_re * v_re - m_im * v_im, m_re * v_im + m_im * v_re], axis=1)
        return dot3(weighted, table_hi, table_lo, dot)

    def gram_map(vector):
        planes[...] = dot3(spectrum_of(vector), back_hi, back_lo, dot)
        m_re, m_im = maps_re[...], maps_im[...]
        f_re, f_im = planes[:, 0:YP], planes[:, YP : 2 * YP]
        real = jnp.sum((m_re * f_re + m_im * f_im).reshape(16, 8, YP), axis=0)
        imag = jnp.sum((m_re * f_im - m_im * f_re).reshape(16, 8, YP), axis=0)
        return real + pltpu.roll(real, 4, axis=0), imag + pltpu.roll(imag, 4, axis=0)

    def folded(first, second):
        product = first[0] * second[0] + first[1] * second[1]
        product = product[:, 0:128] + product[:, 128:256] + product[:, 256:384]
        return 0.5 * jnp.sum(product, axis=0, keepdims=True)

    pairs = [(i, j) for i in range(4) for j in range(i, 4)]
    basis = [right]

    def phase_krylov():
        del basis[1:]
        for _ in range(3):
            mapped = gram_map(basis[-1])
            basis.append((mapped[0] - mean * basis[-1][0], mapped[1] - mean * basis[-1][1]))
        last_spectrum = spectrum_of(basis[-1])
        last_energy = jnp.sum((last_spectrum * last_spectrum).reshape(16, 8, 256), axis=0)
        last_energy = last_energy[:, 0:128] + last_energy[:, 128:256]
        rows = [folded(basis[i], basis[j]) for i, j in pairs]
        rows.append(jnp.sum(last_energy, axis=0, keepdims=True))
        rows.append(jnp.zeros((16 - len(rows), 128), F32))
        packed = jnp.concatenate(rows, axis=0)
        for width in (64, 32, 16, 8):
            packed = packed + lane_roll(packed, width)
        place = lax.broadcasted_iota(jnp.int32, (16, 128), 1) // 8
        owner = lax.broadcasted_iota(jnp.int32, (16, 128), 0)
        return jnp.sum(jnp.where(place == owner, packed, 0.0), axis=0, keepdims=True)

    moments = phase_krylov()
    for stage in range(3):
        moments = finish_stage(1, stage, start_stage(1, stage, moments))
    def phase_solve():
        place = lax.broadcasted_iota(jnp.int32, (1, 128), 1) // 8
        values = [
            jnp.sum(jnp.where(place == i, moments, 0.0), axis=1, keepdims=True) for i in range(len(pairs) + 1)
        ]
        gram = {}
        for row, (i, j) in enumerate(pairs):
            gram[i, j] = gram[j, i] = values[row]
        shift = mean + reg
        matrix = {}
        for i in range(4):
            for j in range(i, 4):
                value = gram[i + 1, j] + shift * gram[i, j] if i < 3 else values[10] + reg * gram[3, 3]
                matrix[i, j] = matrix[j, i] = value
        norm = [jnp.where(matrix[i, i] > 1e-37, lax.rsqrt(jnp.maximum(matrix[i, i], 1e-37)), 0.0) for i in range(4)]
        side = [gram[0, i] * norm[i] for i in range(4)]
        for i in range(4):
            for j in range(i, 4):
                matrix[i, j] = matrix[j, i] = matrix[i, j] * norm[i] * norm[j]
        inverse = []
        for k in range(4):
            pivot = matrix[k, k]
            inverse.append(jnp.where(pivot > 2e-6, 1.0 / jnp.maximum(pivot, 2e-6), 0.0))
            for i in range(k + 1, 4):
                factor = matrix[i, k] * inverse[k]
                for j in range(i, 4):
                    matrix[i, j] = matrix[j, i] = matrix[i, j] - factor * matrix[k, j]
                side[i] = side[i] - factor * side[k]
        weights = [None] * 4
        for k in range(3, -1, -1):
            value = side[k]
            for j in range(k + 1, 4):
                value = value - matrix[k, j] * weights[j]
            weights[k] = value * inverse[k]
        real = sum(weights[k] * norm[k] * basis[k][0] for k in range(4))
        imag = sum(weights[k] * norm[k] * basis[k][1] for k in range(4))
        for t in range(3):
            pair[t, pl.ds(0, 8, stride=2), :] = real[:, 128 * t : 128 * t + 128]
            pair[t, pl.ds(1, 8, stride=2), :] = imag[:, 128 * t : 128 * t + 128]
        write(out_ref)

    phase_solve()


def local(image, sampled_lines, coil_maps, kspace, reg_weight, conv_first, conv_middle, conv_last):
    vmem = pl.BlockSpec(memory_space=pltpu.VMEM)
    anywhere = pl.BlockSpec(memory_space=pltpu.HBM)
    block = pltpu.VMEM((1, XB, 2, Y), F32)
    dma = pltpu.SemaphoreType.DMA
    return pl.pallas_call(
        kernel,
        out_shape=(block, block),
        in_specs=[anywhere] * 8,
        out_specs=(vmem, vmem),
        scratch_shapes=[
            pltpu.VMEM((1, XB, 2, Y), F32),
            pltpu.VMEM((1, NS), jnp.int32),
            pltpu.SMEM((1,), F32),
            pltpu.VMEM((27, 2, CH), BF16),
            pltpu.VMEM((54, CH, CH), BF16),
            pltpu.VMEM((27, 2, CH), BF16),
            pltpu.VMEM((6, 3, 16, 256), BF16),
            pltpu.VMEM((8, YP), F32),
            pltpu.VMEM((3, 6, 24, YP), F32),
            pltpu.VMEM((YP, 1280), F32),
            pltpu.VMEM((256, 1280), BF16),
            pltpu.VMEM((64, 128), F32),
            pltpu.VMEM((128, 128), F32),
            pltpu.VMEM((2, 768, 256), BF16),
            pltpu.VMEM((1152, 128), F32),
            pltpu.VMEM((1152, 128), BF16),
            pltpu.VMEM((5, 10, Y, 128), BF16),
            pltpu.VMEM((4, 8, Y, 128), BF16),
            pltpu.VMEM((3, 6, Y, 128), BF16),
            pltpu.VMEM((2 * YP, 256), BF16),
            pltpu.VMEM((2 * YP, 256), BF16),
            pltpu.VMEM((256, 2 * YP), BF16),
            pltpu.VMEM((256, 2 * YP), BF16),
            pltpu.VMEM((YP, 128), BF16),
            pltpu.VMEM((CL, XW, 2, Y), F32),
            pltpu.VMEM((CL, XW, 2, Y), F32),
            pltpu.VMEM((C, XB, 2, Y), F32),
            pltpu.VMEM((3, 8 * C, 128), F32),
            pltpu.VMEM((4 * C, 2 * YP), F32),
            pltpu.VMEM((4 * C, YP), F32),
            pltpu.VMEM((4 * C, YP), F32),
            pltpu.VMEM((8, 8, YP), F32),
            pltpu.VMEM((8, 8, YP), F32),
            pltpu.VMEM((3, 16, 128), F32),
            pltpu.VMEM((8, 128), F32),
            pltpu.VMEM((2, 3, 8, 1, 128), F32),
            dma((9,)), dma((17,)), dma((17,)), dma((7,)), dma((7,)), dma((7,)), dma((7,)),
            dma((2, 3, 7)), dma((2, 3, 7)), dma((6,)), dma((6,)),
        ],
        compiler_params=pltpu.CompilerParams(
            collective_id=0, has_side_effects=True, vmem_limit_bytes=LIMIT
        ),
    )(
        image, sampled_lines, coil_maps, kspace, reg_weight,
        conv_first.reshape(27, 2, CH), conv_middle.reshape(54, CH, CH), conv_last.transpose(0, 1, 2, 4, 3).reshape(27, 2, CH),
    )


def solution(mesh):
    in_specs = (
        P("slab", "coil", None, None),
        P("slab", None),
        P("coil", "slab", None, None, None),
        P("coil", "slab", None, None, None),
        P(),
        P(),
        P(),
        P(),
    )
    out_specs = (P("slab", "coil", None, None), P("slab", "coil", None, None))
    return jax.shard_map(local, mesh=mesh, in_specs=in_specs, out_specs=out_specs, check_vma=False)
```

```python
import functools
import math

import jax
import jax.numpy as jnp
from jax import lax
from jax.experimental import pallas as pl
from jax.experimental.pallas import tpu as pltpu
from jax.sharding import PartitionSpec as P

MESH = pl.DeviceIdType.MESH
F32 = jnp.float32
BF16 = jnp.bfloat16

Y = 320
YP = 384
XB = 4
CH = 64
C = 32
CL = 4
NS = 80
HALO = 4
XW = 32
Z = 64
X_CHIPS = 4
Y_CHIPS = 8
Z_CHIPS = 8
LIMIT = 56 * 2**20


def dot(a, b):
    return jnp.dot(a, b, preferred_element_type=F32)


def dot_t(a, b):
    return lax.dot_general(a, b, (((1,), (1,)), ((), ())), preferred_element_type=F32)


def split(v):
    high = v.astype(BF16)
    return high, (v - high.astype(F32)).astype(BF16)


def dot3(v, high_ref, low_ref, op):
    high, low = split(v)
    rows = v.shape[0]
    both = op(jnp.concatenate([high, low], axis=0), high_ref[...])
    return both[0:rows] + both[rows : 2 * rows] + op(high, low_ref[...])


def lane_roll(v, amount):
    return pltpu.roll(v, amount % v.shape[1], axis=1)


def kernel(
    image_hbm, lines_hbm, maps_hbm, kspace_hbm, reg_hbm, first_hbm, middle_hbm, last_hbm,
    denoised_ref, out_ref,
    image_ref, lines_ref, reg_ref, first_ref, middle_ref, last_ref,
    halo, own_image, feats, w1f, w1, wt, wl, wm, w4f, w4, p1, p2, p3,
    table_hi, table_lo, back_hi, back_lo, pick, local_maps, local_kspace, own_maps, inter, planes, maps_re, maps_im,
    part_send, part_recv, pair, energy_out, slots,
    local_sem, img_send, img_recv, map_send, map_recv, rhs_send, rhs_recv, sum_send, sum_recv,
    core_send, core_recv,
):
    s = lax.axis_index("slab")
    c = lax.axis_index("coil")
    x_chip, z_lo = c % X_CHIPS, c // X_CHIPS
    core, y_chip, z_hi = s % 2, (s // 2) % Y_CHIPS, s // (2 * Y_CHIPS)
    z_chip = z_hi * 2 + z_lo

    outward = 2 * core - 1
    offsets = [(r, dx) for r in (4, 3, 1, 2, 0, -1) for dx in (-1, 1, 0) if (r, dx) != (0, 0)]

    def needing(r, dx):
        away = r if r % 2 == 0 else -r
        return ((s - outward * away + Z) % Z, (c + dx + 8) % 8)

    def stage_partner(stage, d):
        if stage == 0:
            return (
                z_hi * 16 + y_chip * 2 + (core + d // 4) % 2,
                z_lo * 4 + (x_chip + d % 4) % 4,
            )
        if stage == 1:
            return (z_hi * 16 + ((y_chip + d) % 8) * 2 + core, c)
        z_new = (z_chip + d) % 8
        return ((z_new // 2) * 16 + y_chip * 2 + core, (z_new % 2) * 4 + x_chip)

    stage_index = (core * 4 + x_chip, y_chip, z_chip)

    image_in, lines_in, reg_in, first_in, middle_in, last_in = [
        pltpu.make_async_copy(source, target, local_sem.at[3 + i])
        for i, (source, target) in enumerate(
            (
                (image_hbm, image_ref),
                (lines_hbm, lines_ref),
                (reg_hbm, reg_ref),
                (first_hbm, first_ref),
                (middle_hbm, middle_ref),
                (last_hbm, last_ref),
            )
        )
    ]
    image_in.start()

    partners = [((s + outward * r + Z) % Z, (c + dx + 8) % 8) for r, dx in offsets]
    partners += [(s, (c + d) % 8) for d in range(1, 8)]
    partners += [stage_partner(stage, d) for stage in range(3) for d in range(1, 8)]
    barrier = pltpu.get_barrier_semaphore()
    for partner in partners:
        pl.semaphore_signal(barrier, inc=1, device_id=partner, device_id_type=MESH)

    for copy in (lines_in, first_in, last_in, reg_in):
        copy.start()
    local_copies = [
        pltpu.make_async_copy(maps_hbm.at[:, 0], local_maps, local_sem.at[0]),
        pltpu.make_async_copy(kspace_hbm.at[:, 0], local_kspace, local_sem.at[1]),
        pltpu.make_async_copy(
            maps_hbm.at[:, 0, pl.ds(c * XB, XB)], own_maps.at[pl.ds(c * CL, CL)], local_sem.at[2]
        ),
    ]
    for copy in local_copies:
        copy.start()
    middle_in.start()

    own_image[...] = jnp.zeros_like(own_image)
    image_in.wait()
    for x in range(XB):
        own_image[2 * x : 2 * x + 2, 0:Y] = image_ref[0, x]
    mine = own_image[...]
    tail = jnp.concatenate([mine[:, 256:384], jnp.zeros((8, 128), F32)], axis=1)
    halo[1, 1] = jnp.concatenate([mine[:, 0:256], tail], axis=0).astype(BF16)

    pl.semaphore_wait(barrier, len(partners))

    image_copies = {}
    for i, (r, dx) in enumerate(offsets):
        copy = pltpu.make_async_remote_copy(
            src_ref=halo.at[1, 1],
            dst_ref=halo.at[r + 1, 1 - dx],
            send_sem=img_send.at[i],
            recv_sem=img_recv.at[i],
            device_id=needing(r, dx),
            device_id_type=MESH,
        )
        copy.start()
        image_copies[r, dx] = copy
    lines_in.wait()

    def phase_tables():
        lines = jnp.concatenate([lines_ref[...], jnp.full((1, 128 - NS), -1, jnp.int32)], axis=1)
        position = lax.broadcasted_iota(jnp.int32, (YP, 128), 0)
        line = jnp.broadcast_to(lines, (YP, 128))
        inside = (position < Y) & (line >= 0)
        product = (position * line).astype(F32)
        phase = product - Y * jnp.floor((product + 0.5) * (1.0 / Y))
        half = jnp.abs(jnp.where(phase > Y / 2, phase - Y, phase))
        sine_sign = jnp.where(phase > Y / 2, -1.0, 1.0)
        low_half = half <= Y / 4
        angle = jnp.where(low_half, half, Y / 2 - half) * (2.0 * math.pi / Y)
        square = angle * angle
        cosine = jnp.full((YP, 128), 1.0 / math.factorial(14), F32) * -1.0
        sine = jnp.full((YP, 128), 1.0 / math.factorial(13), F32)
        for order in range(6, -1, -1):
            cosine = cosine * square + (-1.0) ** order / math.factorial(2 * order)
            if order < 6:
                sine = sine * square + (-1.0) ** order / math.factorial(2 * order + 1)
        scale = 1.0 / math.sqrt(Y)
        cosine = jnp.where(inside, jnp.where(low_half, cosine, -cosine) * scale, 0.0)
        sine = jnp.where(inside, sine * angle * sine_sign * scale, 0.0)
        for row, column, value in (
            (0, 0, cosine), (0, 128, -sine), (YP, 0, sine), (YP, 128, cosine),
        ):
            high, low = split(value)
            table_hi[row : row + YP, column : column + 128] = high
            table_lo[row : row + YP, column : column + 128] = low
        for row, column, value in (
            (0, 0, cosine), (128, 0, -sine), (0, YP, sine), (128, YP, cosine),
        ):
            high, low = split(jnp.transpose(value))
            back_hi[row : row + 128, column : column + YP] = high
            back_lo[row : row + 128, column : column + YP] = low
        pick[...] = jnp.where(inside & (position == line), 1.0, 0.0).astype(BF16)

    phase_tables()

    groups = inter.reshape(3, C, 8, 128)
    tiles = ((0, 128), (1, 128), (2, Y - 256))

    def plane_of(ref, start, count):
        return jnp.concatenate([ref[t, pl.ds(start, count, stride=2), :] for t in range(3)], axis=1)

    def load_planes(source):
        def move(group, carry):
            for x in range(XB):
                value = source(group, x)
                for t, width in tiles:
                    groups[t, group, 2 * x : 2 * x + 2, 0:width] = value[:, 128 * t : 128 * t + width]
            return carry

        lax.fori_loop(0, C, move, 0)
        return plane_of(inter, 0, 4 * C), plane_of(inter, 1, 4 * C)

    for copy in local_copies:
        copy.wait()
    inter[...] = jnp.zeros_like(inter)

    def phase_adjoint():
        kspace_re, kspace_im = load_planes(lambda group, x: local_kspace[group // 8, (group % 8) * XB + x])
        spectrum = []
        for plane in (kspace_re, kspace_im):
            high, low = split(plane)
            spectrum.append(dot(high, pick[...]) + dot(low, pick[...]))
        field = dot3(jnp.concatenate(spectrum, axis=1), back_hi, back_lo, dot)
        planes[...] = field
        s_re, s_im = load_planes(lambda group, x: local_maps[group // 8, (group % 8) * XB + x])
        energy = s_re * s_re + s_im * s_im
        energy = jnp.sum(energy.reshape(16, 8, YP), axis=0)
        energy_out[...] = energy[:, 0:128] + energy[:, 128:256] + energy[:, 256:384]
        f_re, f_im = planes[:, 0:YP], planes[:, YP : 2 * YP]
        sum_re = jnp.sum((s_re * f_re + s_im * f_im).reshape(CL, XW, YP), axis=0)
        sum_im = jnp.sum((s_re * f_im - s_im * f_re).reshape(CL, XW, YP), axis=0)
        for k in range(8):
            part_send[k, 0:4] = sum_re[4 * k : 4 * k + 4]
            part_send[k, 4:8] = sum_im[4 * k : 4 * k + 4]
        part_recv[c] = part_send[c]

    phase_adjoint()
    def start_stage(which, stage, value):
        index = stage_index[stage]
        slots[which, stage, index] = value
        copies = []
        for d in range(1, 8):
            copy = pltpu.make_async_remote_copy(
                src_ref=slots.at[which, stage, index],
                dst_ref=slots.at[which, stage, index],
                send_sem=sum_send.at[which, stage, d - 1],
                recv_sem=sum_recv.at[which, stage, d - 1],
                device_id=stage_partner(stage, d),
                device_id_type=MESH,
            )
            copy.start()
            copies.append(copy)
        return copies

    def finish_stage(which, stage, copies):
        for copy in copies:
            copy.wait()
        return jnp.sum(slots[which, stage], axis=0)

    energy_copies = start_stage(0, 0, jnp.sum(energy_out[...], axis=0, keepdims=True))

    def tap_slice(dz):
        return dz * core + (2 - dz) * (1 - core)

    def last_all():
        wl[...] = jnp.zeros_like(wl)
        for k in range(27):
            wl[2 * k : 2 * k + 2, 0:CH] = last_ref[tap_slice(k // 9) * 9 + k % 9].astype(F32)
        return wl[...]

    for copy in (first_in, middle_in, last_in, reg_in):
        copy.wait()

    def phase_weights():
        wt[...] = jnp.zeros_like(wt)
        for dy in range(3):
            for dz in range(3):
                for dx in range(3):
                    row = 2 * (dy * 9 + dz * 3 + dx)
                    wt[row : row + 2, 0:CH] = first_ref[tap_slice(dz) * 9 + dx * 3 + dy].astype(F32)
        w1f[...] = jnp.zeros_like(w1f)
        row8 = lax.broadcasted_iota(jnp.int32, (8, 128), 0)
        for q in range(9):
            low = jnp.where(row8 < 6, wt[6 * q : 6 * q + 8, :], 0.0)
            both = low + lane_roll(pltpu.roll(low, 2, axis=0), CH)
            for x in range(10):
                if x < 9:
                    w1f[24 * q + 2 * x : 24 * q + 2 * x + 8, 128 * x : 128 * x + 128] = both
                else:
                    w1f[24 * q + 18 : 24 * q + 24, 128 * x : 128 * x + 128] = low[0:6]
        w1[...] = w1f[0:256, :].astype(BF16)

        wm[...] = jnp.zeros_like(wm)

        def middle_weights(i, carry):
            layer, dz = i // 3, i % 3
            for dx in range(3):
                taps = [middle_ref[layer * 27 + tap_slice(dz) * 9 + dx * 3 + dy] for dy in range(3)]
                wm[layer, pl.ds(pl.multiple_of(dz * 256 + dx * CH, CH), CH), 0:128] = jnp.concatenate([taps[0], taps[2]], axis=1)
                wm[layer, pl.ds(pl.multiple_of(dz * 256 + dx * CH, CH), CH), 128:256] = jnp.concatenate([taps[1], taps[1]], axis=1)
            return carry

        lax.fori_loop(0, 6, middle_weights, 0)

        w4f[...] = jnp.zeros_like(w4f)
        turned = jnp.transpose(last_all())[0:CH]
        column = lax.broadcasted_iota(jnp.int32, (CH, 128), 1)
        for dz in range(3):
            for dx in range(3):
                merged = None
                for dy in range(3):
                    first_column = 2 * (dz * 9 + dx * 3 + dy)
                    tap = jnp.where((column >= first_column) & (column < first_column + 2), turned, 0.0)
                    tap = lane_roll(tap, 8 * dy - first_column)
                    merged = tap if merged is None else merged + tap
                for x in range(XB):
                    base = dz * 384 + (x + dx) * CH
                    w4f[base : base + CH, :] += merged if x == 0 else lane_roll(merged, 2 * x)
        w4[...] = w4f[...].astype(BF16)

    phase_weights()

    for (r, _), copy in image_copies.items():
        if r <= 1:
            copy.wait()
    energy_copies = start_stage(0, 1, finish_stage(0, 0, energy_copies))
    row24 = lax.broadcasted_iota(jnp.int32, (24, YP), 0) // 8 + (c - 1)

    def feature_slice(zi):
        slice_index = s + outward * (zi - 1)
        valid = (row24 >= 0) & (row24 < 8) & (slice_index >= 0) & (slice_index < Z)
        blocks = [halo[zi, k].astype(F32) for k in range(3)]
        value = jnp.concatenate(
            [jnp.concatenate([block[0:8], block[8:16, 0:128]], axis=1) for block in blocks], axis=0
        )
        value = jnp.where(valid, value, 0.0)
        feats[0, zi] = lane_roll(value, 1)
        feats[1, zi] = value
        feats[2, zi] = lane_roll(value, -1)

    lane = lax.broadcasted_iota(jnp.int32, (1, 256), 1)

    def first_layer(z):
        slice_index = s + outward * z
        slice_valid = (slice_index >= 0) & (slice_index < Z)
        columns = jnp.concatenate(
            [feats[dy, z : z + 3].reshape(72, YP) for dy in range(3)] + [jnp.zeros((40, YP), F32)],
            axis=0,
        )
        tall = jnp.transpose(columns)[0:Y].astype(BF16)
        for x in range(0, 10, 2):
            at = c * XB - 3 + x + lane // CH - lane // 128
            mask = jnp.where((at >= 0) & (at < XW) & slice_valid, 1.0, 0.0)
            product = dot(tall, w1[:, 128 * x : 128 * x + 256])
            product = (jnp.maximum(product, 0.0) * mask).astype(BF16)
            p1[z + 1, x] = product[:, 0:128]
            p1[z + 1, x + 1] = product[:, 128:256]

    low_lanes = lax.broadcasted_iota(jnp.int32, (Y, 128), 1) < CH

    rowi = lax.broadcasted_iota(jnp.int32, (Y, 128), 0)
    edge = jnp.where((low_lanes & (rowi == 0)) | (jnp.logical_not(low_lanes) & (rowi == Y - 1)), 0.0, 1.0)

    def middle_slice(layer, source, target, rows, z, sent=()):
        reach_x = (rows - XB) // 2
        slice_index = s + outward * z
        slice_valid = (slice_index >= 0) & (slice_index < Z)
        before = None
        for x in range(rows):
            operand = jnp.concatenate(
                [source[z + dz, x + 2 * k] for dz in range(3) for k in range(2)], axis=1
            )
            product = dot(operand, wm[layer])
            at = c * XB - reach_x + x
            mask = jnp.where((at >= 0) & (at < XW) & slice_valid, 1.0, 0.0).astype(F32)
            first_half = product[:, 0:128]
            outer = jnp.where(
                low_lanes, pltpu.roll(first_half, 1, axis=0), pltpu.roll(first_half, Y - 1, axis=0)
            )
            outer = outer * edge
            value = outer + lane_roll(outer, CH) + product[:, 128:256]
            value = jnp.maximum(value, 0.0) * mask
            if before is not None:
                target[z + 1, x - 1] = jnp.where(low_lanes, before, value).astype(BF16)
            before = value
            for count, copy in sent:
                if count == x:
                    copy.start()
        target[z + 1, rows - 1] = before.astype(BF16)
        for count, copy in sent:
            if count == rows:
                copy.start()

    def to_other_core(ref, blocks, index):
        return pltpu.make_async_remote_copy(
            src_ref=ref.at[1, blocks],
            dst_ref=ref.at[0, blocks],
            send_sem=core_send.at[index],
            recv_sem=core_recv.at[index],
            device_id=(s + 1 - 2 * core, c),
            device_id_type=MESH,
        )

    first_copy = to_other_core(p1, pl.ds(0, 10), 0)
    middle_copies = [(4, to_other_core(p2, pl.ds(0, 4), 1)), (8, to_other_core(p2, pl.ds(4, 4), 2))]
    hidden_copies = [(x + 1, to_other_core(p3, pl.ds(x, 1), 3 + x // 2)) for x in (0, 2, 4)]

    def phase_firstA():
        for zi in range(3):
            feature_slice(zi)
        first_layer(0)

    phase_firstA()
    first_copy.start()
    map_copies = []
    for d in range(1, 8):
        target = (c + d) % 8
        copy = pltpu.make_async_remote_copy(
            src_ref=maps_hbm.at[:, 0, pl.ds(target * XB, XB)],
            dst_ref=own_maps.at[pl.ds(c * CL, CL)],
            send_sem=map_send.at[d - 1],
            recv_sem=map_recv.at[d - 1],
            device_id=(s, target),
            device_id_type=MESH,
        )
        copy.start()
        map_copies.append(copy)
    rhs_copies = []
    for d in range(1, 8):
        target = (c + d) % 8
        copy = pltpu.make_async_remote_copy(
            src_ref=part_send.at[target],
            dst_ref=part_recv.at[c],
            send_sem=rhs_send.at[d - 1],
            recv_sem=rhs_recv.at[d - 1],
            device_id=(s, target),
            device_id_type=MESH,
        )
        copy.start()
        rhs_copies.append(copy)
    for z in range(1, 4):
        for dx in (-1, 0, 1):
            image_copies[z + 1, dx].wait()
        feature_slice(z + 2)
        first_layer(z)

    def phase_middleA():
        middle_slice(0, p1, p2, 8, 2)

    phase_middleA()
    first_copy.wait()

    def phase_middleB():
        middle_slice(0, p1, p2, 8, 0, middle_copies)

    phase_middleB()
    energy_copies = start_stage(0, 2, finish_stage(0, 1, energy_copies))

    def phase_middleC():
        middle_slice(0, p1, p2, 8, 1)

    phase_middleC()
    for _, copy in middle_copies:
        copy.wait()

    def phase_hiddenA():
        middle_slice(1, p2, p3, 6, 0, hidden_copies)

    phase_hiddenA()

    def phase_hiddenB():
        middle_slice(1, p2, p3, 6, 1)

    phase_hiddenB()

    def write(ref):
        for x in range(XB):
            for t, width in tiles:
                ref[0, x, :, 128 * t : 128 * t + width] = pair[t, 2 * x : 2 * x + 2, 0:width]

    for copy in map_copies:
        copy.wait()

    def phase_maps():
        s_re, s_im = load_planes(lambda group, x: own_maps[group, x])
        maps_re[...] = s_re
        maps_im[...] = s_im

    phase_maps()
    for _, copy in hidden_copies:
        copy.wait()

    def phase_last():
        operand = jnp.concatenate([p3[dz, 2 * k] for dz in range(3) for k in range(3)], axis=1)
        w1f[0:YP, 0:128] = jnp.zeros((YP, 128), F32)
        w1f[0:Y, 0:128] = dot(operand, w4[...])
        turned = jnp.transpose(w1f[0:YP, 0:128])
        residual = lane_roll(turned[0:8], 1) + turned[8:16] + lane_roll(turned[16:24], -1)
        lane8 = lax.broadcasted_iota(jnp.int32, (8, YP), 1)
        denoised = own_image[...] + jnp.where(lane8 < Y, residual, 0.0)
        for t in range(3):
            pair[t, 0:8] = denoised[:, 128 * t : 128 * t + 128]
            pair[t, 8:16] = denoised[:, 128 * t : 128 * t + 128]

        write(denoised_ref)

    phase_last()
    den_re, den_im = plane_of(pair, 0, 8), plane_of(pair, 1, 8)

    reg = reg_ref[0]
    for copy in rhs_copies:
        copy.wait()
    adjoint = jnp.sum(part_recv[...], axis=0)
    other = pltpu.roll(adjoint, 4, axis=0)
    first_rows = lax.broadcasted_iota(jnp.int32, (8, YP), 0) < 4
    right = (
        jnp.where(first_rows, adjoint, other) + reg * den_re,
        jnp.where(first_rows, other, adjoint) + reg * den_im,
    )
    def spectrum_of(vector):
        v_re = jnp.broadcast_to(vector[0][None], (16, 8, YP)).reshape(128, YP)
        v_im = jnp.broadcast_to(vector[1][None], (16, 8, YP)).reshape(128, YP)
        m_re, m_im = maps_re[...], maps_im[...]
        weighted = jnp.concatenate([m_re * v_re - m_im * v_im, m_re * v_im + m_im * v_re], axis=1)
        return dot3(weighted, table_hi, table_lo, dot)

    def gram_map(vector):
        planes[...] = dot3(spectrum_of(vector), back_hi, back_lo, dot)
        m_re, m_im = maps_re[...], maps_im[...]
        f_re, f_im = planes[:, 0:YP], planes[:, YP : 2 * YP]
        real = jnp.sum((m_re * f_re + m_im * f_im).reshape(16, 8, YP), axis=0)
        imag = jnp.sum((m_re * f_im - m_im * f_re).reshape(16, 8, YP), axis=0)
        return real + pltpu.roll(real, 4, axis=0), imag + pltpu.roll(imag, 4, axis=0)

    def folded(first, second):
        product = first[0] * second[0] + first[1] * second[1]
        product = product[:, 0:128] + product[:, 128:256] + product[:, 256:384]
        return 0.5 * jnp.sum(product, axis=0, keepdims=True)

    pairs = [(i, j) for i in range(4) for j in range(i, 4)]
    basis = [right]
    first_mapped = gram_map(right)
    energy = finish_stage(0, 2, energy_copies)

    mean = jnp.sum(energy, axis=1, keepdims=True) * (NS / Y / (Z * XW * Y))

    def phase_krylov():
        del basis[1:]
        for step in range(3):
            mapped = gram_map(basis[-1]) if step else first_mapped
            basis.append((mapped[0] - mean * basis[-1][0], mapped[1] - mean * basis[-1][1]))
        last_spectrum = spectrum_of(basis[-1])
        last_energy = jnp.sum((last_spectrum * last_spectrum).reshape(16, 8, 256), axis=0)
        last_energy = last_energy[:, 0:128] + last_energy[:, 128:256]
        rows = [folded(basis[i], basis[j]) for i, j in pairs]
        rows.append(jnp.sum(last_energy, axis=0, keepdims=True))
        rows.append(jnp.zeros((16 - len(rows), 128), F32))
        packed = jnp.concatenate(rows, axis=0)
        for width in (64, 32, 16, 8):
            packed = packed + lane_roll(packed, width)
        place = lax.broadcasted_iota(jnp.int32, (16, 128), 1) // 8
        owner = lax.broadcasted_iota(jnp.int32, (16, 128), 0)
        return jnp.sum(jnp.where(place == owner, packed, 0.0), axis=0, keepdims=True)

    moments = phase_krylov()
    for stage in range(3):
        moments = finish_stage(1, stage, start_stage(1, stage, moments))
    def phase_solve():
        place = lax.broadcasted_iota(jnp.int32, (1, 128), 1) // 8
        values = [
            jnp.sum(jnp.where(place == i, moments, 0.0), axis=1, keepdims=True) for i in range(len(pairs) + 1)
        ]
        gram = {}
        for row, (i, j) in enumerate(pairs):
            gram[i, j] = gram[j, i] = values[row]
        shift = mean + reg
        matrix = {}
        for i in range(4):
            for j in range(i, 4):
                value = gram[i + 1, j] + shift * gram[i, j] if i < 3 else values[10] + reg * gram[3, 3]
                matrix[i, j] = matrix[j, i] = value
        norm = [jnp.where(matrix[i, i] > 1e-37, lax.rsqrt(jnp.maximum(matrix[i, i], 1e-37)), 0.0) for i in range(4)]
        side = [gram[0, i] * norm[i] for i in range(4)]
        for i in range(4):
            for j in range(i, 4):
                matrix[i, j] = matrix[j, i] = matrix[i, j] * norm[i] * norm[j]
        inverse = []
        for k in range(4):
            pivot = matrix[k, k]
            inverse.append(jnp.where(pivot > 2e-6, 1.0 / jnp.maximum(pivot, 2e-6), 0.0))
            for i in range(k + 1, 4):
                factor = matrix[i, k] * inverse[k]
                for j in range(i, 4):
                    matrix[i, j] = matrix[j, i] = matrix[i, j] - factor * matrix[k, j]
                side[i] = side[i] - factor * side[k]
        weights = [None] * 4
        for k in range(3, -1, -1):
            value = side[k]
            for j in range(k + 1, 4):
                value = value - matrix[k, j] * weights[j]
            weights[k] = value * inverse[k]
        real = sum(weights[k] * norm[k] * basis[k][0] for k in range(4))
        imag = sum(weights[k] * norm[k] * basis[k][1] for k in range(4))
        for t in range(3):
            pair[t, pl.ds(0, 8, stride=2), :] = real[:, 128 * t : 128 * t + 128]
            pair[t, pl.ds(1, 8, stride=2), :] = imag[:, 128 * t : 128 * t + 128]
        write(out_ref)

    phase_solve()


def local(image, sampled_lines, coil_maps, kspace, reg_weight, conv_first, conv_middle, conv_last):
    vmem = pl.BlockSpec(memory_space=pltpu.VMEM)
    anywhere = pl.BlockSpec(memory_space=pltpu.HBM)
    block = pltpu.VMEM((1, XB, 2, Y), F32)
    dma = pltpu.SemaphoreType.DMA
    return pl.pallas_call(
        kernel,
        out_shape=(block, block),
        in_specs=[anywhere] * 8,
        out_specs=(vmem, vmem),
        scratch_shapes=[
            pltpu.VMEM((1, XB, 2, Y), F32),
            pltpu.VMEM((1, NS), jnp.int32),
            pltpu.SMEM((1,), F32),
            pltpu.VMEM((27, 2, CH), BF16),
            pltpu.VMEM((54, CH, CH), BF16),
            pltpu.VMEM((27, 2, CH), BF16),
            pltpu.VMEM((6, 3, 16, 256), BF16),
            pltpu.VMEM((8, YP), F32),
            pltpu.VMEM((3, 6, 24, YP), F32),
            pltpu.VMEM((YP, 1280), F32),
            pltpu.VMEM((256, 1280), BF16),
            pltpu.VMEM((64, 128), F32),
            pltpu.VMEM((128, 128), F32),
            pltpu.VMEM((2, 768, 256), BF16),
            pltpu.VMEM((1152, 128), F32),
            pltpu.VMEM((1152, 128), BF16),
            pltpu.VMEM((5, 10, Y, 128), BF16),
            pltpu.VMEM((4, 8, Y, 128), BF16),
            pltpu.VMEM((3, 6, Y, 128), BF16),
            pltpu.VMEM((2 * YP, 256), BF16),
            pltpu.VMEM((2 * YP, 256), BF16),
            pltpu.VMEM((256, 2 * YP), BF16),
            pltpu.VMEM((256, 2 * YP), BF16),
            pltpu.VMEM((YP, 128), BF16),
            pltpu.VMEM((CL, XW, 2, Y), F32),
            pltpu.VMEM((CL, XW, 2, Y), F32),
            pltpu.VMEM((C, XB, 2, Y), F32),
            pltpu.VMEM((3, 8 * C, 128), F32),
            pltpu.VMEM((4 * C, 2 * YP), F32),
            pltpu.VMEM((4 * C, YP), F32),
            pltpu.VMEM((4 * C, YP), F32),
            pltpu.VMEM((8, 8, YP), F32),
            pltpu.VMEM((8, 8, YP), F32),
            pltpu.VMEM((3, 16, 128), F32),
            pltpu.VMEM((8, 128), F32),
            pltpu.VMEM((2, 3, 8, 1, 128), F32),
            dma((9,)), dma((17,)), dma((17,)), dma((7,)), dma((7,)), dma((7,)), dma((7,)),
            dma((2, 3, 7)), dma((2, 3, 7)), dma((6,)), dma((6,)),
        ],
        compiler_params=pltpu.CompilerParams(
            collective_id=0, has_side_effects=True, vmem_limit_bytes=LIMIT
        ),
    )(
        image, sampled_lines, coil_maps, kspace, reg_weight,
        conv_first.reshape(27, 2, CH), conv_middle.reshape(54, CH, CH), conv_last.transpose(0, 1, 2, 4, 3).reshape(27, 2, CH),
    )


def solution(mesh):
    in_specs = (
        P("slab", "coil", None, None),
        P("slab", None),
        P("coil", "slab", None, None, None),
        P("coil", "slab", None, None, None),
        P(),
        P(),
        P(),
        P(),
    )
    out_specs = (P("slab", "coil", None, None), P("slab", "coil", None, None))
    return jax.shard_map(local, mesh=mesh, in_specs=in_specs, out_specs=out_specs, check_vma=False)
```
